128 devices in a mesh: ctx: 32 (over x_lo, z, y), wsh: 4 (over x_hi, core).
Axes of the slice: x: 4 (x_hi: 2, x_lo: 2; x = x_hi * 2 + x_lo), y: 4, z: 4, core: 2. Of those that a mesh axis runs over, the one named last changes fastest.
Arguments:
- tokens: bfloat16 [16384, 896], P(('ctx', 'wsh')), may hold values from -6 to 6
- out_grad: bfloat16 [16384, 896], P(('ctx', 'wsh')), may hold values from -6 to 6
- norm1_gain: bfloat16 [896], P('wsh'), may hold values from 0.099609375 to 1.8984375
- qkv_weight: bfloat16 [896, 1152], P('wsh'), may hold values from -0.25 to 0.25
- qkv_bias: bfloat16 [1152], P('wsh'), may hold values from -3 to 3
- out_weight: bfloat16 [896, 896], P('wsh'), may hold values from -2 to 2
- norm2_gain: bfloat16 [896], P('wsh'), may hold values from 0.099609375 to 1.8984375
- gate_weight: bfloat16 [896, 4864], P(None, 'wsh'), may hold values from -0.1875 to 0.1875
- up_weight: bfloat16 [896, 4864], P(None, 'wsh'), may hold values from -0.1875 to 0.1875
- down_weight: bfloat16 [4864, 896], P('wsh'), may hold values from -0.15625 to 0.15625
- positions: int32 [16384], P(('ctx', 'wsh')), may hold values from 0 to 16383, as said below
Outputs:
- output: bfloat16 [16384, 896], P(('ctx', 'wsh'))
- token_grad: float32 [16384, 896], P(('ctx', 'wsh'))
- norm1_gain_grad: float32 [896], P('wsh')
- qkv_weight_grad: float32 [896, 1152], P('wsh')
- qkv_bias_grad: float32 [1152], P('wsh')
- out_weight_grad: float32 [896, 896], P('wsh')
- norm2_gain_grad: float32 [896], P('wsh')
- gate_weight_grad: float32 [896, 4864], P(None, 'wsh')
- up_weight_grad: float32 [896, 4864], P(None, 'wsh')
- down_weight_grad: float32 [4864, 896], P('wsh')
The draws below stay inside these ranges and needn't reach their ends.
Inputs may be any that keep to these rules, and one draw needn't show every extreme that they name: A permutation of the positions. The sequence is cut into 64 blocks of 256 consecutive positions. Each index c of ctx holds two blocks, b(c) and 63 - b(c), where b is a permutation of 0 to 31 drawn from the seed. The device at index w of wsh in it holds, in order, positions b(c) * 256 + w * 64 onward in its first 64 rows, and the same stretch of block 63 - b(c) in its other rows.
All inputs are finite; a program needn't handle non-finite values.
Results may differ from the reference program's by a relative error of at most 0.035.
Values may be sent and summed in bfloat16 or wider, within the bound.
A program may use at most 192 MiB of HBM per device.

```python
import math
import jax
import jax.numpy as jnp
from jax import lax

D = 896
H = 14
KVH = 2
HD = 64
FF = 4864
TOK_DEV = 128
TOKENS = 16384
QKV = 1152
N_CTX = 32
N_WSH = 4


def draw_positions(key, part):
    key = jax.random.fold_in(key, 11)
    early_blocks = jax.random.permutation(key, N_CTX).astype(jnp.int32)
    half_rows = TOK_DEV // 2
    block_rows = half_rows * N_WSH
    row_index = jnp.arange(TOKENS, dtype=jnp.int32)
    cycle_index = row_index // (N_WSH * TOK_DEV)
    shard_index = row_index // TOK_DEV % N_WSH
    inner_row = row_index % TOK_DEV
    first_block = early_blocks[cycle_index]
    block_index = jnp.where(inner_row < half_rows, first_block, 2 * N_CTX - 1 - first_block)
    return (block_index * block_rows + shard_index * half_rows + inner_row % half_rows).astype(jnp.int32)


def steps_of(stream_key, shape, split, low, largest):
    gain, own = 1.0, jax.random.fold_in(stream_key, 6)
    for axis_at, blocks in split:
        heights = jnp.exp(jax.random.uniform(jax.random.fold_in(own, axis_at), (blocks,), jnp.float32, low / len(split), largest / len(split)))
        gain = gain * jnp.repeat(heights, shape[axis_at] // blocks).reshape([-1 if axis == axis_at else 1 for axis in range(len(shape))])
    return gain


def gaussian(rng, shape, spread, most, cuts=(), held_as=jnp.bfloat16):
    entries = jax.random.normal(rng, shape, jnp.float32) * spread
    if len(cuts) > 0:
        entries = steps_of(rng, shape, cuts, -0.22, 0.18) * entries
    return jnp.clip(entries, min=-most, max=most).astype(held_as)


def setup_inputs(seed: int = 0) -> dict:
    streams_of = jax.random.split(jax.random.key(seed), 12)
    tokens = gaussian(streams_of[0], (TOKENS, D), 1.0, 6.0, ((0, 128),))
    out_grad = gaussian(streams_of[1], (TOKENS, D), 1.0, 6.0, ((0, 128),))
    norm1_gain = jnp.clip(1.0 + 0.18 * jax.random.normal(streams_of[2], (D,), jnp.float32), 0.099609375, 1.8984375).astype(jnp.bfloat16)
    qkv_weight = gaussian(streams_of[3], (D, QKV), (D // 2) ** -0.5, 0.25, ((0, 4),))
    qkv_bias = gaussian(streams_of[4], (QKV,), 0.5, 3.0, ((0, 4),))
    out_weight = gaussian(streams_of[5], (H * HD, D), (max(H * HD // 128, 1)) ** -0.5, 2.0, ((0, 4),))
    norm2_gain = jnp.clip(1.0 + 0.18 * jax.random.normal(streams_of[6], (D,), jnp.float32), 0.099609375, 1.8984375).astype(jnp.bfloat16)
    gate_weight = gaussian(streams_of[7], (D, FF), D ** -0.5, 0.1875, ((1, 4),))
    up_weight = gaussian(streams_of[8], (D, FF), D ** -0.5, 0.1875, ((1, 4),))
    down_weight = gaussian(streams_of[9], (FF, D), (FF // 4) ** -0.5, 0.15625, ((0, 4),))
    positions = draw_positions(jax.random.fold_in(streams_of[11], 71), 0)
    return dict(tokens=tokens, out_grad=out_grad, norm1_gain=norm1_gain, qkv_weight=qkv_weight, qkv_bias=qkv_bias, out_weight=out_weight, norm2_gain=norm2_gain, gate_weight=gate_weight, up_weight=up_weight, down_weight=down_weight, positions=positions)


norm_eps = 1e-06
rope_base = 1000000.0
masked_score = -1e+30
highest = lax.Precision.HIGHEST

@jax.custom_vjp
def low(v):
    return lax.optimization_barrier(v.astype(jnp.bfloat16)).astype(jnp.float32)

@jax.custom_vjp
def low_back(v):
    return v

def low_keep(v):
    return (low(v), None)

def low_pass(kept, grad):
    return (grad,)

def back_keep(v):
    return (v, None)

def back_low(kept, grad):
    return (low(grad),)
low.defvjp(low_keep, low_pass)
low_back.defvjp(back_keep, back_low)

def rms_norm(values, gain_vec):
    return values * lax.rsqrt(lax.optimization_barrier(jnp.mean(values * values, -1, keepdims=True)) + norm_eps) * gain_vec

def rotary_tables(positions, width):
    half_width = width // 2
    frequency = rope_base ** (-(2.0 * jnp.arange(half_width, dtype=jnp.float32)) / width)
    angles = positions.astype(jnp.float32)[:, None] * frequency[None, :]
    return (jnp.cos(angles)[:, None, :], jnp.sin(angles)[:, None, :])

def rotate(values, cosine, sine_vals):
    half_width = values.shape[-1] // 2
    first_half = values[..., :half_width]
    second_half = values[..., half_width:]
    return jnp.concatenate([first_half * cosine - second_half * sine_vals, second_half * cosine + first_half * sine_vals], -1)

def attend_block(queries, query_pos, key_rows, value_rows, key_pos):
    row_count = queries.shape[0]
    grouped = queries.reshape(row_count, KVH, H // KVH, HD)
    scores = jnp.einsum('rkgd,nkd->kgrn', grouped, key_rows, precision=highest) * (1.0 / math.sqrt(HD))
    visible = query_pos[:, None] >= key_pos[None, :]
    scores = low_back(jnp.where(visible[None, None], scores, masked_score))
    row_max = lax.optimization_barrier(jnp.max(scores, -1, keepdims=True))
    weights_raw = jnp.exp(scores - row_max)
    probabilities = weights_raw / lax.optimization_barrier(jnp.sum(weights_raw, -1, keepdims=True))
    mixed_rows = jnp.einsum('kgrn,nkd->rkgd', low(probabilities), value_rows, precision=highest)
    return mixed_rows.reshape(row_count, H * HD)

def layer_forward(tokens, norm1_gain, qkv_weight, qkv_bias, out_weight, norm2_gain, gate_weight, up_weight, down_weight, positions):
    normed_one = low(rms_norm(tokens, norm1_gain))
    projected = low_back(jnp.dot(normed_one, qkv_weight, precision=highest) + qkv_bias)
    cosine, sine_vals = rotary_tables(positions, HD)
    queries = low(rotate(projected[:, :H * HD].reshape(TOKENS, H, HD), cosine, sine_vals))
    key_rows = low(rotate(projected[:, H * HD:(H + KVH) * HD].reshape(TOKENS, KVH, HD), cosine, sine_vals))
    value_rows = low(projected[:, (H + KVH) * HD:].reshape(TOKENS, KVH, HD))
    block_rows = min(256, TOKENS)
    block_count = TOKENS // block_rows
    attend = jax.checkpoint(lambda inputs_pair: attend_block(inputs_pair[0], inputs_pair[1], key_rows, value_rows, positions))
    attended = lax.map(attend, (queries.reshape(block_count, block_rows, H, HD), positions.reshape(block_count, block_rows)))
    attended = low_back(low(attended.reshape(TOKENS, H * HD)))
    stream = tokens + low_back(jnp.dot(attended, out_weight, precision=highest))
    normed_two = low(rms_norm(stream, norm2_gain))

    def feed_forward(rows_in):
        gate_pre = low_back(jnp.dot(rows_in, gate_weight, precision=highest))
        up_pre = low_back(jnp.dot(rows_in, up_weight, precision=highest))
        hidden = low(jax.nn.silu(gate_pre) * up_pre)
        return low_back(jnp.dot(hidden, down_weight, precision=highest))
    mlp_rows = min(4096, TOKENS)
    branch = lax.map(jax.checkpoint(feed_forward), normed_two.reshape(TOKENS // mlp_rows, mlp_rows, D))
    return stream + branch.reshape(TOKENS, D)

def reference(tokens, out_grad, norm1_gain, qkv_weight, qkv_bias, out_weight, norm2_gain, gate_weight, up_weight, down_weight, positions):
    floats = [array_in.astype(jnp.float32) for array_in in (tokens, norm1_gain, qkv_weight, qkv_bias, out_weight, norm2_gain, gate_weight, up_weight, down_weight)]

    def wrapped(*params):
        return layer_forward(*params, positions)
    result, pullback = jax.vjp(wrapped, *floats)
    grads = pullback(out_grad.astype(jnp.float32))
    return (result.astype(jnp.bfloat16), grads[0], grads[1], grads[2], grads[3], grads[4], grads[5], grads[6], grads[7], grads[8])
```

```python
import functools
import math

import jax
import jax.numpy as jnp
from jax import lax
from jax.experimental import pallas as pl
from jax.experimental.pallas import tpu as pltpu
from jax.sharding import PartitionSpec as P

H = 14
KVH = 2
HD = 64
G = H // KVH
D = 896
FS = 1216
QKV = 1152
QC = G * HD
PC = QC + 2 * HD
TOK = 128
CHIP = 256
KROWS = 272

MESH = pl.DeviceIdType.MESH
VLIM = 56 * 1024 * 1024
norm_eps = 1e-06
rope_base = 1000000.0
f32 = jnp.float32
bf16 = jnp.bfloat16


def my_place():
    c = lax.axis_index("ctx")
    w = lax.axis_index("wsh")
    return (w // 2) * 2 + c // 16, c % 4, (c // 4) % 4, w % 2


def dev(x, y, z, core):
    return ((x % 2) * 16 + z * 4 + y, (x // 2) * 2 + core)


def moved(place, axis, by):
    x, y, z, core = place
    if axis == "x":
        return dev((x + by + 4) % 4, y, z, core)
    if axis == "y":
        return dev(x, (y + by + 4) % 4, z, core)
    return dev(x, y, (z + by + 4) % 4, core)


def along(place, axis):
    return place["xyz".index(axis)]


def greet(devices):
    barrier = pltpu.get_barrier_semaphore()
    for device in devices:
        pl.semaphore_signal(barrier, inc=1, device_id=device, device_id_type=MESH)
    pl.semaphore_wait(barrier, len(devices))


class Sems:
    def __init__(self, send, recv):
        self.send, self.recv, self.at = send, recv, 0
        self.started = []

    def copy(self, src, dst, device):
        i = self.at
        self.at += 1
        return pltpu.make_async_remote_copy(
            src_ref=src,
            dst_ref=dst,
            send_sem=self.send.at[i],
            recv_sem=self.recv.at[i],
            device_id=device,
            device_id_type=MESH,
        )

    def start(self, src, dst, device):
        copy = self.copy(src, dst, device)
        copy.start()
        self.started.append(copy)
        return copy

    def finish(self):
        for copy in self.started:
            copy.wait_send()


def call(kernel, out_shape, scratch, n_sems, cid, args, specs=None):
    vmem = pl.BlockSpec(memory_space=pltpu.VMEM)
    outs = jax.tree.map(lambda _: vmem, out_shape)
    return pl.pallas_call(
        kernel,
        out_shape=out_shape,
        in_specs=specs if specs is not None else [vmem] * len(args),
        out_specs=outs,
        scratch_shapes=[
            *scratch,
            pltpu.SemaphoreType.DMA((n_sems,)),
            pltpu.SemaphoreType.DMA((n_sems,)),
        ],
        compiler_params=pltpu.CompilerParams(
            collective_id=cid, has_side_effects=True, vmem_limit_bytes=VLIM
        ),
    )(*args)


def pair_of(place):
    x, y, z, core = place
    return dev(x, y, z, 1 - core), dev(3 - x, y, z, core)


def start_kernel(w_ref, t_ref, w_out, t_out, local_sem, send, recv):
    place = my_place()
    x, y, z, core = place
    sibling, cross = pair_of(place)
    greet([sibling, cross])
    sems = Sems(send, recv)
    mine = (x // 2) * 2 + core
    theirs = (1 - x // 2) * 2 + core
    pieces = [pl.ds(48 * i, 48) for i in range(5)]
    over = [sems.start(w_ref.at[p], w_out.at[mine, p], cross) for p in pieces]
    toks = sems.start(t_ref, t_out.at[:, :, core], sibling)
    own = sems.start(w_ref, w_out.at[mine], sibling)
    keep = [
        pltpu.make_async_copy(w_ref, w_out.at[mine], local_sem.at[0]),
        pltpu.make_async_copy(t_ref, t_out.at[:, :, core], local_sem.at[1]),
    ]
    for copy in keep:
        copy.start()
    passed = []
    for copy, p in zip(over, pieces):
        copy.wait_recv()
        passed.append(sems.start(w_out.at[theirs, p], w_out.at[theirs, p], sibling))
    for copy in [toks, own, *passed]:
        copy.wait_recv()
    for copy in keep:
        copy.wait()
    sems.finish()


def group_kernel(a_ref, out_ref, local_sem, send, recv):
    place = my_place()
    core = place[3]
    sibling, cross = pair_of(place)
    greet([sibling, cross])
    sems = Sems(send, recv)
    pieces = [pl.ds(64 * i, 64) for i in range(4)]
    over = [sems.start(a_ref.at[p], out_ref.at[1, core, p], cross) for p in pieces]
    own = sems.start(a_ref, out_ref.at[0, core], sibling)
    keep = pltpu.make_async_copy(a_ref, out_ref.at[0, core], local_sem.at[0])
    keep.start()
    passed = []
    for copy, p in zip(over, pieces):
        copy.wait_recv()
        passed.append(sems.start(out_ref.at[1, core, p], out_ref.at[1, core, p], sibling))
    for copy in [own, *passed]:
        copy.wait_recv()
    keep.wait()
    sems.finish()


def group_gather(array, cid):
    return call(
        group_kernel,
        jax.ShapeDtypeStruct((2, 2, *array.shape), array.dtype),
        [pltpu.SemaphoreType.DMA((1,))],
        9,
        cid,
        (array,),
    )


def group_sum_kernel(p_ref, out_ref, got, total, far, send, recv):
    place = my_place()
    core = place[3]
    sibling, cross = pair_of(place)
    greet([sibling, cross])
    sems = Sems(send, recv)
    in_other = [sems.start(p_ref.at[1, h, 1 - core], got.at[1, h], sibling) for h in range(2)]
    in_own = [sems.start(p_ref.at[0, h, 1 - core], got.at[0, h], sibling) for h in range(2)]
    over = []
    for h in range(2):
        in_other[h].wait_recv()
        total[1, h] = (p_ref[1, h, core].astype(f32) + got[1, h].astype(f32)).astype(bf16)
        over.append(sems.start(total.at[1, h], far.at[h], cross))
    last = []
    for h in range(2):
        in_own[h].wait_recv()
        over[h].wait_recv()
        out_ref[h, core] = (
            p_ref[0, h, core].astype(f32) + got[0, h].astype(f32) + far[h].astype(f32)
        ).astype(bf16)
        last.append(sems.start(out_ref.at[h, core], out_ref.at[h, core], sibling))
    for copy in last:
        copy.wait_recv()
    sems.finish()


def group_sum(part, cid):
    rows = (2, 64, D)
    return call(
        group_sum_kernel,
        jax.ShapeDtypeStruct((2, 2, 64, D), bf16),
        [pltpu.VMEM((2, *rows), bf16), pltpu.VMEM((2, *rows), bf16), pltpu.VMEM(rows, bf16)],
        8,
        cid,
        (part,),
    )


orders = (("z", "y", "x"), ("y", "x", "z"), ("x", "z", "y"))


def chips(ref, place, free, axis, at, rows):
    x, y, z, _ = place
    index = {"x": x, "y": y, "z": z}
    index[axis] = at
    every = slice(None)
    xlo, xhi = (every, every) if "x" in free else (index["x"] % 2, index["x"] // 2)
    return ref.at[
        xlo, every if "z" in free else index["z"], every if "y" in free else index["y"], xhi, rows
    ]


def kv_gather_kernel(own_ref, all_ref, local_sem, send, recv):
    place = my_place()
    x, y, z, core = place
    greet([moved(place, a, b) for a in "xyz" for b in (1, -1)])
    sems = Sems(send, recv)
    parts = [(0, 48, 48), (96, 48, 48), (192, 48, 32)]
    keep = pltpu.make_async_copy(own_ref, all_ref.at[x % 2, z, y, x // 2], local_sem.at[0])
    keep.start()
    keep.wait()
    for stage in range(3):
        firsts = []
        for (row, n0, n1), order in zip(parts, orders):
            axis, free = order[stage], order[:stage]
            at = along(place, axis)
            here = chips(all_ref, place, free, axis, at, pl.ds(row, n0 + n1))
            firsts.append(
                [sems.start(here, here, moved(place, axis, by)) for by in (1, -1)]
            )
        seconds = []
        for (row, n0, n1), order, (to_right, to_left) in zip(parts, orders, firsts):
            axis, free = order[stage], order[:stage]
            at = along(place, axis)
            to_right.wait_recv()
            left = chips(all_ref, place, free, axis, (at + 3) % 4, pl.ds(row, n0))
            seconds.append(sems.start(left, left, moved(place, axis, 1)))
            to_left.wait_recv()
            right = chips(all_ref, place, free, axis, (at + 1) % 4, pl.ds(row + n0, n1))
            seconds.append(sems.start(right, right, moved(place, axis, -1)))
        for copy in seconds:
            copy.wait_recv()
    sems.finish()


def kv_gather(chunk, cid):
    return call(
        kv_gather_kernel,
        jax.ShapeDtypeStruct((2, 4, 4, 2, KROWS, 128), bf16),
        [pltpu.SemaphoreType.DMA((1,))],
        36,
        cid,
        (chunk,),
    )


def added(into, terms, shape):
    if not shape:
        into[...] = sum([t[...].astype(f32) for t in terms], into[...].astype(f32)).astype(bf16)
        return

    def one(i, carry):
        rest, index = i, []
        for size in reversed(shape):
            index.insert(0, rest % size)
            rest = rest // size
        index = tuple(index)
        into[index] = sum(
            [t[index].astype(f32) for t in terms], into[index].astype(f32)
        ).astype(bf16)
        return carry

    lax.fori_loop(0, math.prod(shape), one, 0)


def ring_sum(place, sems, jobs):
    state = []
    for axis, view, land, shape in jobs:
        at = along(place, axis)
        right, left = moved(place, axis, 1), moved(place, axis, -1)
        far = (at + 2) % 4
        state.append(
            (
                sems.start(view(far, 1), land[0], right),
                sems.start(view(far, 0), land[1], left),
                sems.start(view((at + 1) % 4, 0), land[2], right),
                sems.start(view((at + 3) % 4, 1), land[3], left),
            )
        )
    lasts = []
    for (axis, view, land, shape), (far_right, far_left, _, _) in zip(jobs, state):
        at = along(place, axis)
        right, left = moved(place, axis, 1), moved(place, axis, -1)
        far_right.wait_recv()
        added(view((at + 1) % 4, 1), [land[0]], shape)
        one = sems.start(view((at + 1) % 4, 1), land[4], right)
        far_left.wait_recv()
        added(view((at + 3) % 4, 0), [land[1]], shape)
        lasts.append((one, sems.start(view((at + 3) % 4, 0), land[5], left)))
    for (axis, view, land, shape), (_, _, near_r, near_l), (one, two) in zip(jobs, state, lasts):
        at = along(place, axis)
        near_r.wait_recv()
        two.wait_recv()
        added(view(at, 0), [land[2], land[5]], shape)
        near_l.wait_recv()
        one.wait_recv()
        added(view(at, 1), [land[3], land[4]], shape)


sum_parts = [(0, 48, 48), (96, 48, 48), (192, 32, 32)]


def kv_lead(free):
    return sum([(2, 2) if a == "x" else (4,) for a in free], ())


def kv_shape(free):
    lead = ()
    if "x" in free:
        lead += (2,)
    if "z" in free:
        lead += (4,)
    if "y" in free:
        lead += (4,)
    if "x" in free:
        lead += (2,)
    return lead


def kv_sum_kernel(part_ref, out_ref, work, local_sem, *rest):
    lands, (send, recv) = rest[:-2], rest[-2:]
    place = my_place()
    x, y, z, core = place
    greet([moved(place, a, b) for a in "xyz" for b in (1, -1)])
    keep = pltpu.make_async_copy(part_ref, work, local_sem.at[0])
    keep.start()
    keep.wait()
    sems = Sems(send, recv)
    at_land = 0
    for stage in range(3):
        jobs = []
        for (row, n0, n1), order in zip(sum_parts, orders):
            axis, free = order[stage], order[stage + 1 :]

            def view(at, half, row=row, n0=n0, n1=n1, axis=axis, free=free):
                rows = pl.ds(row, n0) if half == 0 else pl.ds(row + n0, n1)
                return chips(work, place, free, axis, at, rows)

            jobs.append((axis, view, lands[at_land : at_land + 6], kv_shape(free)))
            at_land += 6
        ring_sum(place, sems, jobs)
    out_ref[...] = work[x % 2, z, y, x // 2].astype(f32)
    sems.finish()


def kv_sum(part, cid):
    lands = []
    for stage in range(3):
        for (row, n0, n1), order in zip(sum_parts, orders):
            lead = kv_shape(order[stage + 1 :])
            for n in (n1, n0, n0, n1, n1, n0):
                lands.append(pltpu.VMEM((*lead, n, 128), bf16))
    shape = (2, 4, 4, 2, CHIP, 128)
    return call(
        kv_sum_kernel,
        jax.ShapeDtypeStruct((CHIP, 128), f32),
        [pltpu.VMEM(shape, bf16), pltpu.SemaphoreType.DMA((1,)), *lands],
        54,
        cid,
        (part,),
    )


weight_parts = [
    (0, 0, 32, 32, "zy"),
    (0, 64, 16, 32, "yz"),
    (1, 0, 32, 16, "zy"),
    (1, 48, 32, 32, "yz"),
]
wide = (FS, D)
chunk_rows = 112


def weight_view(ref, place, first, at, rows, second=None):
    _, y, z, _ = place
    every = slice(None)
    if second is None:
        return ref.at[at, every, rows] if first == "z" else ref.at[every, at, rows]
    return ref.at[z, at, rows] if first == "z" else ref.at[at, y, rows]


def weight_kernel(gate, up, down, rest_ref, out_a, out_b, work_a, work_b, local_sem, *more):
    lands, (send, recv) = more[:-2], more[-2:]
    place = my_place()
    x, y, z, core = place
    mate = dev(x + 1 - 2 * (x % 2), y, z, core)
    works, outs = (work_a, work_b), (out_a, out_b)
    loads = [
        pltpu.make_async_copy(gate, work_a.at[0:2], local_sem.at[0]),
        pltpu.make_async_copy(up, work_a.at[2:4], local_sem.at[1]),
        pltpu.make_async_copy(down, work_b.at[0:2], local_sem.at[2]),
        pltpu.make_async_copy(rest_ref, work_b.at[2:4], local_sem.at[3]),
    ]
    for copy in loads:
        copy.start()
    greet([moved(place, a, b) for a in "yz" for b in (1, -1)] + [mate])
    for copy in loads:
        copy.wait()
    sems = Sems(send, recv)
    at_land = 0
    for stage in range(2):
        jobs = []
        for buf, row, n0, n1, order in weight_parts:

            def view(at, half, buf=buf, row=row, n0=n0, n1=n1, order=order):
                rows = pl.ds(row, n0) if half == 0 else pl.ds(row + n0, n1)
                if stage == 0:
                    return weight_view(works[buf], place, order[0], at, rows)
                return weight_view(works[buf], place, order[0], at, rows, order[1])

            jobs.append(
                (order[stage], view, lands[at_land : at_land + 6], (4,) if stage == 0 else ())
            )
            at_land += 6
        ring_sum(place, sems, jobs)
    swaps = []
    for buf, row, n0, n1, order in weight_parts:
        mine = works[buf].at[z, y, pl.ds(row, n0 + n1)]
        swaps.append(sems.start(mine, lands[at_land], mate))
        at_land += 1
    for i, ((buf, row, n0, n1, order), copy) in enumerate(zip(weight_parts, swaps)):
        copy.wait_recv()
        rows = pl.ds(row, n0 + n1)
        land = lands[at_land - len(weight_parts) + i]
        outs[buf][z, y, rows] = (
            works[buf][z, y, rows].astype(f32) + land[...].astype(f32)
        ).astype(bf16)
    for stage in (1, 0):
        firsts = []
        for buf, row, n0, n1, order in weight_parts:
            axis = order[stage]
            rows = pl.ds(row, n0 + n1)
            second = order[1] if stage == 1 else None
            here = weight_view(outs[buf], place, order[0], along(place, axis), rows, second)
            firsts.append([sems.start(here, here, moved(place, axis, by)) for by in (1, -1)])
        seconds = []
        for (buf, row, n0, n1, order), (to_right, to_left) in zip(weight_parts, firsts):
            axis = order[stage]
            at = along(place, axis)
            second = order[1] if stage == 1 else None
            to_right.wait_recv()
            left = weight_view(
                outs[buf], place, order[0], (at + 3) % 4, pl.ds(row, n0), second
            )
            seconds.append(sems.start(left, left, moved(place, axis, 1)))
            to_left.wait_recv()
            right = weight_view(
                outs[buf], place, order[0], (at + 1) % 4, pl.ds(row + n0, n1), second
            )
            seconds.append(sems.start(right, right, moved(place, axis, -1)))
        for copy in seconds:
            copy.wait_recv()
    sems.finish()


def weight_sum(gate, up, down, rest, cid):
    lands = []
    for stage in range(2):
        for buf, row, n0, n1, order in weight_parts:
            lead = (4,) if stage == 0 else ()
            for n in (n1, n0, n0, n1, n1, n0):
                lands.append(pltpu.VMEM((*lead, n, wide[buf]), bf16))
    for buf, row, n0, n1, order in weight_parts:
        lands.append(pltpu.VMEM((n0 + n1, wide[buf]), bf16))
    big = [(4, 4, chunk_rows, w) for w in wide]
    half = (2, 4, chunk_rows)
    args = (
        gate.reshape(*half, FS),
        up.reshape(*half, FS),
        down.reshape(*half, D),
        rest.reshape(*half, D),
    )
    return call(
        weight_kernel,
        tuple(jax.ShapeDtypeStruct(s, bf16) for s in big),
        [*[pltpu.VMEM(s, bf16) for s in big], pltpu.SemaphoreType.DMA((4,)), *lands],
        4 * 6 * 2 + 4 + 4 * 4 * 2,
        cid,
        args,
        [pl.BlockSpec(memory_space=pl.ANY)] * 4,
    )


NT = (((1,), (1,)), ((), ()))
ROWS = G * 128


def lanes(shape):
    return lax.broadcasted_iota(jnp.int32, shape, len(shape) - 1)


def split3(value):
    one = value.astype(bf16).astype(f32)
    two = (value - one).astype(bf16).astype(f32)
    three = (value - one - two).astype(bf16).astype(f32)
    return one, two, three


def keys_of(kv_ref, c, half):
    rows = pl.ds(pl.multiple_of(half * 128, 128), 128)
    tile = kv_ref[c, :, rows, :].reshape(256, 128)
    lane = lanes((256, 128))
    ones = jnp.ones((256, 128), bf16)
    return jnp.where(lane < HD, tile, ones), jnp.where(lane < HD, ones, tile)


def hidden_keys(xhi):
    row = lax.broadcasted_iota(jnp.int32, (ROWS, 256), 0) % 128
    key = lax.broadcasted_iota(jnp.int32, (ROWS, 256), 1)
    return key > row + xhi * 128


def forward_kernel(scal, q_ref, kv_ref, o_ref, qe_ref, peak, acc):
    me, xhi = scal[32], scal[33]
    lane = lanes((128, 128))
    for h in range(2):
        for g in range(G):
            piece = q_ref[h, :, g * HD : (g + 1) * HD].astype(f32) * (1.0 / math.sqrt(HD))
            wide_piece = jnp.concatenate([piece, jnp.zeros((128, HD), f32)], 1)
            qe_ref[h, g * 128 : (g + 1) * 128, :] = wide_piece.astype(bf16)
    peak[...] = jnp.full((2, ROWS, 128), -1e30, f32)
    acc[...] = jnp.zeros((2, ROWS, 128), f32)

    def scores(half, kk):
        return lax.dot_general(qe_ref[half], kk, NT, preferred_element_type=f32)

    def top(half, s):
        peak[half] = jnp.maximum(peak[half], jnp.maximum(s[:, :128], s[:, 128:]))

    def fold(half, s, vv):
        p = jnp.exp(s).astype(bf16)
        acc[half] += jnp.dot(p, vv, preferred_element_type=f32)

    def others(work):
        def one(i, carry):
            c = (me + i) % 32
            kk, vv = keys_of(kv_ref, c, 0)
            work(1, kk, vv, None)
            sel = scal[c]
            kk, vv = keys_of(kv_ref, c, sel)
            work(sel, kk, vv, None)
            return carry

        lax.fori_loop(1, 32, one, 0)
        early_k, early_v = keys_of(kv_ref, me, 0)
        late_k, late_v = keys_of(kv_ref, me, 1)
        work(1, early_k, early_v, None)
        work(0, early_k, early_v, hidden_keys(xhi))
        work(1, late_k, late_v, hidden_keys(xhi))

    def first(half, kk, vv, hide):
        s = scores(half, kk)
        top(half, s if hide is None else jnp.where(hide, -1e30, s))

    def second(half, kk, vv, hide):
        s = scores(half, kk)
        fold(half, s if hide is None else jnp.where(hide, -1e30, s), vv)

    others(first)
    wide_lane = lanes((ROWS, 128))

    def with_column(half, column):
        one, two, three = split3(-column)
        held = qe_ref[half].astype(f32)
        held = jnp.where(wide_lane == HD, one, held)
        held = jnp.where(wide_lane == HD + 1, two, held)
        held = jnp.where(wide_lane == HD + 2, three, held)
        qe_ref[half] = held.astype(bf16)

    for h in range(2):
        highest = jnp.max(peak[h], 1, keepdims=True)
        peak[h] = jnp.broadcast_to(highest, (ROWS, 128))
        with_column(h, highest)
    others(second)
    for h in range(2):
        total = acc[h][:, :1]
        with_column(h, peak[h][:, :1] + jnp.log(total))
        out = acc[h] / total
        for g in range(G):
            o_ref[h, :, g * HD : (g + 1) * HD] = out[g * 128 : (g + 1) * 128, HD:]


def local_call(kernel, out_shape, scratch, args, flops):
    vmem = pl.BlockSpec(memory_space=pltpu.VMEM)
    return pl.pallas_call(
        kernel,
        out_shape=out_shape,
        in_specs=[pl.BlockSpec(memory_space=pltpu.SMEM)] + [vmem] * (len(args) - 1),
        out_specs=jax.tree.map(lambda _: vmem, out_shape),
        scratch_shapes=scratch,
        compiler_params=pltpu.CompilerParams(vmem_limit_bytes=VLIM),
        cost_estimate=pl.CostEstimate(
            flops=flops, bytes_accessed=10_000_000, transcendentals=15_000_000
        ),
    )(*args)


def attention_forward(scal, q, kv):
    return local_call(
        forward_kernel,
        (
            jax.ShapeDtypeStruct((2, 128, QC), f32),
            jax.ShapeDtypeStruct((2, ROWS, 128), bf16),
        ),
        [pltpu.VMEM((2, ROWS, 128), f32), pltpu.VMEM((2, ROWS, 128), f32)],
        (scal, q, kv),
        20_000_000_000,
    )


def backward_kernel(scal, qe_ref, o_ref, g_ref, kv_ref, dq_ref, dkv_ref, ge, qt, gt, dq, step):
    me, xhi = scal[32], scal[33]
    lane = lanes((128, 128))
    for h in range(2):
        for g in range(G):
            cols = slice(g * HD, (g + 1) * HD)
            piece = g_ref[h, :, cols].astype(f32)
            delta = jnp.sum(piece * o_ref[h, :, cols], 1, keepdims=True)
            one, two, three = split3(-delta)
            held = jnp.concatenate([jnp.zeros((128, HD), f32), piece], 1)
            held = jnp.where(lane == 0, one, held)
            held = jnp.where(lane == 1, two, held)
            held = jnp.where(lane == 2, three, held)
            rows = slice(g * 128, (g + 1) * 128)
            ge[h, rows, :] = held.astype(bf16)
            gt[h, :, rows] = held.T.astype(bf16)
            qt[h, :, rows] = qe_ref[h, rows, :].astype(f32).T.astype(bf16)
    dq[...] = jnp.zeros((2, ROWS, 128), f32)
    under = lax.broadcasted_iota(jnp.int32, (128, 256), 0) < HD

    def tile(half, kk, vv, hide):
        s = lax.dot_general(qe_ref[half], kk, NT, preferred_element_type=f32)
        if hide is not None:
            s = jnp.where(hide, -1e30, s)
        p = jnp.exp(s)
        dp = lax.dot_general(ge[half], vv, NT, preferred_element_type=f32)
        ds = (p * dp).astype(bf16)
        dq[half] += jnp.dot(ds, kk, preferred_element_type=f32)
        dk = jnp.dot(qt[half], ds, preferred_element_type=f32)
        dv = jnp.dot(gt[half], p.astype(bf16), preferred_element_type=f32)
        return jnp.where(under, dk, dv).T

    def put(c, half, value):
        rows = pl.ds(pl.multiple_of(half * 128, 128), 128)
        dkv_ref[c, :, rows, :] = value.astype(bf16).reshape(2, 128, 128)

    def one(i, carry):
        c = (me + i) % 32
        kk, vv = keys_of(kv_ref, c, 0)
        step[0] = tile(1, kk, vv, None)
        step[1] = jnp.zeros((256, 128), f32)
        sel = scal[c]
        kk, vv = keys_of(kv_ref, c, sel)
        step[sel] += tile(sel, kk, vv, None)
        put(c, 0, step[0])
        put(c, 1, step[1])
        return carry

    lax.fori_loop(1, 32, one, 0)
    early_k, early_v = keys_of(kv_ref, me, 0)
    late_k, late_v = keys_of(kv_ref, me, 1)
    put(
        me,
        0,
        tile(1, early_k, early_v, None) + tile(0, early_k, early_v, hidden_keys(xhi)),
    )
    put(me, 1, tile(1, late_k, late_v, hidden_keys(xhi)))
    for h in range(2):
        for g in range(G):
            dq_ref[h, :, g * HD : (g + 1) * HD] = dq[h, g * 128 : (g + 1) * 128, :HD] * (
                1.0 / math.sqrt(HD)
            )


def attention_backward(scal, qe, o, grad, kv):
    return local_call(
        backward_kernel,
        (
            jax.ShapeDtypeStruct((2, 128, QC), f32),
            jax.ShapeDtypeStruct((32, 2, CHIP, 128), bf16),
        ),
        [
            pltpu.VMEM((2, ROWS, 128), bf16),
            pltpu.VMEM((2, 128, ROWS), bf16),
            pltpu.VMEM((2, 128, ROWS), bf16),
            pltpu.VMEM((2, ROWS, 128), f32),
            pltpu.VMEM((2, 256, 128), f32),
        ],
        (scal, qe, o, grad, kv),
        50_000_000_000,
    )


def rms_inverse(values):
    return lax.rsqrt(jnp.mean(values * values, -1, keepdims=True) + norm_eps)


def rms_pull(values, inverse, gain, grad):
    scaled = values * inverse
    e = grad * gain
    return inverse * (e - scaled * jnp.mean(e * scaled, -1, keepdims=True))


def rotation(positions):
    frequency = rope_base ** (-(2.0 * jnp.arange(HD // 2, dtype=f32)) / HD)
    angles = positions.astype(f32)[:, None] * frequency[None, :]
    cosine, sine = jnp.cos(angles), jnp.sin(angles)
    return (
        jnp.tile(jnp.concatenate([cosine, cosine], 1), (1, G + 1)),
        jnp.tile(jnp.concatenate([-sine, sine], 1), (1, G + 1)),
    )


def swapped(values):
    heads = values.shape[1] // HD
    parts = values.reshape(-1, heads, 2, HD // 2)
    return jnp.flip(parts, 2).reshape(values.shape)


def dot(a, b):
    return jnp.dot(a, b, preferred_element_type=f32)


def body(
    tokens,
    out_grad,
    norm1_gain,
    qkv_weight,
    qkv_bias,
    out_weight,
    norm2_gain,
    gate_weight,
    up_weight,
    down_weight,
    positions,
):
    ctx = lax.axis_index("ctx")
    wsh = lax.axis_index("wsh")
    xhi, core = wsh // 2, wsh % 2
    my_block = positions[0] // 256

    def cut(array, start, size, axis):
        return lax.dynamic_slice_in_dim(array, start, size, axis)

    def own_rows(array):
        return cut(array.reshape(2, 2, 64, -1), core, 1, 1).reshape(TOK, -1)

    swap = [
        (c * 4 + w, ((c + 16) % 32) * 4 + (w + 2) % 4) for c in range(32) for w in range(4)
    ]
    twin = [(c * 4 + w, c * 4 + w + 1 - 2 * (w % 2)) for c in range(32) for w in range(4)]

    def crossed(array):
        return lax.ppermute(array, ("ctx", "wsh"), swap)

    small = jnp.stack(
        [jnp.pad(v, (0, QKV - v.shape[0])) for v in (qkv_bias, norm1_gain, norm2_gain)]
    )
    w_in = jnp.concatenate([qkv_weight, jnp.pad(small, ((0, 13), (0, 0)))], 0)
    t_in = jnp.stack([tokens, out_grad]).reshape(2, 2, 64, D)
    w_all, t_all = call(
        start_kernel,
        (
            jax.ShapeDtypeStruct((4, 240, QKV), bf16),
            jax.ShapeDtypeStruct((2, 2, 2, 64, D), bf16),
        ),
        [pltpu.SemaphoreType.DMA((2,))],
        12,
        0,
        (w_in, t_in),
    )
    out_full = lax.all_gather(out_weight, "wsh", axis=0, tiled=True)
    qkv_full = w_all[:, :224].reshape(D, QKV)
    bias_full = w_all[:, 224, :288].reshape(QKV).astype(f32)
    gain_one = w_all[:, 225, :224].reshape(D).astype(f32)
    gain_two = w_all[:, 226, :224].reshape(D).astype(f32)
    t_chip = t_all.reshape(2, CHIP, D)

    def my_columns(array):
        return jnp.concatenate(
            [
                cut(array, core * QC, QC, array.ndim - 1),
                cut(array, H * HD + core * HD, HD, array.ndim - 1),
                cut(array, (H + KVH) * HD + core * HD, HD, array.ndim - 1),
            ],
            -1,
        )

    resid = t_chip[0].astype(f32)
    normed_one = (resid * rms_inverse(resid) * gain_one).astype(bf16)
    projected = dot(normed_one, my_columns(qkv_full)) + my_columns(bias_full)
    offset = jnp.arange(128, dtype=jnp.int32) + xhi * 128
    cosine, sine = rotation(
        jnp.concatenate([my_block * 256 + offset, (63 - my_block) * 256 + offset])
    )
    turning = projected[:, : QC + HD]
    turned = (turning * cosine + swapped(turning) * sine).astype(bf16)
    queries = turned[:, :QC].reshape(2, 128, QC)
    chunk = jnp.concatenate([turned[:, QC:], projected[:, QC + HD :].astype(bf16)], 1)
    mark = jnp.broadcast_to(my_block.astype(bf16), (KROWS - CHIP, 128))
    kv_all = kv_gather(jnp.concatenate([chunk, mark], 0), 1).reshape(32, 2, KROWS, 128)
    blocks = kv_all[:, 0, CHIP, 0].astype(jnp.int32)
    scal = jnp.concatenate(
        [(blocks > my_block).astype(jnp.int32), jnp.stack([ctx, xhi]).astype(jnp.int32)]
    )
    t_chip, kv_all = lax.optimization_barrier((t_chip, kv_all))
    t_other = crossed(t_chip)
    attended_f, qe = attention_forward(scal, queries, kv_all)
    att = group_gather(attended_f.astype(bf16).reshape(CHIP, QC), 2)
    t_both = jnp.stack([t_chip, t_other], 1).reshape(2, 2 * CHIP, D)
    resid_both = t_both[0].astype(f32)
    cot = t_both[1]
    att_cols = [att[:, i].reshape(2 * CHIP, QC) for i in range(2)]
    stream = resid_both + dot(att_cols[0], out_full[:QC]) + dot(att_cols[1], out_full[QC:])
    inv_two = rms_inverse(stream)
    normed_two = (stream * inv_two * gain_two).astype(bf16)
    gate_pre = dot(normed_two, gate_weight)
    up_pre = dot(normed_two, up_weight)
    hidden_grad = jnp.einsum("td,fd->tf", cot, down_weight, preferred_element_type=f32)
    sigma = jax.nn.sigmoid(gate_pre)
    activated = gate_pre * sigma
    hidden = (activated * up_pre).astype(bf16)
    gate_grad = (hidden_grad * up_pre * sigma * (1.0 + gate_pre * (1.0 - sigma))).astype(bf16)
    up_grad = (hidden_grad * activated).astype(bf16)
    norm_part = jnp.einsum(
        "tf,df->td", gate_grad, gate_weight, preferred_element_type=f32
    ) + jnp.einsum("tf,df->td", up_grad, up_weight, preferred_element_type=f32)
    norm_grad = group_sum(norm_part.astype(bf16).reshape(2, 2, 2, 64, D), 3).reshape(CHIP, D)

    mlp_part = dot(hidden, down_weight).astype(bf16).reshape(2, 2, 2, 64, D)
    norm_other = crossed(norm_grad)
    mlp_got = lax.ppermute(cut(mlp_part, 1 - core, 1, 2), ("ctx", "wsh"), twin)
    mlp_sum = cut(mlp_part, core, 1, 2).astype(f32) + mlp_got.astype(f32)
    mlp_far = crossed(mlp_sum[1].astype(bf16))
    mlp_own = (mlp_sum[0] + mlp_far.astype(f32)).reshape(TOK, D)
    output = (own_rows(stream[:CHIP]) + mlp_own).astype(bf16)
    gate_wgrad = jnp.einsum("td,tf->df", normed_two, gate_grad, preferred_element_type=f32)
    up_wgrad = jnp.einsum("td,tf->df", normed_two, up_grad, preferred_element_type=f32)
    down_wgrad = jnp.einsum("tf,td->fd", hidden, cot, preferred_element_type=f32)

    def stream_pull(part, grad):
        rows = slice(part * CHIP, (part + 1) * CHIP)
        return cot[rows].astype(f32) + rms_pull(
            stream[rows], inv_two[rows], gain_two, grad.astype(f32)
        )

    stream_grad = stream_pull(0, norm_grad)
    branch_grad = stream_grad.astype(bf16)
    att_grad = jnp.einsum(
        "td,id->ti", branch_grad, cut(out_full, core * QC, QC, 0), preferred_element_type=f32
    ).astype(bf16)
    dq, dkv_part = attention_backward(
        scal, qe, attended_f, att_grad.reshape(2, 128, QC), kv_all
    )
    dkv = kv_sum(dkv_part.reshape(2, 4, 4, 2, CHIP, 128), 4)
    turning = jnp.concatenate([dq.reshape(CHIP, QC), dkv[:, :HD]], 1)
    turned = turning * cosine - swapped(turning) * sine
    pg_mine = jnp.concatenate([turned, dkv[:, HD:]], 1).astype(bf16)
    pg = group_gather(pg_mine, 5)
    pg = jnp.concatenate(
        [
            pg[:, 0, :, :QC],
            pg[:, 1, :, :QC],
            pg[:, 0, :, QC : QC + HD],
            pg[:, 1, :, QC : QC + HD],
            pg[:, 0, :, QC + HD :],
            pg[:, 1, :, QC + HD :],
        ],
        -1,
    ).reshape(2 * CHIP, QKV)

    bias_grad = cut(jnp.sum(pg.astype(f32), 0), wsh * 288, 288, 0)
    inv_one = rms_inverse(resid_both)
    scaled_one = cut(resid_both, wsh * 224, 224, 1) * inv_one
    normed_cols = (scaled_one * norm1_gain.astype(f32)).astype(bf16)
    qkv_wgrad = jnp.einsum("td,tf->df", normed_cols, pg, preferred_element_type=f32)
    one_cols = jnp.einsum("tf,df->td", pg, qkv_weight, preferred_element_type=f32)
    gain_one_grad = jnp.sum(one_cols * scaled_one, 0)
    branch_both = jnp.concatenate(
        [branch_grad, stream_pull(1, norm_other).astype(bf16)], 0
    )
    norm_both = jnp.concatenate([norm_grad, norm_other], 0)
    scaled_two = cut(stream, wsh * 224, 224, 1) * inv_two
    gain_two_grad = jnp.sum(cut(norm_both, wsh * 224, 224, 1).astype(f32) * scaled_two, 0)
    att_mine = cut(jnp.where(wsh < 2, att_cols[0], att_cols[1]), (wsh % 2) * 224, 224, 1)
    out_wgrad = jnp.einsum("ti,td->id", att_mine, branch_both, preferred_element_type=f32)
    pg_own = own_rows(pg[:CHIP])
    one_grad = jnp.einsum("tf,df->td", pg_own, qkv_full, preferred_element_type=f32)
    resid_own = tokens.astype(f32)
    token_grad = own_rows(stream_grad) + rms_pull(
        resid_own, rms_inverse(resid_own), gain_one, one_grad
    )
    vectors = jnp.stack(
        [jnp.pad(v, (0, D - v.shape[0])) for v in (bias_grad, gain_one_grad, gain_two_grad)]
    )
    down_low = down_wgrad.astype(bf16)
    rest = jnp.concatenate(
        [
            down_low[896:],
            out_wgrad.astype(bf16),
            qkv_wgrad.astype(bf16).reshape(288, D),
            jnp.pad(vectors, ((0, 61), (0, 0))).astype(bf16),
        ],
        0,
    )
    sum_a, sum_b = weight_sum(
        gate_wgrad.astype(bf16), up_wgrad.astype(bf16), down_low[:896], rest, 6
    )
    sum_a = sum_a.reshape(2 * D, FS).astype(f32)
    sum_b = sum_b.reshape(2 * D, D).astype(f32)
    return (
        output,
        token_grad,
        sum_b[1729, :224],
        sum_b[1440:1728].reshape(224, QKV),
        sum_b[1728, :288],
        sum_b[1216:1440],
        sum_b[1730, :224],
        sum_a[:D],
        sum_a[D:],
        sum_b[:1216],
    )


def solution(mesh):
    rows = P(("ctx", "wsh"), None)
    return jax.shard_map(
        body,
        mesh=mesh,
        in_specs=(
            rows,
            rows,
            P("wsh"),
            P("wsh", None),
            P("wsh"),
            P("wsh", None),
            P("wsh"),
            P(None, "wsh"),
            P(None, "wsh"),
            P("wsh", None),
            P(("ctx", "wsh")),
        ),
        out_specs=(
            rows,
            rows,
            P("wsh"),
            P("wsh", None),
            P("wsh"),
            P("wsh", None),
            P("wsh"),
            P(None, "wsh"),
            P(None, "wsh"),
            P("wsh", None),
        ),
        check_vma=False,
    )
```

```python
import functools
import math

import jax
import jax.numpy as jnp
from jax import lax
from jax.experimental import pallas as pl
from jax.experimental.pallas import tpu as pltpu
from jax.sharding import PartitionSpec as P

H = 14
KVH = 2
HD = 64
G = H // KVH
D = 896
FS = 1216
QKV = 1152
QC = G * HD
PC = QC + 2 * HD
TOK = 128
CHIP = 256
KROWS = 272

MESH = pl.DeviceIdType.MESH
VLIM = 56 * 1024 * 1024
norm_eps = 1e-06
rope_base = 1000000.0
f32 = jnp.float32
bf16 = jnp.bfloat16


def my_place():
    c = lax.axis_index("ctx")
    w = lax.axis_index("wsh")
    return (w // 2) * 2 + c // 16, c % 4, (c // 4) % 4, w % 2


def dev(x, y, z, core):
    return ((x % 2) * 16 + z * 4 + y, (x // 2) * 2 + core)


def moved(place, axis, by):
    x, y, z, core = place
    if axis == "x":
        return dev((x + by + 4) % 4, y, z, core)
    if axis == "y":
        return dev(x, (y + by + 4) % 4, z, core)
    return dev(x, y, (z + by + 4) % 4, core)


def along(place, axis):
    return place["xyz".index(axis)]


def greet(devices):
    barrier = pltpu.get_barrier_semaphore()
    for device in devices:
        pl.semaphore_signal(barrier, inc=1, device_id=device, device_id_type=MESH)
    pl.semaphore_wait(barrier, len(devices))


class Sems:
    def __init__(self, send, recv):
        self.send, self.recv, self.at = send, recv, 0
        self.started = []

    def copy(self, src, dst, device):
        i = self.at
        self.at += 1
        return pltpu.make_async_remote_copy(
            src_ref=src,
            dst_ref=dst,
            send_sem=self.send.at[i],
            recv_sem=self.recv.at[i],
            device_id=device,
            device_id_type=MESH,
        )

    def start(self, src, dst, device):
        copy = self.copy(src, dst, device)
        copy.start()
        self.started.append(copy)
        return copy

    def finish(self):
        for copy in self.started:
            copy.wait_send()


def call(kernel, out_shape, scratch, n_sems, cid, args, specs=None):
    vmem = pl.BlockSpec(memory_space=pltpu.VMEM)
    outs = jax.tree.map(lambda _: vmem, out_shape)
    return pl.pallas_call(
        kernel,
        out_shape=out_shape,
        in_specs=specs if specs is not None else [vmem] * len(args),
        out_specs=outs,
        scratch_shapes=[
            *scratch,
            pltpu.SemaphoreType.DMA((n_sems,)),
            pltpu.SemaphoreType.DMA((n_sems,)),
        ],
        compiler_params=pltpu.CompilerParams(
            collective_id=cid, has_side_effects=True, vmem_limit_bytes=VLIM
        ),
    )(*args)


def pair_of(place):
    x, y, z, core = place
    return dev(x, y, z, 1 - core), dev(3 - x, y, z, core)


def group_kernel(a_ref, out_ref, local_sem, send, recv):
    place = my_place()
    core = place[3]
    sibling, cross = pair_of(place)
    greet([sibling, cross])
    sems = Sems(send, recv)
    pieces = [pl.ds(64 * i, 64) for i in range(4)]
    over = [sems.start(a_ref.at[p], out_ref.at[1, core, p], cross) for p in pieces]
    own = sems.start(a_ref, out_ref.at[0, core], sibling)
    keep = pltpu.make_async_copy(a_ref, out_ref.at[0, core], local_sem.at[0])
    keep.start()
    passed = []
    for copy, p in zip(over, pieces):
        copy.wait_recv()
        passed.append(sems.start(out_ref.at[1, core, p], out_ref.at[1, core, p], sibling))
    for copy in [own, *passed]:
        copy.wait_recv()
    keep.wait()
    sems.finish()


def group_gather(array, cid):
    return call(
        group_kernel,
        jax.ShapeDtypeStruct((2, 2, *array.shape), array.dtype),
        [pltpu.SemaphoreType.DMA((1,))],
        9,
        cid,
        (array,),
    )


def group_sum_kernel(p_ref, out_ref, got, total, far, send, recv):
    place = my_place()
    core = place[3]
    sibling, cross = pair_of(place)
    greet([sibling, cross])
    sems = Sems(send, recv)
    in_other = [sems.start(p_ref.at[1, h, 1 - core], got.at[1, h], sibling) for h in range(2)]
    in_own = [sems.start(p_ref.at[0, h, 1 - core], got.at[0, h], sibling) for h in range(2)]
    over = []
    for h in range(2):
        in_other[h].wait_recv()
        total[1, h] = (p_ref[1, h, core].astype(f32) + got[1, h].astype(f32)).astype(bf16)
        over.append(sems.start(total.at[1, h], far.at[h], cross))
    last = []
    for h in range(2):
        in_own[h].wait_recv()
        over[h].wait_recv()
        out_ref[h, core] = (
            p_ref[0, h, core].astype(f32) + got[0, h].astype(f32) + far[h].astype(f32)
        ).astype(bf16)
        last.append(sems.start(out_ref.at[h, core], out_ref.at[h, core], sibling))
    for copy in last:
        copy.wait_recv()
    sems.finish()


def group_sum(part, cid):
    rows = (2, 64, D)
    return call(
        group_sum_kernel,
        jax.ShapeDtypeStruct((2, 2, 64, D), bf16),
        [pltpu.VMEM((2, *rows), bf16), pltpu.VMEM((2, *rows), bf16), pltpu.VMEM(rows, bf16)],
        8,
        cid,
        (part,),
    )


orders = (("z", "y", "x"), ("y", "x", "z"), ("x", "z", "y"))


def chips(ref, place, free, axis, at, rows):
    x, y, z, _ = place
    index = {"x": x, "y": y, "z": z}
    index[axis] = at
    every = slice(None)
    xlo, xhi = (every, every) if "x" in free else (index["x"] % 2, index["x"] // 2)
    return ref.at[
        xlo, every if "z" in free else index["z"], every if "y" in free else index["y"], xhi, rows
    ]


def swapped(values):
    width = values.shape[1]
    first = lanes(values.shape) % HD < HD // 2
    return jnp.where(first, pltpu.roll(values, width - 32, 1), pltpu.roll(values, 32, 1))


def opening_kernel(
    tok, cot, w_ref, small, turn, mark, t_out, w_out, s_out, q_out, all_ref, local_sem, send, recv
):
    place = my_place()
    x, y, z, core = place
    sibling, cross = pair_of(place)
    mate = dev(x + 1 - 2 * (x % 2), y, z, core)
    greet([sibling] + [moved(place, a, b) for a in "xyz" for b in (1, -1)])
    sems = Sems(send, recv)
    mine = (x // 2) * 2 + core
    theirs = (1 - x // 2) * 2 + core
    cut = ((0, 48), (48, 64))
    got, sent = (x % 2) * 112, (1 - x % 2) * 112

    def rows(start, at, size):
        return pl.ds(pl.multiple_of(start + at, 16), size)

    mark_rows = pl.ds(CHIP, KROWS - CHIP)
    here = all_ref.at[x % 2, z, y, x // 2]
    own = [sems.start(ref, t_out.at[i, :, core], sibling) for i, ref in enumerate((tok, cot))]
    over = [
        sems.start(w_ref.at[rows(sent, at, n)], w_out.at[mine, rows(sent, at, n)], cross)
        for at, n in cut
    ]
    over_small = sems.start(small, s_out.at[mine], cross)
    own += [sems.start(w_ref, w_out.at[mine], sibling), sems.start(small, s_out.at[mine], sibling)]
    keep = [
        pltpu.make_async_copy(tok, t_out.at[0, :, core], local_sem.at[0]),
        pltpu.make_async_copy(cot, t_out.at[1, :, core], local_sem.at[1]),
        pltpu.make_async_copy(w_ref, w_out.at[mine], local_sem.at[2]),
        pltpu.make_async_copy(small, s_out.at[mine], local_sem.at[3]),
        pltpu.make_async_copy(mark, here.at[mark_rows], local_sem.at[4]),
    ]
    for copy in keep:
        copy.start()
    shared, passed = [], []
    for copy, (at, n) in zip(over, cut):
        copy.wait_recv()
        piece = w_out.at[theirs, rows(got, at, n)]
        shared.append(sems.start(piece, piece, mate))
        passed.append(sems.start(piece, piece, sibling))
    over_small.wait_recv()
    passed.append(sems.start(s_out.at[theirs], s_out.at[theirs], sibling))
    for copy in keep:
        copy.wait()
    own[0].wait_recv()
    resid = t_out[0].reshape(CHIP, D).astype(f32)
    for copy, (at, n) in zip(shared, cut):
        copy.wait_recv()
        piece = w_out.at[theirs, rows(sent, at, n)]
        passed.append(sems.start(piece, piece, sibling))
    for copy in own[1:] + passed:
        copy.wait_recv()
    vectors = jnp.sum(s_out[...].astype(f32), 0)
    inverse = lax.rsqrt(jnp.mean(resid * resid, -1, keepdims=True) + norm_eps)
    normed = (resid * inverse * vectors[1:2, :D]).astype(bf16)
    projected = jnp.dot(
        normed, w_out[...].reshape(D, QKV), preferred_element_type=f32
    ) + vectors[0:1]
    first = core == 0
    queries = jnp.where(first, projected[:, :QC], projected[:, QC : 2 * QC])
    keys = projected[:, H * HD : H * HD + KVH * HD]
    keys = jnp.where(first, keys, pltpu.roll(keys, HD, 1))
    values = projected[:, (H + KVH) * HD :]
    values = jnp.where(first, pltpu.roll(values, HD, 1), values)
    cosine, sine = turn[0], turn[1]
    keys = keys * cosine + swapped(keys) * sine
    wide_turn = [jnp.concatenate([t] * 4, 1)[:, :QC] for t in (cosine, sine)]
    padded = jnp.concatenate([queries, jnp.zeros((CHIP, HD), f32)], 1)
    queries = queries * wide_turn[0] + swapped(padded)[:, :QC] * wide_turn[1]
    q_out[...] = queries.astype(bf16).reshape(2, 128, QC)
    here[0:CHIP, :] = jnp.where(lanes((CHIP, 128)) < HD, keys, values).astype(bf16)

    parts = [(0, 48, 48), (96, 48, 48), (192, 48, 32)]
    for stage in range(3):
        firsts = []
        for (row, n0, n1), order in zip(parts, orders):
            axis, free = order[stage], order[:stage]
            at = along(place, axis)
            block = chips(all_ref, place, free, axis, at, pl.ds(row, n0 + n1))
            firsts.append(
                [sems.start(block, block, moved(place, axis, by)) for by in (1, -1)]
            )
        seconds = []
        for (row, n0, n1), order, (to_right, to_left) in zip(parts, orders, firsts):
            axis, free = order[stage], order[:stage]
            at = along(place, axis)
            to_right.wait_recv()
            left = chips(all_ref, place, free, axis, (at + 3) % 4, pl.ds(row, n0))
            seconds.append(sems.start(left, left, moved(place, axis, 1)))
            to_left.wait_recv()
            right = chips(all_ref, place, free, axis, (at + 1) % 4, pl.ds(row + n0, n1))
            seconds.append(sems.start(right, right, moved(place, axis, -1)))
        for copy in seconds:
            copy.wait_recv()
    sems.finish()


def opening(tokens, out_grad, weight, small, turn, mark, cid):
    return call(
        opening_kernel,
        (
            jax.ShapeDtypeStruct((2, 2, 2, 64, D), bf16),
            jax.ShapeDtypeStruct((4, 224, QKV), bf16),
            jax.ShapeDtypeStruct((4, 16, QKV), bf16),
            jax.ShapeDtypeStruct((2, 128, QC), bf16),
            jax.ShapeDtypeStruct((2, 4, 4, 2, KROWS, 128), bf16),
        ),
        [pltpu.SemaphoreType.DMA((5,))],
        50,
        cid,
        (tokens.reshape(2, 64, D), out_grad.reshape(2, 64, D), weight, small, turn, mark),
    )


def added(into, terms, shape):
    if not shape:
        into[...] = sum([t[...].astype(f32) for t in terms], into[...].astype(f32)).astype(bf16)
        return

    def one(i, carry):
        rest, index = i, []
        for size in reversed(shape):
            index.insert(0, rest % size)
            rest = rest // size
        index = tuple(index)
        into[index] = sum(
            [t[index].astype(f32) for t in terms], into[index].astype(f32)
        ).astype(bf16)
        return carry

    lax.fori_loop(0, math.prod(shape), one, 0)


def ring_sum(place, sems, jobs):
    state = []
    for axis, view, land, shape in jobs:
        at = along(place, axis)
        right, left = moved(place, axis, 1), moved(place, axis, -1)
        far = (at + 2) % 4
        state.append(
            (
                sems.start(view(far, 1), land[0], right),
                sems.start(view(far, 0), land[1], left),
                sems.start(view((at + 1) % 4, 0), land[2], right),
                sems.start(view((at + 3) % 4, 1), land[3], left),
            )
        )
    lasts = []
    for (axis, view, land, shape), (far_right, far_left, _, _) in zip(jobs, state):
        at = along(place, axis)
        right, left = moved(place, axis, 1), moved(place, axis, -1)
        far_right.wait_recv()
        added(view((at + 1) % 4, 1), [land[0]], shape)
        one = sems.start(view((at + 1) % 4, 1), land[4], right)
        far_left.wait_recv()
        added(view((at + 3) % 4, 0), [land[1]], shape)
        lasts.append((one, sems.start(view((at + 3) % 4, 0), land[5], left)))
    for (axis, view, land, shape), (_, _, near_r, near_l), (one, two) in zip(jobs, state, lasts):
        at = along(place, axis)
        near_r.wait_recv()
        two.wait_recv()
        added(view(at, 0), [land[2], land[5]], shape)
        near_l.wait_recv()
        one.wait_recv()
        added(view(at, 1), [land[3], land[4]], shape)


sum_parts = [(0, 48, 48), (96, 48, 48), (192, 32, 32)]


def kv_shape(free):
    lead = ()
    if "x" in free:
        lead += (2,)
    if "z" in free:
        lead += (4,)
    if "y" in free:
        lead += (4,)
    if "x" in free:
        lead += (2,)
    return lead


def closing_kernel(part_ref, dq_ref, turn, out_ref, work, own, group, local_sem, *rest):
    lands, (send, recv) = rest[:-2], rest[-2:]
    place = my_place()
    x, y, z, core = place
    sibling, cross = pair_of(place)
    greet([sibling] + [moved(place, a, b) for a in "xyz" for b in (1, -1)])
    keep = pltpu.make_async_copy(part_ref, work, local_sem.at[0])
    keep.start()
    keep.wait()
    sems = Sems(send, recv)
    at_land = 0
    for stage in range(3):
        jobs = []
        for (row, n0, n1), order in zip(sum_parts, orders):
            axis, free = order[stage], order[stage + 1 :]

            def view(at, half, row=row, n0=n0, n1=n1, axis=axis, free=free):
                rows = pl.ds(row, n0) if half == 0 else pl.ds(row + n0, n1)
                return chips(work, place, free, axis, at, rows)

            jobs.append((axis, view, lands[at_land : at_land + 6], kv_shape(free)))
            at_land += 6
        ring_sum(place, sems, jobs)
    grads = work[x % 2, z, y, x // 2].astype(f32)
    cosine, sine = turn[0], turn[1]
    keys = grads * cosine - swapped(grads) * sine
    dq = dq_ref[...].reshape(CHIP, QC)
    padded = jnp.concatenate([dq, jnp.zeros((CHIP, HD), f32)], 1)
    wide_turn = [jnp.concatenate([t] * 4, 1)[:, :QC] for t in (cosine, sine)]
    queries = dq * wide_turn[0] - swapped(padded)[:, :QC] * wide_turn[1]
    lane = lanes((CHIP, 128))
    both = jnp.where(lane < HD, keys, grads)
    own[...] = jnp.concatenate([queries, jnp.zeros((CHIP, HD), f32), both], 1).astype(bf16)
    pieces = [pl.ds(64 * i, 64) for i in range(4)]
    over = [sems.start(own.at[p], group.at[1, core, p], cross) for p in pieces]
    beside = sems.start(own, group.at[0, core], sibling)
    group[0, core] = own[...]
    passed = []
    for copy, p in zip(over, pieces):
        copy.wait_recv()
        passed.append(sems.start(group.at[1, core, p], group.at[1, core, p], sibling))

    def put(chip):
        low, high = group[chip, 0].astype(f32), group[chip, 1].astype(f32)
        low_kv, high_kv = low[:, 512:], high[:, 512:]
        out_ref[chip] = jnp.concatenate(
            [
                low[:, :QC],
                high[:, :QC],
                jnp.where(lane < HD, low_kv, pltpu.roll(high_kv, HD, 1)),
                jnp.where(lane < HD, pltpu.roll(low_kv, HD, 1), high_kv),
            ],
            1,
        ).astype(bf16)

    beside.wait_recv()
    put(0)
    for copy in passed:
        copy.wait_recv()
    put(1)
    sems.finish()


def closing(part, dq, turn, cid):
    lands = []
    for stage in range(3):
        for (row, n0, n1), order in zip(sum_parts, orders):
            lead = kv_shape(order[stage + 1 :])
            for n in (n1, n0, n0, n1, n1, n0):
                lands.append(pltpu.VMEM((*lead, n, 128), bf16))
    shape = (2, 4, 4, 2, CHIP, 128)
    return call(
        closing_kernel,
        jax.ShapeDtypeStruct((2, CHIP, QKV), bf16),
        [
            pltpu.VMEM(shape, bf16),
            pltpu.VMEM((CHIP, 640), bf16),
            pltpu.VMEM((2, 2, CHIP, 640), bf16),
            pltpu.SemaphoreType.DMA((1,)),
            *lands,
        ],
        63,
        cid,
        (part, dq, turn),
    )


weight_parts = [(0, 80, 64, "zy"), (144, 64, 64, "yz")]


def weight_view(ref, place, first, at, rows, second=None):
    _, y, z, _ = place
    every = slice(None)
    if second is None:
        return ref.at[at, every, rows] if first == "z" else ref.at[every, at, rows]
    return ref.at[z, at, rows] if first == "z" else ref.at[at, y, rows]


def weight_kernel(part_ref, out_ref, work, local_sem, *more):
    lands, (send, recv) = more[:-2], more[-2:]
    place = my_place()
    x, y, z, core = place
    mate = dev(x + 1 - 2 * (x % 2), y, z, core)
    load = pltpu.make_async_copy(part_ref, work, local_sem.at[0])
    load.start()
    greet([moved(place, a, b) for a in "yz" for b in (1, -1)] + [mate])
    load.wait()
    sems = Sems(send, recv)
    at_land = 0
    for stage in range(2):
        jobs = []
        for row, n0, n1, order in weight_parts:

            def view(at, half, row=row, n0=n0, n1=n1, order=order, stage=stage):
                rows = pl.ds(row, n0) if half == 0 else pl.ds(row + n0, n1)
                second = order[1] if stage == 1 else None
                return weight_view(work, place, order[0], at, rows, second)

            jobs.append(
                (order[stage], view, lands[at_land : at_land + 6], (4,) if stage == 0 else ())
            )
            at_land += 6
        ring_sum(place, sems, jobs)
    swaps = []
    for row, n0, n1, order in weight_parts:
        mine = work.at[z, y, pl.ds(row, n0 + n1)]
        swaps.append(sems.start(mine, lands[at_land], mate))
        at_land += 1
    for i, ((row, n0, n1, order), copy) in enumerate(zip(weight_parts, swaps)):
        copy.wait_recv()
        rows = pl.ds(row, n0 + n1)
        land = lands[at_land - len(weight_parts) + i]
        out_ref[z, y, rows] = (
            work[z, y, rows].astype(f32) + land[...].astype(f32)
        ).astype(bf16)
    for stage in (1, 0):
        firsts = []
        for row, n0, n1, order in weight_parts:
            axis = order[stage]
            rows = pl.ds(row, n0 + n1)
            second = order[1] if stage == 1 else None
            here = weight_view(out_ref, place, order[0], along(place, axis), rows, second)
            firsts.append([sems.start(here, here, moved(place, axis, by)) for by in (1, -1)])
        seconds = []
        for (row, n0, n1, order), (to_right, to_left) in zip(weight_parts, firsts):
            axis = order[stage]
            at = along(place, axis)
            second = order[1] if stage == 1 else None
            to_right.wait_recv()
            left = weight_view(out_ref, place, order[0], (at + 3) % 4, pl.ds(row, n0), second)
            seconds.append(sems.start(left, left, moved(place, axis, 1)))
            to_left.wait_recv()
            right = weight_view(
                out_ref, place, order[0], (at + 1) % 4, pl.ds(row + n0, n1), second
            )
            seconds.append(sems.start(right, right, moved(place, axis, -1)))
        for copy in seconds:
            copy.wait_recv()
    sems.finish()


def weight_sum(part, cid):
    lands = []
    for stage in range(2):
        for row, n0, n1, order in weight_parts:
            lead = (4,) if stage == 0 else ()
            for n in (n1, n0, n0, n1, n1, n0):
                lands.append(pltpu.VMEM((*lead, n, D), bf16))
    for row, n0, n1, order in weight_parts:
        lands.append(pltpu.VMEM((n0 + n1, D), bf16))
    big = (4, 4, 272, D)
    return call(
        weight_kernel,
        jax.ShapeDtypeStruct(big, bf16),
        [pltpu.VMEM(big, bf16), pltpu.SemaphoreType.DMA((1,)), *lands],
        len(weight_parts) * (6 * 2 + 1 + 4 * 2),
        cid,
        (part.reshape(big),),
        [pl.BlockSpec(memory_space=pl.ANY)],
    )


NT = (((1,), (1,)), ((), ()))
ROWS = G * 128


def lanes(shape):
    return lax.broadcasted_iota(jnp.int32, shape, len(shape) - 1)


def split3(value):
    one = value.astype(bf16).astype(f32)
    two = (value - one).astype(bf16).astype(f32)
    three = (value - one - two).astype(bf16).astype(f32)
    return one, two, three


def keys_of(kv_ref, c, half):
    rows = pl.ds(pl.multiple_of(half * 128, 128), 128)
    tile = kv_ref[c, :, rows, :].reshape(256, 128)
    lane = lanes((256, 128))
    ones = jnp.ones((256, 128), bf16)
    return jnp.where(lane < HD, tile, ones), jnp.where(lane < HD, ones, tile)


def hidden_keys(xhi):
    row = lax.broadcasted_iota(jnp.int32, (ROWS, 256), 0) % 128
    key = lax.broadcasted_iota(jnp.int32, (ROWS, 256), 1)
    return key > row + xhi * 128


def forward_kernel(scal, q_ref, kv_ref, o_ref, qe_ref, peak, acc):
    me, xhi = scal[32], scal[33]
    lane = lanes((128, 128))
    for h in range(2):
        for g in range(G):
            piece = q_ref[h, :, g * HD : (g + 1) * HD].astype(f32) * (1.0 / math.sqrt(HD))
            wide_piece = jnp.concatenate([piece, jnp.zeros((128, HD), f32)], 1)
            qe_ref[h, g * 128 : (g + 1) * 128, :] = wide_piece.astype(bf16)
    peak[...] = jnp.full((2, ROWS, 128), -1e30, f32)
    acc[...] = jnp.zeros((2, ROWS, 128), f32)

    def scores(half, kk):
        return lax.dot_general(qe_ref[half], kk, NT, preferred_element_type=f32)

    def top(half, s):
        peak[half] = jnp.maximum(peak[half], jnp.maximum(s[:, :128], s[:, 128:]))

    def fold(half, s, vv):
        p = jnp.exp(s).astype(bf16)
        acc[half] += jnp.dot(p, vv, preferred_element_type=f32)

    def others(work):
        def one(i, carry):
            c = (me + i) % 32
            kk, vv = keys_of(kv_ref, c, 0)
            work(1, kk, vv, None)
            sel = scal[c]
            kk, vv = keys_of(kv_ref, c, sel)
            work(sel, kk, vv, None)
            return carry

        lax.fori_loop(1, 32, one, 0)
        early_k, early_v = keys_of(kv_ref, me, 0)
        late_k, late_v = keys_of(kv_ref, me, 1)
        work(1, early_k, early_v, None)
        work(0, early_k, early_v, hidden_keys(xhi))
        work(1, late_k, late_v, hidden_keys(xhi))

    def first(half, kk, vv, hide):
        s = scores(half, kk)
        top(half, s if hide is None else jnp.where(hide, -1e30, s))

    def second(half, kk, vv, hide):
        s = scores(half, kk)
        fold(half, s if hide is None else jnp.where(hide, -1e30, s), vv)

    others(first)
    wide_lane = lanes((ROWS, 128))

    def with_column(half, column):
        one, two, three = split3(-column)
        held = qe_ref[half].astype(f32)
        held = jnp.where(wide_lane == HD, one, held)
        held = jnp.where(wide_lane == HD + 1, two, held)
        held = jnp.where(wide_lane == HD + 2, three, held)
        qe_ref[half] = held.astype(bf16)

    for h in range(2):
        highest = jnp.max(peak[h], 1, keepdims=True)
        peak[h] = jnp.broadcast_to(highest, (ROWS, 128))
        with_column(h, highest)
    others(second)
    for h in range(2):
        total = acc[h][:, :1]
        with_column(h, peak[h][:, :1] + jnp.log(total))
        out = acc[h] / total
        for g in range(G):
            o_ref[h, :, g * HD : (g + 1) * HD] = out[g * 128 : (g + 1) * 128, HD:]


def local_call(kernel, out_shape, scratch, args, flops):
    vmem = pl.BlockSpec(memory_space=pltpu.VMEM)
    return pl.pallas_call(
        kernel,
        out_shape=out_shape,
        in_specs=[pl.BlockSpec(memory_space=pltpu.SMEM)] + [vmem] * (len(args) - 1),
        out_specs=jax.tree.map(lambda _: vmem, out_shape),
        scratch_shapes=scratch,
        compiler_params=pltpu.CompilerParams(vmem_limit_bytes=VLIM),
        cost_estimate=pl.CostEstimate(
            flops=flops, bytes_accessed=10_000_000, transcendentals=15_000_000
        ),
    )(*args)


def attention_forward(scal, q, kv):
    return local_call(
        forward_kernel,
        (
            jax.ShapeDtypeStruct((2, 128, QC), f32),
            jax.ShapeDtypeStruct((2, ROWS, 128), bf16),
        ),
        [pltpu.VMEM((2, ROWS, 128), f32), pltpu.VMEM((2, ROWS, 128), f32)],
        (scal, q, kv),
        20_000_000_000,
    )


def backward_kernel(scal, qe_ref, o_ref, g_ref, kv_ref, dq_ref, dkv_ref, ge, qt, gt, dq, step):
    me, xhi = scal[32], scal[33]
    lane = lanes((128, 128))
    for h in range(2):
        for g in range(G):
            cols = slice(g * HD, (g + 1) * HD)
            piece = g_ref[h, :, cols].astype(f32)
            delta = jnp.sum(piece * o_ref[h, :, cols], 1, keepdims=True)
            one, two, three = split3(-delta)
            held = jnp.concatenate([jnp.zeros((128, HD), f32), piece], 1)
            held = jnp.where(lane == 0, one, held)
            held = jnp.where(lane == 1, two, held)
            held = jnp.where(lane == 2, three, held)
            rows = slice(g * 128, (g + 1) * 128)
            ge[h, rows, :] = held.astype(bf16)
            gt[h, :, rows] = held.T.astype(bf16)
            qt[h, :, rows] = qe_ref[h, rows, :].astype(f32).T.astype(bf16)
    dq[...] = jnp.zeros((2, ROWS, 128), f32)
    under = lax.broadcasted_iota(jnp.int32, (128, 256), 0) < HD

    def tile(half, kk, vv, hide):
        s = lax.dot_general(qe_ref[half], kk, NT, preferred_element_type=f32)
        if hide is not None:
            s = jnp.where(hide, -1e30, s)
        p = jnp.exp(s)
        dp = lax.dot_general(ge[half], vv, NT, preferred_element_type=f32)
        ds = (p * dp).astype(bf16)
        dq[half] += jnp.dot(ds, kk, preferred_element_type=f32)
        dk = jnp.dot(qt[half], ds, preferred_element_type=f32)
        dv = jnp.dot(gt[half], p.astype(bf16), preferred_element_type=f32)
        return jnp.where(under, dk, dv).T

    def put(c, half, value):
        rows = pl.ds(pl.multiple_of(half * 128, 128), 128)
        dkv_ref[c, :, rows, :] = value.astype(bf16).reshape(2, 128, 128)

    def one(i, carry):
        c = (me + i) % 32
        kk, vv = keys_of(kv_ref, c, 0)
        step[0] = tile(1, kk, vv, None)
        step[1] = jnp.zeros((256, 128), f32)
        sel = scal[c]
        kk, vv = keys_of(kv_ref, c, sel)
        step[sel] += tile(sel, kk, vv, None)
        put(c, 0, step[0])
        put(c, 1, step[1])
        return carry

    lax.fori_loop(1, 32, one, 0)
    early_k, early_v = keys_of(kv_ref, me, 0)
    late_k, late_v = keys_of(kv_ref, me, 1)
    put(
        me,
        0,
        tile(1, early_k, early_v, None) + tile(0, early_k, early_v, hidden_keys(xhi)),
    )
    put(me, 1, tile(1, late_k, late_v, hidden_keys(xhi)))
    for h in range(2):
        for g in range(G):
            dq_ref[h, :, g * HD : (g + 1) * HD] = dq[h, g * 128 : (g + 1) * 128, :HD] * (
                1.0 / math.sqrt(HD)
            )


def attention_backward(scal, qe, o, grad, kv):
    return local_call(
        backward_kernel,
        (
            jax.ShapeDtypeStruct((2, 128, QC), f32),
            jax.ShapeDtypeStruct((32, 2, CHIP, 128), bf16),
        ),
        [
            pltpu.VMEM((2, ROWS, 128), bf16),
            pltpu.VMEM((2, 128, ROWS), bf16),
            pltpu.VMEM((2, 128, ROWS), bf16),
            pltpu.VMEM((2, ROWS, 128), f32),
            pltpu.VMEM((2, 256, 128), f32),
        ],
        (scal, qe, o, grad, kv),
        50_000_000_000,
    )


def rms_inverse(values):
    return lax.rsqrt(jnp.mean(values * values, -1, keepdims=True) + norm_eps)


def rms_pull(values, inverse, gain, grad):
    scaled = values * inverse
    e = grad * gain
    return inverse * (e - scaled * jnp.mean(e * scaled, -1, keepdims=True))


def rotation(positions):
    lane = jnp.arange(128)
    frequency = rope_base ** (-(2.0 * (lane % 32).astype(f32)) / HD)
    angles = positions.astype(f32)[:, None] * frequency[None, :]
    sign = jnp.where(lane % HD < HD // 2, -1.0, 1.0)
    return jnp.stack([jnp.cos(angles), jnp.sin(angles) * sign])


def dot(a, b):
    return jnp.dot(a, b, preferred_element_type=f32)


def body(
    tokens,
    out_grad,
    norm1_gain,
    qkv_weight,
    qkv_bias,
    out_weight,
    norm2_gain,
    gate_weight,
    up_weight,
    down_weight,
    positions,
):
    ctx = lax.axis_index("ctx")
    wsh = lax.axis_index("wsh")
    xhi, core = wsh // 2, wsh % 2
    my_block = positions[0] // 256

    def cut(array, start, size, axis):
        return lax.dynamic_slice_in_dim(array, start, size, axis)

    def own_rows(array):
        return cut(array.reshape(2, 2, 64, -1), core, 1, 1).reshape(TOK, -1)

    swap = [
        (c * 4 + w, ((c + 16) % 32) * 4 + (w + 2) % 4) for c in range(32) for w in range(4)
    ]
    twin = [(c * 4 + w, c * 4 + w + 1 - 2 * (w % 2)) for c in range(32) for w in range(4)]

    def crossed(array):
        return lax.ppermute(array, ("ctx", "wsh"), swap)

    def spread(vector, width):
        column = jnp.arange(QKV)
        values = jnp.pad(jnp.tile(vector, 4), (0, QKV - 4 * width))
        return jnp.where(column // width == wsh, values, 0)

    small = jnp.stack([spread(qkv_bias, 288), spread(norm1_gain, 224), spread(norm2_gain, 224)])
    small = jnp.pad(small, ((0, 13), (0, 0))).astype(bf16)
    offset = jnp.arange(128, dtype=jnp.int32) + xhi * 128
    turn = rotation(jnp.concatenate([my_block * 256 + offset, (63 - my_block) * 256 + offset]))
    mark = jnp.broadcast_to(my_block.astype(bf16), (KROWS - CHIP, 128))
    t_all, w_all, s_all, queries, kv_all = opening(
        tokens, out_grad, qkv_weight, small, turn, mark, 0
    )
    out_weight, kv_all = lax.optimization_barrier((out_weight, kv_all))
    out_full = lax.all_gather(out_weight, "wsh", axis=0, tiled=True)
    qkv_full = w_all.reshape(D, QKV)
    vectors = jnp.sum(s_all[:, 1:3, :D].astype(f32), 0)
    gain_one, gain_two = vectors[0], vectors[1]
    t_chip = t_all.reshape(2, CHIP, D)
    kv_all = kv_all.reshape(32, 2, KROWS, 128)
    blocks = kv_all[:, 0, CHIP, 0].astype(jnp.int32)
    scal = jnp.concatenate(
        [(blocks > my_block).astype(jnp.int32), jnp.stack([ctx, xhi]).astype(jnp.int32)]
    )
    t_chip, kv_all = lax.optimization_barrier((t_chip, kv_all))
    t_other = crossed(t_chip)
    attended_f, qe = attention_forward(scal, queries, kv_all)
    att = group_gather(attended_f.astype(bf16).reshape(CHIP, QC), 2)
    t_both = jnp.stack([t_chip, t_other], 1).reshape(2, 2 * CHIP, D)
    resid_both = t_both[0].astype(f32)
    cot = t_both[1]
    att_cols = [att[:, i].reshape(2 * CHIP, QC) for i in range(2)]
    stream = resid_both + dot(att_cols[0], out_full[:QC]) + dot(att_cols[1], out_full[QC:])
    inv_two = rms_inverse(stream)
    normed_two = (stream * inv_two * gain_two).astype(bf16)
    gate_pre = dot(normed_two, gate_weight)
    up_pre = dot(normed_two, up_weight)
    hidden_grad = jnp.einsum("td,fd->tf", cot, down_weight, preferred_element_type=f32)
    sigma = jax.nn.sigmoid(gate_pre)
    activated = gate_pre * sigma
    hidden = (activated * up_pre).astype(bf16)
    gate_grad = (hidden_grad * up_pre * sigma * (1.0 + gate_pre * (1.0 - sigma))).astype(bf16)
    up_grad = (hidden_grad * activated).astype(bf16)
    norm_part = jnp.einsum(
        "tf,df->td", gate_grad, gate_weight, preferred_element_type=f32
    ) + jnp.einsum("tf,df->td", up_grad, up_weight, preferred_element_type=f32)
    norm_grad = group_sum(norm_part.astype(bf16).reshape(2, 2, 2, 64, D), 3).reshape(CHIP, D)

    mlp_part = dot(hidden, down_weight).astype(bf16).reshape(2, 2, 2, 64, D)
    norm_other = crossed(norm_grad)
    mlp_got = lax.ppermute(cut(mlp_part, 1 - core, 1, 2), ("ctx", "wsh"), twin)
    mlp_sum = cut(mlp_part, core, 1, 2).astype(f32) + mlp_got.astype(f32)
    mlp_far = crossed(mlp_sum[1].astype(bf16))
    mlp_own = (mlp_sum[0] + mlp_far.astype(f32)).reshape(TOK, D)
    output = (own_rows(stream[:CHIP]) + mlp_own).astype(bf16)
    gate_wgrad = jnp.einsum("tf,td->fd", gate_grad, normed_two, preferred_element_type=f32)
    up_wgrad = jnp.einsum("tf,td->fd", up_grad, normed_two, preferred_element_type=f32)
    down_wgrad = jnp.einsum("tf,td->fd", hidden, cot, preferred_element_type=f32)

    def stream_pull(part, grad):
        rows = slice(part * CHIP, (part + 1) * CHIP)
        return cot[rows].astype(f32) + rms_pull(
            stream[rows], inv_two[rows], gain_two, grad.astype(f32)
        )

    stream_grad = stream_pull(0, norm_grad)
    branch_grad = stream_grad.astype(bf16)
    att_grad = jnp.einsum(
        "td,id->ti", branch_grad, cut(out_full, core * QC, QC, 0), preferred_element_type=f32
    ).astype(bf16)
    dq, dkv_part = attention_backward(
        scal, qe, attended_f, att_grad.reshape(2, 128, QC), kv_all
    )
    pg = closing(dkv_part.reshape(2, 4, 4, 2, CHIP, 128), dq, turn, 4).reshape(2 * CHIP, QKV)

    bias_grad = cut(jnp.sum(pg.astype(f32), 0), wsh * 288, 288, 0)
    inv_one = rms_inverse(resid_both)
    scaled_one = cut(resid_both, wsh * 224, 224, 1) * inv_one
    normed_cols = (scaled_one * norm1_gain.astype(f32)).astype(bf16)
    qkv_wgrad = jnp.einsum("td,tf->df", normed_cols, pg, preferred_element_type=f32)
    one_cols = jnp.einsum("tf,df->td", pg, qkv_weight, preferred_element_type=f32)
    gain_one_grad = jnp.sum(one_cols * scaled_one, 0)
    branch_both = jnp.concatenate(
        [branch_grad, stream_pull(1, norm_other).astype(bf16)], 0
    )
    norm_both = jnp.concatenate([norm_grad, norm_other], 0)
    scaled_two = cut(stream, wsh * 224, 224, 1) * inv_two
    gain_two_grad = jnp.sum(cut(norm_both, wsh * 224, 224, 1).astype(f32) * scaled_two, 0)
    att_mine = cut(jnp.where(wsh < 2, att_cols[0], att_cols[1]), (wsh % 2) * 224, 224, 1)
    out_wgrad = jnp.einsum("ti,td->id", att_mine, branch_both, preferred_element_type=f32)
    pg_own = own_rows(pg[:CHIP])
    one_grad = jnp.einsum("tf,df->td", pg_own, qkv_full, preferred_element_type=f32)
    resid_own = tokens.astype(f32)
    token_grad = own_rows(stream_grad) + rms_pull(
        resid_own, rms_inverse(resid_own), gain_one, one_grad
    )
    vectors = jnp.stack(
        [jnp.pad(v, (0, D - v.shape[0])) for v in (bias_grad, gain_one_grad, gain_two_grad)]
    )
    part = jnp.concatenate(
        [
            *[w.astype(bf16) for w in (gate_wgrad, up_wgrad, down_wgrad, out_wgrad)],
            qkv_wgrad.astype(bf16).reshape(288, D),
            jnp.pad(vectors, ((0, 189), (0, 0))).astype(bf16),
        ],
        0,
    )
    total = weight_sum(part, 6).reshape(16 * 272, D).astype(f32)
    return (
        output,
        token_grad,
        total[4161, :224],
        total[3872:4160].reshape(224, QKV),
        total[4160, :288],
        total[3648:3872],
        total[4162, :224],
        total[:1216].T,
        total[1216:2432].T,
        total[2432:3648],
    )


def solution(mesh):
    rows = P(("ctx", "wsh"), None)
    return jax.shard_map(
        body,
        mesh=mesh,
        in_specs=(
            rows,
            rows,
            P("wsh"),
            P("wsh", None),
            P("wsh"),
            P("wsh", None),
            P("wsh"),
            P(None, "wsh"),
            P(None, "wsh"),
            P("wsh", None),
            P(("ctx", "wsh")),
        ),
        out_specs=(
            rows,
            rows,
            P("wsh"),
            P("wsh", None),
            P("wsh"),
            P("wsh", None),
            P("wsh"),
            P(None, "wsh"),
            P(None, "wsh"),
            P("wsh", None),
        ),
        check_vma=False,
    )
```

```python
import functools
import math

import jax
import jax.numpy as jnp
from jax import lax
from jax.experimental import pallas as pl
from jax.experimental.pallas import tpu as pltpu
from jax.sharding import PartitionSpec as P

H = 14
KVH = 2
HD = 64
G = H // KVH
D = 896
FS = 1216
QKV = 1152
QC = G * HD
PC = QC + 2 * HD
TOK = 128
CHIP = 256
KROWS = 272

MESH = pl.DeviceIdType.MESH
VLIM = 56 * 1024 * 1024
norm_eps = 1e-06
rope_base = 1000000.0
f32 = jnp.float32
bf16 = jnp.bfloat16


def my_place():
    c = lax.axis_index("ctx")
    w = lax.axis_index("wsh")
    return (w // 2) * 2 + c // 16, c % 4, (c // 4) % 4, w % 2


def dev(x, y, z, core):
    return ((x % 2) * 16 + z * 4 + y, (x // 2) * 2 + core)


def moved(place, axis, by):
    x, y, z, core = place
    if axis == "x":
        return dev((x + by + 4) % 4, y, z, core)
    if axis == "y":
        return dev(x, (y + by + 4) % 4, z, core)
    return dev(x, y, (z + by + 4) % 4, core)


def along(place, axis):
    return place["xyz".index(axis)]


def greet(devices):
    barrier = pltpu.get_barrier_semaphore()
    for device in devices:
        pl.semaphore_signal(barrier, inc=1, device_id=device, device_id_type=MESH)
    pl.semaphore_wait(barrier, len(devices))


class Sems:
    def __init__(self, send, recv):
        self.send, self.recv, self.at = send, recv, 0
        self.started = []

    def copy(self, src, dst, device):
        i = self.at
        self.at += 1
        return pltpu.make_async_remote_copy(
            src_ref=src,
            dst_ref=dst,
            send_sem=self.send.at[i],
            recv_sem=self.recv.at[i],
            device_id=device,
            device_id_type=MESH,
        )

    def ready(self, src, dst, device):
        copy = self.copy(src, dst, device)
        self.started.append(copy)
        return copy

    def start(self, src, dst, device):
        copy = self.ready(src, dst, device)
        copy.start()
        return copy

    def finish(self):
        for copy in self.started:
            copy.wait_send()


def call(kernel, out_shape, scratch, n_sems, cid, args, specs=None):
    vmem = pl.BlockSpec(memory_space=pltpu.VMEM)
    outs = jax.tree.map(lambda _: vmem, out_shape)
    return pl.pallas_call(
        kernel,
        out_shape=out_shape,
        in_specs=specs if specs is not None else [vmem] * len(args),
        out_specs=outs,
        scratch_shapes=[
            *scratch,
            pltpu.SemaphoreType.DMA((n_sems,)),
            pltpu.SemaphoreType.DMA((n_sems,)),
        ],
        compiler_params=pltpu.CompilerParams(
            collective_id=cid, has_side_effects=True, vmem_limit_bytes=VLIM
        ),
    )(*args)


def pair_of(place):
    x, y, z, core = place
    return dev(x, y, z, 1 - core), dev(3 - x, y, z, core)


def group_kernel(a_ref, out_ref, local_sem, send, recv):
    place = my_place()
    core = place[3]
    sibling, cross = pair_of(place)
    greet([sibling, cross])
    sems = Sems(send, recv)
    pieces = [pl.ds(64 * i, 64) for i in range(4)]
    over = [sems.start(a_ref.at[p], out_ref.at[1, core, p], cross) for p in pieces]
    own = sems.start(a_ref, out_ref.at[0, core], sibling)
    keep = pltpu.make_async_copy(a_ref, out_ref.at[0, core], local_sem.at[0])
    keep.start()
    passed = []
    for copy, p in zip(over, pieces):
        copy.wait_recv()
        passed.append(sems.start(out_ref.at[1, core, p], out_ref.at[1, core, p], sibling))
    for copy in [own, *passed]:
        copy.wait_recv()
    keep.wait()
    sems.finish()


def group_gather(array, cid):
    return call(
        group_kernel,
        jax.ShapeDtypeStruct((2, 2, *array.shape), array.dtype),
        [pltpu.SemaphoreType.DMA((1,))],
        9,
        cid,
        (array,),
    )


def group_sum_kernel(p_ref, out_ref, got, total, far, send, recv):
    place = my_place()
    core = place[3]
    sibling, cross = pair_of(place)
    greet([sibling, cross])
    sems = Sems(send, recv)
    in_other = [sems.start(p_ref.at[1, h, 1 - core], got.at[1, h], sibling) for h in range(2)]
    in_own = [sems.start(p_ref.at[0, h, 1 - core], got.at[0, h], sibling) for h in range(2)]
    over = []
    for h in range(2):
        in_other[h].wait_recv()
        total[1, h] = (p_ref[1, h, core].astype(f32) + got[1, h].astype(f32)).astype(bf16)
        over.append(sems.start(total.at[1, h], far.at[h], cross))
    last = []
    for h in range(2):
        in_own[h].wait_recv()
        over[h].wait_recv()
        out_ref[h, core] = (
            p_ref[0, h, core].astype(f32) + got[0, h].astype(f32) + far[h].astype(f32)
        ).astype(bf16)
        last.append(sems.start(out_ref.at[h, core], out_ref.at[h, core], sibling))
    for copy in last:
        copy.wait_recv()
    sems.finish()


def group_sum(part, cid):
    rows = (2, 64, D)
    return call(
        group_sum_kernel,
        jax.ShapeDtypeStruct((2, 2, 64, D), bf16),
        [pltpu.VMEM((2, *rows), bf16), pltpu.VMEM((2, *rows), bf16), pltpu.VMEM(rows, bf16)],
        8,
        cid,
        (part,),
    )


orders = (("z", "y", "x"), ("y", "x", "z"), ("x", "z", "y"))


def chips(ref, place, free, axis, at, rows):
    x, y, z, _ = place
    index = {"x": x, "y": y, "z": z}
    index[axis] = at
    every = slice(None)
    xlo, xhi = (every, every) if "x" in free else (index["x"] % 2, index["x"] // 2)
    return ref.at[
        xlo, every if "z" in free else index["z"], every if "y" in free else index["y"], xhi, rows
    ]


def swapped(values):
    width = values.shape[1]
    first = lanes(values.shape) % HD < HD // 2
    return jnp.where(first, pltpu.roll(values, width - 32, 1), pltpu.roll(values, 32, 1))


def opening_kernel(
    tok, cot, w_ref, small, turn, mark, t_out, w_out, s_out, q_out, all_ref, local_sem, send, recv
):
    place = my_place()
    x, y, z, core = place
    sibling, cross = pair_of(place)
    mate = dev(x + 1 - 2 * (x % 2), y, z, core)
    greet([sibling] + [moved(place, a, b) for a in "xyz" for b in (1, -1)])
    sems = Sems(send, recv)
    mine = (x // 2) * 2 + core
    theirs = (1 - x // 2) * 2 + core
    cut = ((0, 48), (48, 64))
    got, sent = (x % 2) * 112, (1 - x % 2) * 112

    def rows(start, at, size):
        return pl.ds(pl.multiple_of(start + at, 16), size)

    mark_rows = pl.ds(CHIP, KROWS - CHIP)
    here = all_ref.at[x % 2, z, y, x // 2]
    own = [sems.start(ref, t_out.at[i, :, core], sibling) for i, ref in enumerate((tok, cot))]
    over = [
        sems.start(w_ref.at[rows(sent, at, n)], w_out.at[mine, rows(sent, at, n)], cross)
        for at, n in cut
    ]
    over_small = sems.start(small, s_out.at[mine], cross)
    own += [sems.start(w_ref, w_out.at[mine], sibling), sems.start(small, s_out.at[mine], sibling)]
    keep = [
        pltpu.make_async_copy(tok, t_out.at[0, :, core], local_sem.at[0]),
        pltpu.make_async_copy(cot, t_out.at[1, :, core], local_sem.at[1]),
        pltpu.make_async_copy(w_ref, w_out.at[mine], local_sem.at[2]),
        pltpu.make_async_copy(small, s_out.at[mine], local_sem.at[3]),
        pltpu.make_async_copy(mark, here.at[mark_rows], local_sem.at[4]),
    ]
    for copy in keep:
        copy.start()
    shared, passed = [], []
    for copy, (at, n) in zip(over, cut):
        copy.wait_recv()
        piece = w_out.at[theirs, rows(got, at, n)]
        shared.append(sems.start(piece, piece, mate))
        passed.append(sems.start(piece, piece, sibling))
    over_small.wait_recv()
    passed.append(sems.start(s_out.at[theirs], s_out.at[theirs], sibling))
    for copy in keep:
        copy.wait()
    own[0].wait_recv()
    resid = t_out[0].reshape(CHIP, D).astype(f32)
    for copy, (at, n) in zip(shared, cut):
        copy.wait_recv()
        piece = w_out.at[theirs, rows(sent, at, n)]
        passed.append(sems.start(piece, piece, sibling))
    for copy in own[1:] + passed:
        copy.wait_recv()
    vectors = jnp.sum(s_out[...].astype(f32), 0)
    inverse = lax.rsqrt(jnp.mean(resid * resid, -1, keepdims=True) + norm_eps)
    normed = (resid * inverse * vectors[1:2, :D]).astype(bf16)
    projected = jnp.dot(
        normed, w_out[...].reshape(D, QKV), preferred_element_type=f32
    ) + vectors[0:1]
    first = core == 0
    queries = jnp.where(first, projected[:, :QC], projected[:, QC : 2 * QC])
    keys = projected[:, H * HD : H * HD + KVH * HD]
    keys = jnp.where(first, keys, pltpu.roll(keys, HD, 1))
    values = projected[:, (H + KVH) * HD :]
    values = jnp.where(first, pltpu.roll(values, HD, 1), values)
    cosine, sine = turn[0], turn[1]
    keys = keys * cosine + swapped(keys) * sine
    wide_turn = [jnp.concatenate([t] * 4, 1)[:, :QC] for t in (cosine, sine)]
    padded = jnp.concatenate([queries, jnp.zeros((CHIP, HD), f32)], 1)
    queries = queries * wide_turn[0] + swapped(padded)[:, :QC] * wide_turn[1]
    q_out[...] = queries.astype(bf16).reshape(2, 128, QC)
    here[0:CHIP, :] = jnp.where(lanes((CHIP, 128)) < HD, keys, values).astype(bf16)

    parts = [(0, 48, 48), (96, 48, 48), (192, 48, 32)]
    for stage in range(3):
        jobs = []
        for (row, n0, n1), order in zip(parts, orders):
            axis, free = order[stage], order[:stage]

            def view(at, half, row=row, n0=n0, n1=n1, axis=axis, free=free):
                rows = {None: pl.ds(row, n0 + n1), 0: pl.ds(row, n0), 1: pl.ds(row + n0, n1)}
                return chips(all_ref, place, free, axis, at, rows[half])

            jobs.append((axis, view))
        phases(ring_spread(place, sems, jobs))
    sems.finish()


def opening(tokens, out_grad, weight, small, turn, mark, cid):
    return call(
        opening_kernel,
        (
            jax.ShapeDtypeStruct((2, 2, 2, 64, D), bf16),
            jax.ShapeDtypeStruct((4, 224, QKV), bf16),
            jax.ShapeDtypeStruct((4, 16, QKV), bf16),
            jax.ShapeDtypeStruct((2, 128, QC), bf16),
            jax.ShapeDtypeStruct((2, 4, 4, 2, KROWS, 128), bf16),
        ),
        [pltpu.SemaphoreType.DMA((5,))],
        50,
        cid,
        (tokens.reshape(2, 64, D), out_grad.reshape(2, 64, D), weight, small, turn, mark),
    )


def added(into, terms, shape):
    if not shape:
        into[...] = sum([t[...].astype(f32) for t in terms], into[...].astype(f32)).astype(bf16)
        return

    def one(i, carry):
        rest, index = i, []
        for size in reversed(shape):
            index.insert(0, rest % size)
            rest = rest // size
        index = tuple(index)
        into[index] = sum(
            [t[index].astype(f32) for t in terms], into[index].astype(f32)
        ).astype(bf16)
        return carry

    lax.fori_loop(0, math.prod(shape), one, 0)


def ring_sum(place, sems, jobs):
    plans = []
    for axis, view, land, shape in jobs:
        at = along(place, axis)
        after, far, before = (at + 1) % 4, (at + 2) % 4, (at + 3) % 4
        right, left = moved(place, axis, 1), moved(place, axis, -1)
        early = [
            sems.ready(view(far, 1), land[0], right),
            sems.ready(view(far, 0), land[1], left),
            sems.ready(view(after, 0), land[2], right),
            sems.ready(view(before, 1), land[3], left),
        ]
        sums = [view(after, 1), view(before, 0)]
        late = [sems.ready(sums[0], land[4], right), sems.ready(sums[1], land[5], left)]
        plans.append((early, sums, late, [view(at, 0), view(at, 1)], land, shape))

    def first():
        for early, *_ in plans:
            for copy in early[:2]:
                copy.start()
        for early, *_ in plans:
            for copy in early[2:]:
                copy.start()

    def middle():
        for early, sums, late, own, land, shape in plans:
            for i in range(2):
                early[i].wait_recv()
                added(sums[i], [land[i]], shape)
                late[i].start()

    def last():
        for early, sums, late, own, land, shape in plans:
            early[2].wait_recv()
            late[1].wait_recv()
            added(own[0], [land[2], land[5]], shape)
            early[3].wait_recv()
            late[0].wait_recv()
            added(own[1], [land[3], land[4]], shape)

    return first, middle, last


def ring_spread(place, sems, jobs):
    plans = []
    for axis, view in jobs:
        at = along(place, axis)
        after, before = (at + 1) % 4, (at + 3) % 4
        right, left = moved(place, axis, 1), moved(place, axis, -1)
        here, from_left, from_right = view(at, None), view(before, 0), view(after, 1)
        plans.append(
            (
                [sems.ready(here, here, right), sems.ready(here, here, left)],
                [sems.ready(from_left, from_left, right), sems.ready(from_right, from_right, left)],
            )
        )

    def first():
        for one, two in plans:
            for copy in one:
                copy.start()

    def middle():
        for one, two in plans:
            for i in range(2):
                one[i].wait_recv()
                two[i].start()

    def last():
        for one, two in plans:
            for copy in two:
                copy.wait_recv()

    return first, middle, last


def phases(made):
    for phase in made:
        phase()


sum_parts = [(0, 48, 48), (96, 48, 48), (192, 32, 32)]


def kv_shape(free):
    lead = ()
    if "x" in free:
        lead += (2,)
    if "z" in free:
        lead += (4,)
    if "y" in free:
        lead += (4,)
    if "x" in free:
        lead += (2,)
    return lead


def closing_kernel(part_ref, dq_ref, turn, out_ref, work, own, group, local_sem, *rest):
    lands, (send, recv) = rest[:-2], rest[-2:]
    place = my_place()
    x, y, z, core = place
    sibling, cross = pair_of(place)
    greet([sibling] + [moved(place, a, b) for a in "xyz" for b in (1, -1)])
    keep = pltpu.make_async_copy(part_ref, work, local_sem.at[0])
    keep.start()
    keep.wait()
    sems = Sems(send, recv)
    at_land = 0
    for stage in range(3):
        jobs = []
        for (row, n0, n1), order in zip(sum_parts, orders):
            axis, free = order[stage], order[stage + 1 :]

            def view(at, half, row=row, n0=n0, n1=n1, axis=axis, free=free):
                rows = pl.ds(row, n0) if half == 0 else pl.ds(row + n0, n1)
                return chips(work, place, free, axis, at, rows)

            jobs.append((axis, view, lands[at_land : at_land + 6], kv_shape(free)))
            at_land += 6
        phases(ring_sum(place, sems, jobs))
    grads = work[x % 2, z, y, x // 2].astype(f32)
    cosine, sine = turn[0], turn[1]
    keys = grads * cosine - swapped(grads) * sine
    dq = dq_ref[...].reshape(CHIP, QC)
    padded = jnp.concatenate([dq, jnp.zeros((CHIP, HD), f32)], 1)
    wide_turn = [jnp.concatenate([t] * 4, 1)[:, :QC] for t in (cosine, sine)]
    queries = dq * wide_turn[0] - swapped(padded)[:, :QC] * wide_turn[1]
    lane = lanes((CHIP, 128))
    both = jnp.where(lane < HD, keys, grads)
    own[...] = jnp.concatenate([queries, jnp.zeros((CHIP, HD), f32), both], 1).astype(bf16)
    pieces = [pl.ds(64 * i, 64) for i in range(4)]
    over = [sems.start(own.at[p], group.at[1, core, p], cross) for p in pieces]
    beside = sems.start(own, group.at[0, core], sibling)
    group[0, core] = own[...]
    passed = []
    for copy, p in zip(over, pieces):
        copy.wait_recv()
        passed.append(sems.start(group.at[1, core, p], group.at[1, core, p], sibling))

    def put(chip):
        low, high = group[chip, 0].astype(f32), group[chip, 1].astype(f32)
        low_kv, high_kv = low[:, 512:], high[:, 512:]
        out_ref[chip] = jnp.concatenate(
            [
                low[:, :QC],
                high[:, :QC],
                jnp.where(lane < HD, low_kv, pltpu.roll(high_kv, HD, 1)),
                jnp.where(lane < HD, pltpu.roll(low_kv, HD, 1), high_kv),
            ],
            1,
        ).astype(bf16)

    beside.wait_recv()
    put(0)
    for copy in passed:
        copy.wait_recv()
    put(1)
    sems.finish()


def closing(part, dq, turn, cid):
    lands = []
    for stage in range(3):
        for (row, n0, n1), order in zip(sum_parts, orders):
            lead = kv_shape(order[stage + 1 :])
            for n in (n1, n0, n0, n1, n1, n0):
                lands.append(pltpu.VMEM((*lead, n, 128), bf16))
    shape = (2, 4, 4, 2, CHIP, 128)
    return call(
        closing_kernel,
        jax.ShapeDtypeStruct((2, CHIP, QKV), bf16),
        [
            pltpu.VMEM(shape, bf16),
            pltpu.VMEM((CHIP, 640), bf16),
            pltpu.VMEM((2, 2, CHIP, 640), bf16),
            pltpu.SemaphoreType.DMA((1,)),
            *lands,
        ],
        63,
        cid,
        (part, dq, turn),
    )


big_rows, small_rows = 240, 48
big_parts = [
    ("zy", (0, 128, 0, D), (0, 64, 0, D), (64, 64, 0, D)),
    ("yz", (128, 112, 0, D), (128, 64, 0, D), (192, 48, 0, D)),
]
small_parts = [
    ("zy", (0, 48, 0, 512), (0, 48, 0, 256), (0, 48, 256, 256)),
    ("yz", (0, 48, 512, 384), (0, 48, 512, 256), (0, 48, 768, 128)),
]


def block_at(ref, lead, block):
    row, rows, column, columns = block
    return ref.at[(*lead, pl.ds(row, rows), pl.ds(column, columns))]


def weight_view(ref, place, order, stage, halves):
    _, y, z, _ = place
    every = slice(None)

    def view(at, half):
        if stage == 0:
            lead = (at, every) if order[0] == "z" else (every, at)
        else:
            lead = (z, at) if order[0] == "z" else (at, y)
        return block_at(ref, lead, halves[0 if half is None else half + 1])

    return view


def sum_lands(parts, stage):
    lead = (4,) if stage == 0 else ()
    return [
        pltpu.VMEM((*lead, halves[h + 1][1], halves[h + 1][3]), bf16)
        for _, *halves in parts
        for h in (1, 0, 0, 1, 1, 0)
    ]


def weight_ring_sum(place, sems, parts, work, stage, lands):
    return ring_sum(
        place,
        sems,
        [
            (
                order[stage],
                weight_view(work, place, order, stage, halves),
                lands[6 * i : 6 * i + 6],
                (4,) if stage == 0 else (),
            )
            for i, (order, *halves) in enumerate(parts)
        ],
    )


def weight_ring_spread(place, sems, parts, out, stage):
    return ring_spread(
        place,
        sems,
        [
            (order[stage], weight_view(out, place, order, stage, halves))
            for order, *halves in parts
        ],
    )


def mate_of(place):
    x, y, z, core = place
    return dev(x + 1 - 2 * (x % 2), y, z, core)


def final_kernel(big_ref, small_ref, big_out, small_out, work, swap, local_sem, *more):
    lands, (send, recv) = more[:-2], more[-2:]
    place = my_place()
    x, y, z, core = place
    loads = [
        pltpu.make_async_copy(small_ref, work, local_sem.at[0]),
        pltpu.make_async_copy(big_ref, big_out.at[z, y], local_sem.at[1]),
    ]
    for copy in loads:
        copy.start()
    greet([moved(place, a, b) for a in "yz" for b in (1, -1)] + [mate_of(place)])
    for copy in loads:
        copy.wait()
    sems = Sems(send, recv)
    sum0 = weight_ring_sum(place, sems, small_parts, work, 0, lands[:12])
    sum1 = weight_ring_sum(place, sems, small_parts, work, 1, lands[12:])
    pair = sems.ready(work.at[z, y], swap, mate_of(place))
    big1 = weight_ring_spread(place, sems, big_parts, big_out, 1)
    big0 = weight_ring_spread(place, sems, big_parts, big_out, 0)
    out1 = weight_ring_spread(place, sems, small_parts, small_out, 1)
    out0 = weight_ring_spread(place, sems, small_parts, small_out, 0)
    sum0[0]()
    big1[0]()
    sum0[1]()
    big1[1]()
    sum0[2]()
    sum1[0]()
    big1[2]()
    big0[0]()
    sum1[1]()
    sum1[2]()
    pair.start()
    pair.wait_recv()
    small_out[z, y] = (work[z, y].astype(f32) + swap[...].astype(f32)).astype(bf16)
    out1[0]()
    out1[1]()
    out1[2]()
    out0[0]()
    big0[1]()
    out0[1]()
    out0[2]()
    big0[2]()
    sems.finish()


def final(big, small, cid):
    shapes = [(4, 4, n, D) for n in (big_rows, small_rows)]
    return call(
        final_kernel,
        tuple(jax.ShapeDtypeStruct(s, bf16) for s in shapes),
        [
            pltpu.VMEM(shapes[1], bf16),
            pltpu.VMEM((small_rows, D), bf16),
            pltpu.SemaphoreType.DMA((2,)),
            *sum_lands(small_parts, 0),
            *sum_lands(small_parts, 1),
        ],
        24 + 1 + 32,
        cid,
        (big, small.reshape(shapes[1])),
        [pl.BlockSpec(memory_space=pltpu.VMEM), pl.BlockSpec(memory_space=pl.ANY)],
    )


NT = (((1,), (1,)), ((), ()))
ROWS = G * 128


def lanes(shape):
    return lax.broadcasted_iota(jnp.int32, shape, len(shape) - 1)


def split3(value):
    one = value.astype(bf16).astype(f32)
    two = (value - one).astype(bf16).astype(f32)
    three = (value - one - two).astype(bf16).astype(f32)
    return one, two, three


def keys_of(kv_ref, c, half):
    start = half * 128 if isinstance(half, int) else pl.multiple_of(half * 128, 128)
    tile = kv_ref[c, :, pl.ds(start, 128), :].reshape(256, 128)
    lane = lanes((256, 128))
    ones = jnp.ones((256, 128), bf16)
    return jnp.where(lane < HD, tile, ones), jnp.where(lane < HD, ones, tile)


def both_keys(kv_ref, c0, c1):
    pairs = zip(keys_of(kv_ref, c0, 0), keys_of(kv_ref, c1, 0))
    return [jnp.concatenate(pair, 0) for pair in pairs]


def hidden_keys(xhi):
    row = lax.broadcasted_iota(jnp.int32, (ROWS, 256), 0) % 128
    key = lax.broadcasted_iota(jnp.int32, (ROWS, 256), 1)
    return key > row + xhi * 128


def forward_kernel(scal, q_ref, kv_ref, o_ref, qe_ref, peak, acc):
    me, xhi = scal[32], scal[33]
    for h in range(2):
        for g in range(G):
            piece = q_ref[h, :, g * HD : (g + 1) * HD].astype(f32) * (1.0 / math.sqrt(HD))
            wide_piece = jnp.concatenate([piece, jnp.zeros((128, HD), f32)], 1)
            qe_ref[h, g * 128 : (g + 1) * 128, :] = wide_piece.astype(bf16)
    peak[...] = jnp.full((2, ROWS, 128), -1e30, f32)
    acc[...] = jnp.zeros((2, ROWS, 128), f32)

    def fold(half, kk, vv, hide=None):
        s = lax.dot_general(qe_ref[half], kk, NT, preferred_element_type=f32)
        if hide is not None:
            s = jnp.where(hide, -1e30, s)
        tiles = [s[:, e : e + 128] for e in range(0, s.shape[1], 128)]
        old = peak[half]
        top = jnp.maximum(
            old, jnp.max(functools.reduce(jnp.maximum, tiles), 1, keepdims=True)
        )
        peak[half] = top
        p = jnp.concatenate([jnp.exp(t - top) for t in tiles], 1).astype(bf16)
        acc[half] = acc[half] * jnp.exp(old - top) + jnp.dot(p, vv, preferred_element_type=f32)

    def early_pair(c0, c1):
        fold(1, *both_keys(kv_ref, c0, c1))

    def other(c):
        sel = scal[c]
        fold(sel, *keys_of(kv_ref, c, sel))

    def one(i, carry):
        c0, c1 = (me + 2 * i + 1) % 32, (me + 2 * i + 2) % 32
        early_pair(c0, c1)
        other(c0)
        other(c1)
        return carry

    lax.fori_loop(0, 15, one, 0)
    early_pair((me + 31) % 32, me)
    other((me + 31) % 32)
    fold(0, *keys_of(kv_ref, me, 0), hidden_keys(xhi))
    fold(1, *keys_of(kv_ref, me, 1), hidden_keys(xhi))
    lane = lanes((ROWS, 128))
    for h in range(2):
        total = acc[h][:, :1]
        held = qe_ref[h].astype(f32)
        for i, part in enumerate(split3(-(peak[h][:, :1] + jnp.log(total)))):
            held = jnp.where(lane == HD + i, part, held)
        qe_ref[h] = held.astype(bf16)
        out = acc[h] / total
        for g in range(G):
            o_ref[h, :, g * HD : (g + 1) * HD] = out[g * 128 : (g + 1) * 128, HD:]


def local_call(kernel, out_shape, scratch, args, flops):
    vmem = pl.BlockSpec(memory_space=pltpu.VMEM)
    return pl.pallas_call(
        kernel,
        out_shape=out_shape,
        in_specs=[pl.BlockSpec(memory_space=pltpu.SMEM)] + [vmem] * (len(args) - 1),
        out_specs=jax.tree.map(lambda _: vmem, out_shape),
        scratch_shapes=scratch,
        compiler_params=pltpu.CompilerParams(vmem_limit_bytes=VLIM),
        cost_estimate=pl.CostEstimate(
            flops=flops, bytes_accessed=10_000_000, transcendentals=15_000_000
        ),
    )(*args)


def attention_forward(scal, q, kv):
    return local_call(
        forward_kernel,
        (
            jax.ShapeDtypeStruct((2, 128, QC), f32),
            jax.ShapeDtypeStruct((2, ROWS, 128), bf16),
        ),
        [pltpu.VMEM((2, ROWS, 128), f32), pltpu.VMEM((2, ROWS, 128), f32)],
        (scal, q, kv),
        20_000_000_000,
    )


def backward_kernel(
    scal, qe_ref, o_ref, g_ref, kv_ref, part_ref,
    dq_ref, dkv_ref, sum_ref,
    ge, qt, gt, dq, work, swap, local_sem, *more,
):
    lands, (send, recv) = more[:-2], more[-2:]
    place = my_place()
    x, y, z, core = place
    me, xhi = lax.axis_index("ctx"), x // 2
    load = pltpu.make_async_copy(part_ref, work, local_sem.at[0])
    load.start()
    greet([moved(place, a, b) for a in "yz" for b in (1, -1)] + [mate_of(place)])
    load.wait()
    sems = Sems(send, recv)
    sum0 = weight_ring_sum(place, sems, big_parts, work, 0, lands[:12])
    sum1 = weight_ring_sum(place, sems, big_parts, work, 1, lands[12:])
    pair = sems.ready(work.at[z, y], swap, mate_of(place))
    sum0[0]()

    lane = lanes((128, 128))
    for h in range(2):
        for g in range(G):
            cols = slice(g * HD, (g + 1) * HD)
            piece = g_ref[h, :, cols].astype(f32)
            delta = jnp.sum(piece * o_ref[h, :, cols], 1, keepdims=True)
            held = jnp.concatenate([jnp.zeros((128, HD), f32), piece], 1)
            for i, value in enumerate(split3(-delta)):
                held = jnp.where(lane == i, value, held)
            rows = slice(g * 128, (g + 1) * 128)
            ge[h, rows, :] = held.astype(bf16)
            gt[h, :, rows] = held.T.astype(bf16)
            qt[h, :, rows] = qe_ref[h, rows, :].astype(f32).T.astype(bf16)
    dq[...] = jnp.zeros((2, ROWS, 128), f32)

    def picked(sel, early, late):
        return jnp.where(jnp.full(early.shape, sel, jnp.int32) > 0, late, early)

    def tile(half, kk, vv, hide=None, late=None):
        def rows_of(ref):
            return ref[half] if late is None else picked(half, ref[0], ref[1])

        s = lax.dot_general(rows_of(qe_ref), kk, NT, preferred_element_type=f32)
        if hide is not None:
            s = jnp.where(hide, -1e30, s)
        p = jnp.exp(s)
        dp = lax.dot_general(rows_of(ge), vv, NT, preferred_element_type=f32)
        ds = (p * dp).astype(bf16)
        step = jnp.dot(ds, kk, preferred_element_type=f32)
        if late is None:
            dq[half] += step
        else:
            dq[1] += step * late
            dq[0] += step * (1.0 - late)
        dk = jnp.dot(rows_of(qt), ds, preferred_element_type=f32)
        dv = jnp.dot(rows_of(gt), p.astype(bf16), preferred_element_type=f32)
        return jnp.concatenate([dk[:HD], dv[HD:]], 0).T

    def put(c, half, value):
        dkv_ref[c, :, half * 128 : (half + 1) * 128, :] = value.astype(bf16).reshape(2, 128, 128)

    def other(c, early):
        sel = scal[c]
        late = sel.astype(f32)
        pairs = zip(keys_of(kv_ref, c, 0), keys_of(kv_ref, c, 1))
        step = tile(sel, *[picked(sel, *pair) for pair in pairs], late=late)
        put(c, 0, early + step * (1.0 - late))
        put(c, 1, step * late)

    beside = {3: [sum0[1]], 10: [sum0[2], sum1[0]], 12: [sum1[1]], 14: [sum1[2], pair.start]}

    def one(i, carry):
        for at, steps in beside.items():

            @pl.when(i == at)
            def _(steps=steps):
                for step in steps:
                    step()

        c0, c1 = (me + 2 * i + 1) % 32, (me + 2 * i + 2) % 32
        early = tile(1, *both_keys(kv_ref, c0, c1))
        other(c0, early[:256])
        other(c1, early[256:])
        return carry

    lax.fori_loop(0, 15, one, 0)
    final_c = (me + 31) % 32
    early = tile(1, *both_keys(kv_ref, final_c, me))
    other(final_c, early[:256])
    put(me, 0, early[256:] + tile(0, *keys_of(kv_ref, me, 0), hidden_keys(xhi)))
    put(me, 1, tile(1, *keys_of(kv_ref, me, 1), hidden_keys(xhi)))
    for h in range(2):
        for g in range(G):
            dq_ref[h, :, g * HD : (g + 1) * HD] = dq[h, g * 128 : (g + 1) * 128, :HD] * (
                1.0 / math.sqrt(HD)
            )
    pair.wait_recv()
    sum_ref[...] = (work[z, y].astype(f32) + swap[...].astype(f32)).astype(bf16)
    sems.finish()


def attention_backward(scal, qe, o, grad, kv, part, cid):
    big = (4, 4, big_rows, D)
    vmem = pl.BlockSpec(memory_space=pltpu.VMEM)
    return call(
        backward_kernel,
        (
            jax.ShapeDtypeStruct((2, 128, QC), f32),
            jax.ShapeDtypeStruct((32, 2, CHIP, 128), bf16),
            jax.ShapeDtypeStruct((big_rows, D), bf16),
        ),
        [
            pltpu.VMEM((2, ROWS, 128), bf16),
            pltpu.VMEM((2, 128, ROWS), bf16),
            pltpu.VMEM((2, 128, ROWS), bf16),
            pltpu.VMEM((2, ROWS, 128), f32),
            pltpu.VMEM(big, bf16),
            pltpu.VMEM((big_rows, D), bf16),
            pltpu.SemaphoreType.DMA((1,)),
            *sum_lands(big_parts, 0),
            *sum_lands(big_parts, 1),
        ],
        25,
        cid,
        (scal, qe, o, grad, kv, part.reshape(big)),
        [pl.BlockSpec(memory_space=pltpu.SMEM), *[vmem] * 4, pl.BlockSpec(memory_space=pl.ANY)],
    )


def rms_inverse(values):
    return lax.rsqrt(jnp.mean(values * values, -1, keepdims=True) + norm_eps)


def rms_pull(values, inverse, gain, grad):
    scaled = values * inverse
    e = grad * gain
    return inverse * (e - scaled * jnp.mean(e * scaled, -1, keepdims=True))


def rotation(positions):
    lane = jnp.arange(128)
    frequency = rope_base ** (-(2.0 * (lane % 32).astype(f32)) / HD)
    angles = positions.astype(f32)[:, None] * frequency[None, :]
    sign = jnp.where(lane % HD < HD // 2, -1.0, 1.0)
    return jnp.stack([jnp.cos(angles), jnp.sin(angles) * sign])


def dot(a, b):
    return jnp.dot(a, b, preferred_element_type=f32)


def body(
    tokens,
    out_grad,
    norm1_gain,
    qkv_weight,
    qkv_bias,
    out_weight,
    norm2_gain,
    gate_weight,
    up_weight,
    down_weight,
    positions,
):
    ctx = lax.axis_index("ctx")
    wsh = lax.axis_index("wsh")
    xhi, core = wsh // 2, wsh % 2
    my_block = positions[0] // 256

    def cut(array, start, size, axis):
        return lax.dynamic_slice_in_dim(array, start, size, axis)

    def own_rows(array):
        return cut(array.reshape(2, 2, 64, -1), core, 1, 1).reshape(TOK, -1)

    swap = [
        (c * 4 + w, ((c + 16) % 32) * 4 + (w + 2) % 4) for c in range(32) for w in range(4)
    ]
    twin = [(c * 4 + w, c * 4 + w + 1 - 2 * (w % 2)) for c in range(32) for w in range(4)]

    def crossed(array):
        return lax.ppermute(array, ("ctx", "wsh"), swap)

    def spread(vector, width):
        column = jnp.arange(QKV)
        values = jnp.pad(jnp.tile(vector, 4), (0, QKV - 4 * width))
        return jnp.where(column // width == wsh, values, 0)

    small = jnp.stack([spread(qkv_bias, 288), spread(norm1_gain, 224), spread(norm2_gain, 224)])
    small = jnp.pad(small, ((0, 13), (0, 0))).astype(bf16)
    offset = jnp.arange(128, dtype=jnp.int32) + xhi * 128
    turn = rotation(jnp.concatenate([my_block * 256 + offset, (63 - my_block) * 256 + offset]))
    mark = jnp.broadcast_to(my_block.astype(bf16), (KROWS - CHIP, 128))
    t_all, w_all, s_all, queries, kv_all = opening(
        tokens, out_grad, qkv_weight, small, turn, mark, 0
    )
    out_weight, kv_all = lax.optimization_barrier((out_weight, kv_all))
    out_full = lax.all_gather(out_weight, "wsh", axis=0, tiled=True)
    qkv_full = w_all.reshape(D, QKV)
    vectors = jnp.sum(s_all[:, 1:3, :D].astype(f32), 0)
    gain_one, gain_two = vectors[0], vectors[1]
    t_chip = t_all.reshape(2, CHIP, D)
    kv_all = kv_all.reshape(32, 2, KROWS, 128)
    blocks = kv_all[:, 0, CHIP, 0].astype(jnp.int32)
    scal = jnp.concatenate(
        [(blocks > my_block).astype(jnp.int32), jnp.stack([ctx, xhi]).astype(jnp.int32)]
    )
    t_chip, kv_all = lax.optimization_barrier((t_chip, kv_all))
    t_other = crossed(t_chip)
    attended_f, qe = attention_forward(scal, queries, kv_all)
    att = group_gather(attended_f.astype(bf16).reshape(CHIP, QC), 2)
    t_both = jnp.stack([t_chip, t_other], 1).reshape(2, 2 * CHIP, D)
    resid_both = t_both[0].astype(f32)
    cot = t_both[1]
    att_cols = [att[:, i].reshape(2 * CHIP, QC) for i in range(2)]
    stream = resid_both + dot(att_cols[0], out_full[:QC]) + dot(att_cols[1], out_full[QC:])
    inv_two = rms_inverse(stream)
    normed_two = (stream * inv_two * gain_two).astype(bf16)
    gate_pre = dot(normed_two, gate_weight)
    up_pre = dot(normed_two, up_weight)
    hidden_grad = jnp.einsum("td,fd->tf", cot, down_weight, preferred_element_type=f32)
    sigma = jax.nn.sigmoid(gate_pre)
    activated = gate_pre * sigma
    hidden = (activated * up_pre).astype(bf16)
    gate_grad = (hidden_grad * up_pre * sigma * (1.0 + gate_pre * (1.0 - sigma))).astype(bf16)
    up_grad = (hidden_grad * activated).astype(bf16)
    norm_part = jnp.einsum(
        "tf,df->td", gate_grad, gate_weight, preferred_element_type=f32
    ) + jnp.einsum("tf,df->td", up_grad, up_weight, preferred_element_type=f32)
    norm_grad = group_sum(norm_part.astype(bf16).reshape(2, 2, 2, 64, D), 3).reshape(CHIP, D)

    mlp_part = dot(hidden, down_weight).astype(bf16).reshape(2, 2, 2, 64, D)
    norm_other = crossed(norm_grad)
    mlp_got = lax.ppermute(cut(mlp_part, 1 - core, 1, 2), ("ctx", "wsh"), twin)
    mlp_sum = cut(mlp_part, core, 1, 2).astype(f32) + mlp_got.astype(f32)
    mlp_far = crossed(mlp_sum[1].astype(bf16))
    gate_wgrad = jnp.einsum("tf,td->fd", gate_grad, normed_two, preferred_element_type=f32)
    up_wgrad = jnp.einsum("tf,td->fd", up_grad, normed_two, preferred_element_type=f32)
    down_wgrad = jnp.einsum("tf,td->fd", hidden, cot, preferred_element_type=f32)

    def stream_pull(part, grad):
        rows = slice(part * CHIP, (part + 1) * CHIP)
        return cot[rows].astype(f32) + rms_pull(
            stream[rows], inv_two[rows], gain_two, grad.astype(f32)
        )

    stream_grad = stream_pull(0, norm_grad)
    branch_grad = stream_grad.astype(bf16)
    att_grad = jnp.einsum(
        "td,id->ti", branch_grad, cut(out_full, core * QC, QC, 0), preferred_element_type=f32
    ).astype(bf16)
    large = jnp.concatenate(
        [
            *[w.astype(bf16) for w in (gate_wgrad, up_wgrad, down_wgrad)],
            jnp.zeros((16 * big_rows - 3 * FS, D), bf16),
        ],
        0,
    )
    dq, dkv_part, large_own = attention_backward(
        scal, qe, attended_f, att_grad.reshape(2, 128, QC), kv_all, large, 5
    )
    norm_other, mlp_far, dq = lax.optimization_barrier((norm_other, mlp_far, dq))
    pg = closing(dkv_part.reshape(2, 4, 4, 2, CHIP, 128), dq, turn, 4).reshape(2 * CHIP, QKV)

    mlp_own = (mlp_sum[0] + mlp_far.astype(f32)).reshape(TOK, D)
    output = (own_rows(stream[:CHIP]) + mlp_own).astype(bf16)

    bias_grad = cut(jnp.sum(pg.astype(f32), 0), wsh * 288, 288, 0)
    inv_one = rms_inverse(resid_both)
    scaled_one = cut(resid_both, wsh * 224, 224, 1) * inv_one
    normed_cols = (scaled_one * norm1_gain.astype(f32)).astype(bf16)
    qkv_wgrad = jnp.einsum("td,tf->df", normed_cols, pg, preferred_element_type=f32)
    one_cols = jnp.einsum("tf,df->td", pg, qkv_weight, preferred_element_type=f32)
    gain_one_grad = jnp.sum(one_cols * scaled_one, 0)
    branch_both = jnp.concatenate(
        [branch_grad, stream_pull(1, norm_other).astype(bf16)], 0
    )
    norm_both = jnp.concatenate([norm_grad, norm_other], 0)
    scaled_two = cut(stream, wsh * 224, 224, 1) * inv_two
    gain_two_grad = jnp.sum(cut(norm_both, wsh * 224, 224, 1).astype(f32) * scaled_two, 0)
    att_mine = cut(jnp.where(wsh < 2, att_cols[0], att_cols[1]), (wsh % 2) * 224, 224, 1)
    out_wgrad = jnp.einsum("ti,td->id", att_mine, branch_both, preferred_element_type=f32)
    pg_own = own_rows(pg[:CHIP])
    one_grad = jnp.einsum("tf,df->td", pg_own, qkv_full, preferred_element_type=f32)
    resid_own = tokens.astype(f32)
    token_grad = own_rows(stream_grad) + rms_pull(
        resid_own, rms_inverse(resid_own), gain_one, one_grad
    )
    vectors = jnp.stack(
        [jnp.pad(v, (0, D - v.shape[0])) for v in (bias_grad, gain_one_grad, gain_two_grad)]
    )
    small = jnp.concatenate(
        [
            out_wgrad.astype(bf16),
            qkv_wgrad.astype(bf16).reshape(288, D),
            jnp.pad(vectors, ((0, 16 * small_rows - 515), (0, 0))).astype(bf16),
        ],
        0,
    )
    large, small = final(large_own, small, 6)
    large, small = large.reshape(16 * big_rows, D), small.reshape(16 * small_rows, D)
    return (
        output,
        token_grad,
        small[513, :224].astype(f32),
        small[224:512].reshape(224, QKV).astype(f32),
        small[512, :288].astype(f32),
        small[:224].astype(f32),
        small[514, :224].astype(f32),
        large[:FS].astype(f32).T,
        large[FS : 2 * FS].astype(f32).T,
        large[2 * FS : 3 * FS].astype(f32),
    )


def solution(mesh):
    rows = P(("ctx", "wsh"), None)
    return jax.shard_map(
        body,
        mesh=mesh,
        in_specs=(
            rows,
            rows,
            P("wsh"),
            P("wsh", None),
            P("wsh"),
            P("wsh", None),
            P("wsh"),
            P(None, "wsh"),
            P(None, "wsh"),
            P("wsh", None),
            P(("ctx", "wsh")),
        ),
        out_specs=(
            rows,
            rows,
            P("wsh"),
            P("wsh", None),
            P("wsh"),
            P("wsh", None),
            P("wsh"),
            P(None, "wsh"),
            P(None, "wsh"),
            P("wsh", None),
        ),
        check_vma=False,
    )
```

```python
import functools
import math

import jax
import jax.numpy as jnp
from jax import lax
from jax.experimental import pallas as pl
from jax.experimental.pallas import tpu as pltpu
from jax.sharding import PartitionSpec as P

H = 14
KVH = 2
HD = 64
G = H // KVH
D = 896
FS = 1216
QKV = 1152
QC = G * HD
PC = QC + 2 * HD
TOK = 128
CHIP = 256
KROWS = 272

MESH = pl.DeviceIdType.MESH
VLIM = 56 * 1024 * 1024
norm_eps = 1e-06
rope_base = 1000000.0
f32 = jnp.float32
bf16 = jnp.bfloat16


def my_place():
    c = lax.axis_index("ctx")
    w = lax.axis_index("wsh")
    return (w // 2) * 2 + c // 16, c % 4, (c // 4) % 4, w % 2


def dev(x, y, z, core):
    return ((x % 2) * 16 + z * 4 + y, (x // 2) * 2 + core)


def moved(place, axis, by):
    x, y, z, core = place
    if axis == "x":
        return dev((x + by + 4) % 4, y, z, core)
    if axis == "y":
        return dev(x, (y + by + 4) % 4, z, core)
    return dev(x, y, (z + by + 4) % 4, core)


def along(place, axis):
    return place["xyz".index(axis)]


def others(place, axes):
    return [moved(place, a, k) for a in axes for k in (1, 2, 3)]


def greet(devices):
    barrier = pltpu.get_barrier_semaphore()
    for device in devices:
        pl.semaphore_signal(barrier, inc=1, device_id=device, device_id_type=MESH)
    pl.semaphore_wait(barrier, len(devices))


class Sems:
    def __init__(self, send, recv):
        self.send, self.recv, self.at = send, recv, 0
        self.started = []

    def copy(self, src, dst, device):
        i = self.at
        self.at += 1
        return pltpu.make_async_remote_copy(
            src_ref=src,
            dst_ref=dst,
            send_sem=self.send.at[i],
            recv_sem=self.recv.at[i],
            device_id=device,
            device_id_type=MESH,
        )

    def ready(self, src, dst, device):
        copy = self.copy(src, dst, device)
        self.started.append(copy)
        return copy

    def start(self, src, dst, device):
        copy = self.ready(src, dst, device)
        copy.start()
        return copy

    def finish(self):
        for copy in self.started:
            copy.wait_send()


def call(kernel, out_shape, scratch, n_sems, cid, args, specs=None):
    vmem = pl.BlockSpec(memory_space=pltpu.VMEM)
    outs = jax.tree.map(lambda _: vmem, out_shape)
    return pl.pallas_call(
        kernel,
        out_shape=out_shape,
        in_specs=specs if specs is not None else [vmem] * len(args),
        out_specs=outs,
        scratch_shapes=[
            *scratch,
            pltpu.SemaphoreType.DMA((n_sems,)),
            pltpu.SemaphoreType.DMA((n_sems,)),
        ],
        compiler_params=pltpu.CompilerParams(
            collective_id=cid, has_side_effects=True, vmem_limit_bytes=VLIM
        ),
    )(*args)


def pair_of(place):
    x, y, z, core = place
    return dev(x, y, z, 1 - core), dev(3 - x, y, z, core)


def group_kernel(a_ref, out_ref, local_sem, send, recv):
    place = my_place()
    core = place[3]
    sibling, cross = pair_of(place)
    greet([sibling, cross])
    sems = Sems(send, recv)
    pieces = [pl.ds(64 * i, 64) for i in range(4)]
    over = [sems.start(a_ref.at[p], out_ref.at[1, core, p], cross) for p in pieces]
    own = sems.start(a_ref, out_ref.at[0, core], sibling)
    keep = pltpu.make_async_copy(a_ref, out_ref.at[0, core], local_sem.at[0])
    keep.start()
    passed = []
    for copy, p in zip(over, pieces):
        copy.wait_recv()
        passed.append(sems.start(out_ref.at[1, core, p], out_ref.at[1, core, p], sibling))
    for copy in [own, *passed]:
        copy.wait_recv()
    keep.wait()
    sems.finish()


def group_gather(array, cid):
    return call(
        group_kernel,
        jax.ShapeDtypeStruct((2, 2, *array.shape), array.dtype),
        [pltpu.SemaphoreType.DMA((1,))],
        9,
        cid,
        (array,),
    )


def group_sum_kernel(p_ref, out_ref, got, total, far, send, recv):
    place = my_place()
    core = place[3]
    sibling, cross = pair_of(place)
    greet([sibling, cross])
    sems = Sems(send, recv)
    in_other = [sems.start(p_ref.at[1, h, 1 - core], got.at[1, h], sibling) for h in range(2)]
    in_own = [sems.start(p_ref.at[0, h, 1 - core], got.at[0, h], sibling) for h in range(2)]
    over = []
    for h in range(2):
        in_other[h].wait_recv()
        total[1, h] = (p_ref[1, h, core].astype(f32) + got[1, h].astype(f32)).astype(bf16)
        over.append(sems.start(total.at[1, h], far.at[h], cross))
    last = []
    for h in range(2):
        in_own[h].wait_recv()
        over[h].wait_recv()
        out_ref[h, core] = (
            p_ref[0, h, core].astype(f32) + got[0, h].astype(f32) + far[h].astype(f32)
        ).astype(bf16)
        last.append(sems.start(out_ref.at[h, core], out_ref.at[h, core], sibling))
    for copy in last:
        copy.wait_recv()
    sems.finish()


def group_sum(part, cid):
    rows = (2, 64, D)
    return call(
        group_sum_kernel,
        jax.ShapeDtypeStruct((2, 2, 64, D), bf16),
        [pltpu.VMEM((2, *rows), bf16), pltpu.VMEM((2, *rows), bf16), pltpu.VMEM(rows, bf16)],
        8,
        cid,
        (part,),
    )


orders = (("z", "y", "x"), ("y", "x", "z"), ("x", "z", "y"))


def chips(ref, place, free, axis, at, rows):
    x, y, z, _ = place
    index = {"x": x, "y": y, "z": z}
    index[axis] = at
    every = slice(None)
    xlo, xhi = (every, every) if "x" in free else (index["x"] % 2, index["x"] // 2)
    return ref.at[
        xlo, every if "z" in free else index["z"], every if "y" in free else index["y"], xhi, rows
    ]


def swapped(values):
    width = values.shape[1]
    first = lanes(values.shape) % HD < HD // 2
    return jnp.where(first, pltpu.roll(values, width - 32, 1), pltpu.roll(values, 32, 1))


def opening_kernel(
    tok, cot, w_ref, small, turn, mark, t_out, w_out, s_out, q_out, all_ref, local_sem, send, recv
):
    place = my_place()
    x, y, z, core = place
    sibling, cross = pair_of(place)
    mate = dev(x + 1 - 2 * (x % 2), y, z, core)
    greet([sibling] + others(place, "xyz"))
    sems = Sems(send, recv)
    mine = (x // 2) * 2 + core
    theirs = (1 - x // 2) * 2 + core
    cut = ((0, 48), (48, 64))
    got, sent = (x % 2) * 112, (1 - x % 2) * 112

    def rows(start, at, size):
        return pl.ds(pl.multiple_of(start + at, 16), size)

    mark_rows = pl.ds(CHIP, KROWS - CHIP)
    here = all_ref.at[x % 2, z, y, x // 2]
    own = [sems.start(ref, t_out.at[i, :, core], sibling) for i, ref in enumerate((tok, cot))]
    over = [
        sems.start(w_ref.at[rows(sent, at, n)], w_out.at[mine, rows(sent, at, n)], cross)
        for at, n in cut
    ]
    over_small = sems.start(small, s_out.at[mine], cross)
    own += [sems.start(w_ref, w_out.at[mine], sibling), sems.start(small, s_out.at[mine], sibling)]
    keep = [
        pltpu.make_async_copy(tok, t_out.at[0, :, core], local_sem.at[0]),
        pltpu.make_async_copy(cot, t_out.at[1, :, core], local_sem.at[1]),
        pltpu.make_async_copy(w_ref, w_out.at[mine], local_sem.at[2]),
        pltpu.make_async_copy(small, s_out.at[mine], local_sem.at[3]),
        pltpu.make_async_copy(mark, here.at[mark_rows], local_sem.at[4]),
    ]
    for copy in keep:
        copy.start()
    shared, passed = [], []
    for copy, (at, n) in zip(over, cut):
        copy.wait_recv()
        piece = w_out.at[theirs, rows(got, at, n)]
        shared.append(sems.start(piece, piece, mate))
        passed.append(sems.start(piece, piece, sibling))
    over_small.wait_recv()
    passed.append(sems.start(s_out.at[theirs], s_out.at[theirs], sibling))
    for copy in keep:
        copy.wait()
    own[0].wait_recv()
    resid = t_out[0].reshape(CHIP, D).astype(f32)
    for copy, (at, n) in zip(shared, cut):
        copy.wait_recv()
        piece = w_out.at[theirs, rows(sent, at, n)]
        passed.append(sems.start(piece, piece, sibling))
    for copy in own[1:] + passed:
        copy.wait_recv()
    vectors = jnp.sum(s_out[...].astype(f32), 0)
    inverse = lax.rsqrt(jnp.mean(resid * resid, -1, keepdims=True) + norm_eps)
    normed = (resid * inverse * vectors[1:2, :D]).astype(bf16)
    projected = jnp.dot(
        normed, w_out[...].reshape(D, QKV), preferred_element_type=f32
    ) + vectors[0:1]
    first = core == 0
    queries = jnp.where(first, projected[:, :QC], projected[:, QC : 2 * QC])
    keys = projected[:, H * HD : H * HD + KVH * HD]
    keys = jnp.where(first, keys, pltpu.roll(keys, HD, 1))
    values = projected[:, (H + KVH) * HD :]
    values = jnp.where(first, pltpu.roll(values, HD, 1), values)
    cosine, sine = turn[0], turn[1]
    keys = keys * cosine + swapped(keys) * sine
    wide_turn = [jnp.concatenate([t] * 4, 1)[:, :QC] for t in (cosine, sine)]
    padded = jnp.concatenate([queries, jnp.zeros((CHIP, HD), f32)], 1)
    queries = queries * wide_turn[0] + swapped(padded)[:, :QC] * wide_turn[1]
    q_out[...] = queries.astype(bf16).reshape(2, 128, QC)
    here[0:CHIP, :] = jnp.where(lanes((CHIP, 128)) < HD, keys, values).astype(bf16)

    parts = [(0, 48, 48), (96, 48, 48), (192, 48, 32)]
    for stage in range(3):
        jobs = []
        for (row, n0, n1), order in zip(parts, orders):
            axis, free = order[stage], order[:stage]

            def view(at, half, row=row, n0=n0, n1=n1, axis=axis, free=free):
                rows = {None: pl.ds(row, n0 + n1), 0: pl.ds(row, n0), 1: pl.ds(row + n0, n1)}
                return chips(all_ref, place, free, axis, at, rows[half])

            jobs.append((axis, view))
        phases((ring_spread if stage == 2 else direct_spread)(place, sems, jobs))
    sems.finish()


def opening(tokens, out_grad, weight, small, turn, mark, cid):
    return call(
        opening_kernel,
        (
            jax.ShapeDtypeStruct((2, 2, 2, 64, D), bf16),
            jax.ShapeDtypeStruct((4, 224, QKV), bf16),
            jax.ShapeDtypeStruct((4, 16, QKV), bf16),
            jax.ShapeDtypeStruct((2, 128, QC), bf16),
            jax.ShapeDtypeStruct((2, 4, 4, 2, KROWS, 128), bf16),
        ),
        [pltpu.SemaphoreType.DMA((5,))],
        50,
        cid,
        (tokens.reshape(2, 64, D), out_grad.reshape(2, 64, D), weight, small, turn, mark),
    )


def added(into, terms, shape):
    if not shape:
        into[...] = sum([t[...].astype(f32) for t in terms], into[...].astype(f32)).astype(bf16)
        return

    def one(i, carry):
        rest, index = i, []
        for size in reversed(shape):
            index.insert(0, rest % size)
            rest = rest // size
        index = tuple(index)
        into[index] = sum(
            [t[index].astype(f32) for t in terms], into[index].astype(f32)
        ).astype(bf16)
        return carry

    lax.fori_loop(0, math.prod(shape), one, 0)


def ring_sum(place, sems, jobs):
    plans = []
    for axis, view, land, shape in jobs:
        at = along(place, axis)
        after, far, before = (at + 1) % 4, (at + 2) % 4, (at + 3) % 4
        right, left = moved(place, axis, 1), moved(place, axis, -1)
        early = [
            sems.ready(view(far, 1), land[0], right),
            sems.ready(view(far, 0), land[1], left),
            sems.ready(view(after, 0), land[2], right),
            sems.ready(view(before, 1), land[3], left),
        ]
        sums = [view(after, 1), view(before, 0)]
        late = [sems.ready(sums[0], land[4], right), sems.ready(sums[1], land[5], left)]
        plans.append((early, sums, late, [view(at, 0), view(at, 1)], land, shape))

    def first():
        for early, *_ in plans:
            for copy in early[:2]:
                copy.start()
        for early, *_ in plans:
            for copy in early[2:]:
                copy.start()

    def middle():
        for early, sums, late, own, land, shape in plans:
            for i in range(2):
                early[i].wait_recv()
                added(sums[i], [land[i]], shape)
                late[i].start()

    def last():
        for early, sums, late, own, land, shape in plans:
            early[2].wait_recv()
            late[1].wait_recv()
            added(own[0], [land[2], land[5]], shape)
            early[3].wait_recv()
            late[0].wait_recv()
            added(own[1], [land[3], land[4]], shape)

    return first, middle, last


def ring_spread(place, sems, jobs):
    plans = []
    for axis, view in jobs:
        at = along(place, axis)
        after, before = (at + 1) % 4, (at + 3) % 4
        right, left = moved(place, axis, 1), moved(place, axis, -1)
        here, from_left, from_right = view(at, None), view(before, 0), view(after, 1)
        plans.append(
            (
                [sems.ready(here, here, right), sems.ready(here, here, left)],
                [sems.ready(from_left, from_left, right), sems.ready(from_right, from_right, left)],
            )
        )

    def first():
        for one, two in plans:
            for copy in one:
                copy.start()

    def middle():
        for one, two in plans:
            for i in range(2):
                one[i].wait_recv()
                two[i].start()

    def last():
        for one, two in plans:
            for copy in two:
                copy.wait_recv()

    return first, middle, last


def direct_sum(place, sems, jobs):
    plans = []
    for axis, view, land, shape in jobs:
        at = along(place, axis)
        copies = [
            sems.ready(view((at + k) % 4, None), land[k - 1], moved(place, axis, k))
            for k in (1, 3, 2)
        ]
        plans.append((copies, view(at, None), land, shape))

    def first():
        for copies, *_ in plans:
            for copy in copies:
                copy.start()

    def last():
        for copies, own, land, shape in plans:
            for copy in copies:
                copy.wait_recv()
            added(own, land, shape)

    return first, last


def direct_spread(place, sems, jobs):
    plans = []
    for axis, view in jobs:
        here = view(along(place, axis), None)
        plans.append([sems.ready(here, here, moved(place, axis, k)) for k in (1, 3, 2)])

    def first():
        for copies in plans:
            for copy in copies:
                copy.start()

    def last():
        for copies in plans:
            for copy in copies:
                copy.wait_recv()

    return first, last


def whole_sum(place, sems, axis, source, land, result):
    copies = [
        sems.ready(source, land[k - 1], moved(place, axis, k)) for k in (1, 3, 2)
    ]

    def first():
        for copy in copies:
            copy.start()

    def last():
        for copy in copies:
            copy.wait_recv()
        total = sum([t[...].astype(f32) for t in land], source[...].astype(f32))
        result[...] = total.astype(bf16)

    return first, last


def phases(made):
    for phase in made:
        phase()


sum_parts = [(0, 48, 48), (96, 48, 48), (192, 32, 32)]


def kv_shape(free):
    lead = ()
    if "x" in free:
        lead += (2,)
    if "z" in free:
        lead += (4,)
    if "y" in free:
        lead += (4,)
    if "x" in free:
        lead += (2,)
    return lead


def closing_kernel(part_ref, dq_ref, turn, out_ref, work, own, group, local_sem, *rest):
    lands, (send, recv) = rest[:-2], rest[-2:]
    place = my_place()
    x, y, z, core = place
    sibling, cross = pair_of(place)
    greet([sibling] + others(place, "xyz"))
    keep = pltpu.make_async_copy(part_ref, work, local_sem.at[0])
    keep.start()
    keep.wait()
    sems = Sems(send, recv)
    at_land = 0
    for stage in range(3):
        jobs = []
        for (row, n0, n1), order in zip(sum_parts, orders):
            axis, free = order[stage], order[stage + 1 :]

            def view(at, half, row=row, n0=n0, n1=n1, axis=axis, free=free):
                rows = {None: pl.ds(row, n0 + n1), 0: pl.ds(row, n0), 1: pl.ds(row + n0, n1)}
                return chips(work, place, free, axis, at, rows[half])

            n_lands = 6 if stage == 0 else 3
            jobs.append((axis, view, lands[at_land : at_land + n_lands], kv_shape(free)))
            at_land += n_lands
        phases((ring_sum if stage == 0 else direct_sum)(place, sems, jobs))
    grads = work[x % 2, z, y, x // 2].astype(f32)
    cosine, sine = turn[0], turn[1]
    keys = grads * cosine - swapped(grads) * sine
    dq = dq_ref[...].reshape(CHIP, QC)
    padded = jnp.concatenate([dq, jnp.zeros((CHIP, HD), f32)], 1)
    wide_turn = [jnp.concatenate([t] * 4, 1)[:, :QC] for t in (cosine, sine)]
    queries = dq * wide_turn[0] - swapped(padded)[:, :QC] * wide_turn[1]
    lane = lanes((CHIP, 128))
    both = jnp.where(lane < HD, keys, grads)
    own[...] = jnp.concatenate([queries, jnp.zeros((CHIP, HD), f32), both], 1).astype(bf16)
    pieces = [pl.ds(64 * i, 64) for i in range(4)]
    over = [sems.start(own.at[p], group.at[1, core, p], cross) for p in pieces]
    beside = sems.start(own, group.at[0, core], sibling)
    group[0, core] = own[...]
    passed = []
    for copy, p in zip(over, pieces):
        copy.wait_recv()
        passed.append(sems.start(group.at[1, core, p], group.at[1, core, p], sibling))

    def put(chip):
        low, high = group[chip, 0].astype(f32), group[chip, 1].astype(f32)
        low_kv, high_kv = low[:, 512:], high[:, 512:]
        out_ref[chip] = jnp.concatenate(
            [
                low[:, :QC],
                high[:, :QC],
                jnp.where(lane < HD, low_kv, pltpu.roll(high_kv, HD, 1)),
                jnp.where(lane < HD, pltpu.roll(low_kv, HD, 1), high_kv),
            ],
            1,
        ).astype(bf16)

    beside.wait_recv()
    put(0)
    for copy in passed:
        copy.wait_recv()
    put(1)
    sems.finish()


def closing(part, dq, turn, cid):
    lands = []
    for stage in range(3):
        for (row, n0, n1), order in zip(sum_parts, orders):
            lead = kv_shape(order[stage + 1 :])
            for n in (n1, n0, n0, n1, n1, n0) if stage == 0 else [n0 + n1] * 3:
                lands.append(pltpu.VMEM((*lead, n, 128), bf16))
    shape = (2, 4, 4, 2, CHIP, 128)
    return call(
        closing_kernel,
        jax.ShapeDtypeStruct((2, CHIP, QKV), bf16),
        [
            pltpu.VMEM(shape, bf16),
            pltpu.VMEM((CHIP, 640), bf16),
            pltpu.VMEM((2, 2, CHIP, 640), bf16),
            pltpu.SemaphoreType.DMA((1,)),
            *lands,
        ],
        63,
        cid,
        (part, dq, turn),
    )


big_rows, small_rows = 240, 32
big_parts = [
    ("zy", (0, 128, 0, D), (0, 64, 0, D), (64, 64, 0, D)),
    ("yz", (128, 112, 0, D), (128, 64, 0, D), (192, 48, 0, D)),
]
small_parts = [("zy", (0, 32, 0, 512)), ("yz", (0, 32, 512, 384))]


def block_at(ref, lead, block):
    row, rows, column, columns = block
    return ref.at[(*lead, pl.ds(row, rows), pl.ds(column, columns))]


def weight_view(ref, place, order, stage, halves, only=slice(None)):
    _, y, z, _ = place

    def view(at, half):
        if stage == 0:
            lead = (at, only) if order[0] == "z" else (only, at)
        else:
            lead = (z, at) if order[0] == "z" else (at, y)
        return block_at(ref, lead, halves[0 if half is None else half + 1])

    return view


def sum_lands(parts, stage):
    lead = (4,) if stage == 0 else ()
    return [
        pltpu.VMEM((*lead, halves[h + 1][1], halves[h + 1][3]), bf16)
        for _, *halves in parts
        for h in (1, 0, 0, 1, 1, 0)
    ]


def weight_sum(kind, place, sems, parts, work, stage, lands):
    n = len(lands) // len(parts)
    return kind(
        place,
        sems,
        [
            (
                order[stage],
                weight_view(work, place, order, stage, halves),
                lands[n * i : n * i + n],
                (4,) if stage == 0 else (),
            )
            for i, (order, *halves) in enumerate(parts)
        ],
    )


def weight_spread(kind, place, sems, parts, out, stage, only=slice(None)):
    return kind(
        place,
        sems,
        [
            (order[stage], weight_view(out, place, order, stage, halves, only))
            for order, *halves in parts
        ],
    )


def mate_of(place):
    x, y, z, core = place
    return dev(x + 1 - 2 * (x % 2), y, z, core)


def final_kernel(
    big_ref, small_ref, vec_ref, big_out, small_out, vec_out,
    work, swap, vec_sums, vec_lands, local_sem, *more,
):
    lands, (send, recv) = more[:-2], more[-2:]
    place = my_place()
    x, y, z, core = place
    mate = mate_of(place)
    loads = [
        pltpu.make_async_copy(small_ref, work, local_sem.at[0]),
        pltpu.make_async_copy(big_ref, big_out.at[z, y], local_sem.at[1]),
    ]
    for copy in loads:
        copy.start()
    greet([*others(place, "yz"), mate])
    for copy in loads:
        copy.wait()
    sems = Sems(send, recv)
    sum0 = weight_sum(direct_sum, place, sems, small_parts, work, 0, lands[:6])
    sum1 = weight_sum(direct_sum, place, sems, small_parts, work, 1, lands[6:])
    vec_land = [vec_lands.at[i] for i in range(7)]
    vec0 = whole_sum(place, sems, "z", vec_ref, vec_land[:3], vec_sums.at[0])
    vec1 = whole_sum(place, sems, "y", vec_sums.at[0], vec_land[3:6], vec_sums.at[1])
    vec_pair = sems.ready(vec_sums.at[1], vec_land[6], mate)
    pair = sems.ready(work.at[z, y], swap, mate)
    big1 = weight_spread(direct_spread, place, sems, big_parts, big_out, 1)
    big0 = [
        weight_spread(ring_spread, place, sems, big_parts, big_out, 0, only) for only in range(4)
    ]
    out1 = weight_spread(direct_spread, place, sems, small_parts, small_out, 1)
    out0 = weight_spread(direct_spread, place, sems, small_parts, small_out, 0)
    sum0[0]()
    vec0[0]()
    big1[0]()
    sum0[1]()
    vec0[1]()
    sum1[0]()
    vec1[0]()
    big1[1]()
    big0[0][0]()
    big0[1][0]()
    sum1[1]()
    vec1[1]()
    pair.start()
    vec_pair.start()
    big0[0][1]()
    big0[2][0]()
    pair.wait_recv()
    small_out[z, y] = (work[z, y].astype(f32) + swap[...].astype(f32)).astype(bf16)
    out1[0]()
    vec_pair.wait_recv()
    vec_out[...] = vec_sums[1].astype(f32) + vec_land[6][...].astype(f32)
    big0[1][1]()
    big0[3][0]()
    out1[1]()
    out0[0]()
    big0[2][1]()
    big0[3][1]()
    out0[1]()
    for one in big0:
        one[2]()
    sems.finish()


def final(big, small, vectors, cid):
    shapes = [(4, 4, n, D) for n in (big_rows, small_rows)]
    vmem = pl.BlockSpec(memory_space=pltpu.VMEM)
    return call(
        final_kernel,
        (*[jax.ShapeDtypeStruct(s, bf16) for s in shapes], jax.ShapeDtypeStruct((16, D), f32)),
        [
            pltpu.VMEM(shapes[1], bf16),
            pltpu.VMEM((small_rows, D), bf16),
            pltpu.VMEM((2, 16, D), bf16),
            pltpu.VMEM((7, 16, D), bf16),
            pltpu.SemaphoreType.DMA((2,)),
            *[
                pltpu.VMEM((*lead, block[1], block[3]), bf16)
                for lead in ((4,), ())
                for _, block in small_parts
                for _ in range(3)
            ],
        ],
        12 + 8 + 6 + 32 + 12,
        cid,
        (big, small.reshape(shapes[1]), vectors),
        [vmem, pl.BlockSpec(memory_space=pl.ANY), vmem],
    )


NT = (((1,), (1,)), ((), ()))
ROWS = G * 128


def lanes(shape):
    return lax.broadcasted_iota(jnp.int32, shape, len(shape) - 1)


def split3(value):
    one = value.astype(bf16).astype(f32)
    two = (value - one).astype(bf16).astype(f32)
    three = (value - one - two).astype(bf16).astype(f32)
    return one, two, three


def keys_of(kv_ref, c, half):
    start = half * 128 if isinstance(half, int) else pl.multiple_of(half * 128, 128)
    tile = kv_ref[c, :, pl.ds(start, 128), :].reshape(256, 128)
    lane = lanes((256, 128))
    ones = jnp.ones((256, 128), bf16)
    return jnp.where(lane < HD, tile, ones), jnp.where(lane < HD, ones, tile)


def both_keys(kv_ref, c0, c1):
    pairs = zip(keys_of(kv_ref, c0, 0), keys_of(kv_ref, c1, 0))
    return [jnp.concatenate(pair, 0) for pair in pairs]


def hidden_keys(xhi):
    row = lax.broadcasted_iota(jnp.int32, (ROWS, 256), 0) % 128
    key = lax.broadcasted_iota(jnp.int32, (ROWS, 256), 1)
    return key > row + xhi * 128


def forward_kernel(scal, q_ref, kv_ref, o_ref, qe_ref, peak, acc):
    me, xhi = scal[32], scal[33]
    for h in range(2):
        for g in range(G):
            piece = q_ref[h, :, g * HD : (g + 1) * HD].astype(f32) * (1.0 / math.sqrt(HD))
            wide_piece = jnp.concatenate([piece, jnp.zeros((128, HD), f32)], 1)
            qe_ref[h, g * 128 : (g + 1) * 128, :] = wide_piece.astype(bf16)
    peak[...] = jnp.full((2, ROWS, 128), -1e30, f32)
    acc[...] = jnp.zeros((2, ROWS, 128), f32)

    def fold(half, kk, vv, hide=None):
        s = lax.dot_general(qe_ref[half], kk, NT, preferred_element_type=f32)
        if hide is not None:
            s = jnp.where(hide, -1e30, s)
        tiles = [s[:, e : e + 128] for e in range(0, s.shape[1], 128)]
        old = peak[half]
        top = jnp.maximum(
            old, jnp.max(functools.reduce(jnp.maximum, tiles), 1, keepdims=True)
        )
        peak[half] = top
        p = jnp.concatenate([jnp.exp(t - top) for t in tiles], 1).astype(bf16)
        acc[half] = acc[half] * jnp.exp(old - top) + jnp.dot(p, vv, preferred_element_type=f32)

    def early_pair(c0, c1):
        fold(1, *both_keys(kv_ref, c0, c1))

    def other(c):
        sel = scal[c]
        fold(sel, *keys_of(kv_ref, c, sel))

    def one(i, carry):
        c0, c1 = (me + 2 * i + 1) % 32, (me + 2 * i + 2) % 32
        early_pair(c0, c1)
        other(c0)
        other(c1)
        return carry

    lax.fori_loop(0, 15, one, 0)
    early_pair((me + 31) % 32, me)
    other((me + 31) % 32)
    fold(0, *keys_of(kv_ref, me, 0), hidden_keys(xhi))
    fold(1, *keys_of(kv_ref, me, 1), hidden_keys(xhi))
    lane = lanes((ROWS, 128))
    for h in range(2):
        total = acc[h][:, :1]
        held = qe_ref[h].astype(f32)
        for i, part in enumerate(split3(-(peak[h][:, :1] + jnp.log(total)))):
            held = jnp.where(lane == HD + i, part, held)
        qe_ref[h] = held.astype(bf16)
        out = acc[h] / total
        for g in range(G):
            o_ref[h, :, g * HD : (g + 1) * HD] = out[g * 128 : (g + 1) * 128, HD:]


def local_call(kernel, out_shape, scratch, args, flops):
    vmem = pl.BlockSpec(memory_space=pltpu.VMEM)
    return pl.pallas_call(
        kernel,
        out_shape=out_shape,
        in_specs=[pl.BlockSpec(memory_space=pltpu.SMEM)] + [vmem] * (len(args) - 1),
        out_specs=jax.tree.map(lambda _: vmem, out_shape),
        scratch_shapes=scratch,
        compiler_params=pltpu.CompilerParams(vmem_limit_bytes=VLIM),
        cost_estimate=pl.CostEstimate(
            flops=flops, bytes_accessed=10_000_000, transcendentals=15_000_000
        ),
    )(*args)


def attention_forward(scal, q, kv):
    return local_call(
        forward_kernel,
        (
            jax.ShapeDtypeStruct((2, 128, QC), f32),
            jax.ShapeDtypeStruct((2, ROWS, 128), bf16),
        ),
        [pltpu.VMEM((2, ROWS, 128), f32), pltpu.VMEM((2, ROWS, 128), f32)],
        (scal, q, kv),
        20_000_000_000,
    )


def backward_kernel(
    scal, qe_ref, o_ref, g_ref, kv_ref, gate_ref, up_ref, down_ref,
    dq_ref, dkv_ref, sum_ref,
    ge, qt, gt, dq, work, swap, local_sem, *more,
):
    lands, (send, recv) = more[:-2], more[-2:]
    place = my_place()
    x, y, z, core = place
    me, xhi = lax.axis_index("ctx"), x // 2
    loads = []
    for i, ref in enumerate((gate_ref, up_ref, down_ref)):
        row = 0
        while row < FS:
            chunk, at = divmod(i * FS + row, big_rows)
            n = min(FS - row, big_rows - at)
            into = work.at[chunk // 4, chunk % 4, pl.ds(at, n)]
            loads.append(
                pltpu.make_async_copy(ref.at[pl.ds(row, n)], into, local_sem.at[len(loads)])
            )
            row += n
    for copy in loads:
        copy.start()
    unused = 3 * FS - 15 * big_rows
    work[3, 3, unused:] = jnp.zeros((big_rows - unused, D), bf16)
    greet([moved(place, a, b) for a in "yz" for b in (1, -1)] + [mate_of(place)])
    for copy in loads:
        copy.wait()
    sems = Sems(send, recv)
    sum0 = weight_sum(ring_sum, place, sems, big_parts, work, 0, lands[:12])
    sum1 = weight_sum(ring_sum, place, sems, big_parts, work, 1, lands[12:])
    pair = sems.ready(work.at[z, y], swap, mate_of(place))
    sum0[0]()

    lane = lanes((128, 128))
    for h in range(2):
        for g in range(G):
            cols = slice(g * HD, (g + 1) * HD)
            piece = g_ref[h, :, cols].astype(f32)
            delta = jnp.sum(piece * o_ref[h, :, cols], 1, keepdims=True)
            held = jnp.concatenate([jnp.zeros((128, HD), f32), piece], 1)
            for i, value in enumerate(split3(-delta)):
                held = jnp.where(lane == i, value, held)
            rows = slice(g * 128, (g + 1) * 128)
            ge[h, rows, :] = held.astype(bf16)
            gt[h, :, rows] = held.T.astype(bf16)
            qt[h, :, rows] = qe_ref[h, rows, :].astype(f32).T.astype(bf16)
    dq[...] = jnp.zeros((2, ROWS, 128), f32)

    def picked(sel, early, late):
        return jnp.where(jnp.full(early.shape, sel, jnp.int32) > 0, late, early)

    def tile(half, kk, vv, hide=None, late=None):
        def rows_of(ref):
            return ref[half] if late is None else picked(half, ref[0], ref[1])

        s = lax.dot_general(rows_of(qe_ref), kk, NT, preferred_element_type=f32)
        if hide is not None:
            s = jnp.where(hide, -1e30, s)
        p = jnp.exp(s)
        dp = lax.dot_general(rows_of(ge), vv, NT, preferred_element_type=f32)
        ds = (p * dp).astype(bf16)
        step = jnp.dot(ds, kk, preferred_element_type=f32)
        if late is None:
            dq[half] += step
        else:
            dq[1] += step * late
            dq[0] += step * (1.0 - late)
        dk = jnp.dot(rows_of(qt), ds, preferred_element_type=f32)
        dv = jnp.dot(rows_of(gt), p.astype(bf16), preferred_element_type=f32)
        return jnp.concatenate([dk[:HD], dv[HD:]], 0).T

    def put(c, half, value):
        dkv_ref[c, :, half * 128 : (half + 1) * 128, :] = value.astype(bf16).reshape(2, 128, 128)

    def other(c, early):
        sel = scal[c]
        late = sel.astype(f32)
        pairs = zip(keys_of(kv_ref, c, 0), keys_of(kv_ref, c, 1))
        step = tile(sel, *[picked(sel, *pair) for pair in pairs], late=late)
        put(c, 0, early + step * (1.0 - late))
        put(c, 1, step * late)

    beside = {3: [sum0[1]], 10: [sum0[2], sum1[0]], 12: [sum1[1]], 14: [sum1[2], pair.start]}

    def one(i, carry):
        for at, steps in beside.items():

            @pl.when(i == at)
            def _(steps=steps):
                for step in steps:
                    step()

        c0, c1 = (me + 2 * i + 1) % 32, (me + 2 * i + 2) % 32
        early = tile(1, *both_keys(kv_ref, c0, c1))
        other(c0, early[:256])
        other(c1, early[256:])
        return carry

    lax.fori_loop(0, 15, one, 0)
    final_c = (me + 31) % 32
    early = tile(1, *both_keys(kv_ref, final_c, me))
    other(final_c, early[:256])
    put(me, 0, early[256:] + tile(0, *keys_of(kv_ref, me, 0), hidden_keys(xhi)))
    put(me, 1, tile(1, *keys_of(kv_ref, me, 1), hidden_keys(xhi)))
    for h in range(2):
        for g in range(G):
            dq_ref[h, :, g * HD : (g + 1) * HD] = dq[h, g * 128 : (g + 1) * 128, :HD] * (
                1.0 / math.sqrt(HD)
            )
    pair.wait_recv()
    sum_ref[...] = (work[z, y].astype(f32) + swap[...].astype(f32)).astype(bf16)
    sems.finish()


def attention_backward(scal, qe, o, grad, kv, weight_grads, cid):
    big = (4, 4, big_rows, D)
    vmem = pl.BlockSpec(memory_space=pltpu.VMEM)
    return call(
        backward_kernel,
        (
            jax.ShapeDtypeStruct((2, 128, QC), f32),
            jax.ShapeDtypeStruct((32, 2, CHIP, 128), bf16),
            jax.ShapeDtypeStruct((big_rows, D), bf16),
        ),
        [
            pltpu.VMEM((2, ROWS, 128), bf16),
            pltpu.VMEM((2, 128, ROWS), bf16),
            pltpu.VMEM((2, 128, ROWS), bf16),
            pltpu.VMEM((2, ROWS, 128), f32),
            pltpu.VMEM(big, bf16),
            pltpu.VMEM((big_rows, D), bf16),
            pltpu.SemaphoreType.DMA((20,)),
            *sum_lands(big_parts, 0),
            *sum_lands(big_parts, 1),
        ],
        25,
        cid,
        (scal, qe, o, grad, kv, *weight_grads),
        [
            pl.BlockSpec(memory_space=pltpu.SMEM),
            *[vmem] * 4,
            *[pl.BlockSpec(memory_space=pl.ANY)] * 3,
        ],
    )


def rms_inverse(values):
    return lax.rsqrt(jnp.mean(values * values, -1, keepdims=True) + norm_eps)


def rms_pull(values, inverse, gain, grad):
    scaled = values * inverse
    e = grad * gain
    return inverse * (e - scaled * jnp.mean(e * scaled, -1, keepdims=True))


def rotation(positions):
    lane = jnp.arange(128)
    frequency = rope_base ** (-(2.0 * (lane % 32).astype(f32)) / HD)
    angles = positions.astype(f32)[:, None] * frequency[None, :]
    sign = jnp.where(lane % HD < HD // 2, -1.0, 1.0)
    return jnp.stack([jnp.cos(angles), jnp.sin(angles) * sign])


def dot(a, b):
    return jnp.dot(a, b, preferred_element_type=f32)


def body(
    tokens,
    out_grad,
    norm1_gain,
    qkv_weight,
    qkv_bias,
    out_weight,
    norm2_gain,
    gate_weight,
    up_weight,
    down_weight,
    positions,
):
    ctx = lax.axis_index("ctx")
    wsh = lax.axis_index("wsh")
    xhi, core = wsh // 2, wsh % 2
    my_block = positions[0] // 256

    def cut(array, start, size, axis):
        return lax.dynamic_slice_in_dim(array, start, size, axis)

    def own_rows(array):
        return cut(array.reshape(2, 2, 64, -1), core, 1, 1).reshape(TOK, -1)

    swap = [
        (c * 4 + w, ((c + 16) % 32) * 4 + (w + 2) % 4) for c in range(32) for w in range(4)
    ]
    twin = [(c * 4 + w, c * 4 + w + 1 - 2 * (w % 2)) for c in range(32) for w in range(4)]

    def crossed(array):
        return lax.ppermute(array, ("ctx", "wsh"), swap)

    def spread(vector, width):
        column = jnp.arange(QKV)
        values = jnp.pad(jnp.tile(vector, 4), (0, QKV - 4 * width))
        return jnp.where(column // width == wsh, values, 0)

    small = jnp.stack([spread(qkv_bias, 288), spread(norm1_gain, 224), spread(norm2_gain, 224)])
    small = jnp.pad(small, ((0, 13), (0, 0))).astype(bf16)
    offset = jnp.arange(128, dtype=jnp.int32) + xhi * 128
    turn = rotation(jnp.concatenate([my_block * 256 + offset, (63 - my_block) * 256 + offset]))
    mark = jnp.broadcast_to(my_block.astype(bf16), (KROWS - CHIP, 128))
    t_all, w_all, s_all, queries, kv_all = opening(
        tokens, out_grad, qkv_weight, small, turn, mark, 0
    )
    out_weight, kv_all = lax.optimization_barrier((out_weight, kv_all))
    out_full = lax.all_gather(out_weight, "wsh", axis=0, tiled=True)
    qkv_full = w_all.reshape(D, QKV)
    vectors = jnp.sum(s_all[:, 1:3, :D].astype(f32), 0)
    gain_one, gain_two = vectors[0], vectors[1]
    t_chip = t_all.reshape(2, CHIP, D)
    kv_all = kv_all.reshape(32, 2, KROWS, 128)
    blocks = kv_all[:, 0, CHIP, 0].astype(jnp.int32)
    scal = jnp.concatenate(
        [(blocks > my_block).astype(jnp.int32), jnp.stack([ctx, xhi]).astype(jnp.int32)]
    )
    t_chip, kv_all = lax.optimization_barrier((t_chip, kv_all))
    t_other = crossed(t_chip)
    attended_f, qe = attention_forward(scal, queries, kv_all)
    att = group_gather(attended_f.astype(bf16).reshape(CHIP, QC), 2)
    t_both = jnp.stack([t_chip, t_other], 1).reshape(2, 2 * CHIP, D)
    resid_both = t_both[0].astype(f32)
    cot = t_both[1]
    att_cols = [att[:, i].reshape(2 * CHIP, QC) for i in range(2)]
    stream = resid_both + dot(att_cols[0], out_full[:QC]) + dot(att_cols[1], out_full[QC:])
    inv_two = rms_inverse(stream)
    normed_two = (stream * inv_two * gain_two).astype(bf16)
    gate_pre = dot(normed_two, gate_weight)
    up_pre = dot(normed_two, up_weight)
    hidden_grad = jnp.einsum("td,fd->tf", cot, down_weight, preferred_element_type=f32)
    sigma = jax.nn.sigmoid(gate_pre)
    activated = gate_pre * sigma
    hidden = (activated * up_pre).astype(bf16)
    gate_grad = (hidden_grad * up_pre * sigma * (1.0 + gate_pre * (1.0 - sigma))).astype(bf16)
    up_grad = (hidden_grad * activated).astype(bf16)
    norm_part = jnp.einsum(
        "tf,df->td", gate_grad, gate_weight, preferred_element_type=f32
    ) + jnp.einsum("tf,df->td", up_grad, up_weight, preferred_element_type=f32)
    norm_grad = group_sum(norm_part.astype(bf16).reshape(2, 2, 2, 64, D), 3).reshape(CHIP, D)

    mlp_part = dot(hidden, down_weight).astype(bf16).reshape(2, 2, 2, 64, D)
    norm_other = crossed(norm_grad)
    mlp_got = lax.ppermute(cut(mlp_part, 1 - core, 1, 2), ("ctx", "wsh"), twin)
    mlp_sum = cut(mlp_part, core, 1, 2).astype(f32) + mlp_got.astype(f32)
    mlp_far = crossed(mlp_sum[1].astype(bf16))
    gate_wgrad = jnp.einsum("tf,td->fd", gate_grad, normed_two, preferred_element_type=f32)
    up_wgrad = jnp.einsum("tf,td->fd", up_grad, normed_two, preferred_element_type=f32)
    down_wgrad = jnp.einsum("tf,td->fd", hidden, cot, preferred_element_type=f32)

    def stream_pull(part, grad):
        rows = slice(part * CHIP, (part + 1) * CHIP)
        return cot[rows].astype(f32) + rms_pull(
            stream[rows], inv_two[rows], gain_two, grad.astype(f32)
        )

    stream_grad = stream_pull(0, norm_grad)
    branch_grad = stream_grad.astype(bf16)
    att_grad = jnp.einsum(
        "td,id->ti", branch_grad, cut(out_full, core * QC, QC, 0), preferred_element_type=f32
    ).astype(bf16)
    large = [w.astype(bf16) for w in (gate_wgrad, up_wgrad, down_wgrad)]
    dq, dkv_part, large_own = attention_backward(
        scal, qe, attended_f, att_grad.reshape(2, 128, QC), kv_all, large, 5
    )
    norm_other, mlp_far, dq = lax.optimization_barrier((norm_other, mlp_far, dq))
    pg = closing(dkv_part.reshape(2, 4, 4, 2, CHIP, 128), dq, turn, 4).reshape(2 * CHIP, QKV)

    mlp_own = (mlp_sum[0] + mlp_far.astype(f32)).reshape(TOK, D)
    output = (own_rows(stream[:CHIP]) + mlp_own).astype(bf16)

    bias_grad = cut(jnp.sum(pg.astype(f32), 0), wsh * 288, 288, 0)
    inv_one = rms_inverse(resid_both)
    scaled_one = cut(resid_both, wsh * 224, 224, 1) * inv_one
    normed_cols = (scaled_one * norm1_gain.astype(f32)).astype(bf16)
    qkv_wgrad = jnp.einsum("td,tf->df", normed_cols, pg, preferred_element_type=f32)
    one_cols = jnp.einsum("tf,df->td", pg, qkv_weight, preferred_element_type=f32)
    gain_one_grad = jnp.sum(one_cols * scaled_one, 0)
    branch_both = jnp.concatenate(
        [branch_grad, stream_pull(1, norm_other).astype(bf16)], 0
    )
    norm_both = jnp.concatenate([norm_grad, norm_other], 0)
    scaled_two = cut(stream, wsh * 224, 224, 1) * inv_two
    gain_two_grad = jnp.sum(cut(norm_both, wsh * 224, 224, 1).astype(f32) * scaled_two, 0)
    att_mine = cut(jnp.where(wsh < 2, att_cols[0], att_cols[1]), (wsh % 2) * 224, 224, 1)
    out_wgrad = jnp.einsum("ti,td->id", att_mine, branch_both, preferred_element_type=f32)
    pg_own = own_rows(pg[:CHIP])
    one_grad = jnp.einsum("tf,df->td", pg_own, qkv_full, preferred_element_type=f32)
    resid_own = tokens.astype(f32)
    token_grad = own_rows(stream_grad) + rms_pull(
        resid_own, rms_inverse(resid_own), gain_one, one_grad
    )
    vectors = jnp.stack(
        [jnp.pad(v, (0, D - v.shape[0])) for v in (bias_grad, gain_one_grad, gain_two_grad)]
    )
    small = jnp.concatenate(
        [out_wgrad.astype(bf16), qkv_wgrad.astype(bf16).reshape(288, D)], 0
    )
    vectors = jnp.pad(vectors, ((0, 13), (0, 0))).astype(bf16)
    large, small, vectors = final(large_own, small, vectors, 6)
    large, small = large.reshape(16 * big_rows, D), small.reshape(16 * small_rows, D)
    return (
        output,
        token_grad,
        vectors[1, :224],
        small[224:].reshape(224, QKV).astype(f32),
        vectors[0, :288],
        small[:224].astype(f32),
        vectors[2, :224],
        large[:FS].astype(f32).T,
        large[FS : 2 * FS].astype(f32).T,
        large[2 * FS : 3 * FS].astype(f32),
    )


def solution(mesh):
    rows = P(("ctx", "wsh"), None)
    return jax.shard_map(
        body,
        mesh=mesh,
        in_specs=(
            rows,
            rows,
            P("wsh"),
            P("wsh", None),
            P("wsh"),
            P("wsh", None),
            P("wsh"),
            P(None, "wsh"),
            P(None, "wsh"),
            P("wsh", None),
            P(("ctx", "wsh")),
        ),
        out_specs=(
            rows,
            rows,
            P("wsh"),
            P("wsh", None),
            P("wsh"),
            P("wsh", None),
            P("wsh"),
            P(None, "wsh"),
            P(None, "wsh"),
            P("wsh", None),
        ),
        check_vma=False,
    )
```

```python
import functools
import math

import jax
import jax.numpy as jnp
from jax import lax
from jax.experimental import pallas as pl
from jax.experimental.pallas import tpu as pltpu
from jax.sharding import PartitionSpec as P

H = 14
KVH = 2
HD = 64
G = H // KVH
D = 896
FS = 1216
QKV = 1152
QC = G * HD
PC = QC + 2 * HD
TOK = 128
CHIP = 256
KROWS = 272

MESH = pl.DeviceIdType.MESH
VLIM = 56 * 1024 * 1024
norm_eps = 1e-06
rope_base = 1000000.0
f32 = jnp.float32
bf16 = jnp.bfloat16


def my_place():
    c = lax.axis_index("ctx")
    w = lax.axis_index("wsh")
    return (w // 2) * 2 + c // 16, c % 4, (c // 4) % 4, w % 2


def dev(x, y, z, core):
    return ((x % 2) * 16 + z * 4 + y, (x // 2) * 2 + core)


def moved(place, axis, by):
    x, y, z, core = place
    if axis == "x":
        return dev((x + by + 4) % 4, y, z, core)
    if axis == "y":
        return dev(x, (y + by + 4) % 4, z, core)
    return dev(x, y, (z + by + 4) % 4, core)


def along(place, axis):
    return place["xyz".index(axis)]


def others(place, axes):
    return [moved(place, a, k) for a in axes for k in (1, 2, 3)]


def greet(devices):
    barrier = pltpu.get_barrier_semaphore()
    for device in devices:
        pl.semaphore_signal(barrier, inc=1, device_id=device, device_id_type=MESH)
    pl.semaphore_wait(barrier, len(devices))


class Sems:
    def __init__(self, send, recv):
        self.send, self.recv, self.at = send, recv, 0
        self.started = []

    def copy(self, src, dst, device):
        i = self.at
        self.at += 1
        return pltpu.make_async_remote_copy(
            src_ref=src,
            dst_ref=dst,
            send_sem=self.send.at[i],
            recv_sem=self.recv.at[i],
            device_id=device,
            device_id_type=MESH,
        )

    def ready(self, src, dst, device):
        copy = self.copy(src, dst, device)
        self.started.append(copy)
        return copy

    def start(self, src, dst, device):
        copy = self.ready(src, dst, device)
        copy.start()
        return copy

    def finish(self):
        for copy in self.started:
            copy.wait_send()


def call(kernel, out_shape, scratch, n_sems, cid, args, specs=None):
    vmem = pl.BlockSpec(memory_space=pltpu.VMEM)
    outs = jax.tree.map(lambda _: vmem, out_shape)
    return pl.pallas_call(
        kernel,
        out_shape=out_shape,
        in_specs=specs if specs is not None else [vmem] * len(args),
        out_specs=outs,
        scratch_shapes=[
            *scratch,
            pltpu.SemaphoreType.DMA((n_sems,)),
            pltpu.SemaphoreType.DMA((n_sems,)),
        ],
        compiler_params=pltpu.CompilerParams(
            collective_id=cid, has_side_effects=True, vmem_limit_bytes=VLIM
        ),
    )(*args)


def pair_of(place):
    x, y, z, core = place
    return dev(x, y, z, 1 - core), dev(3 - x, y, z, core)


def group_kernel(a_ref, out_ref, local_sem, send, recv):
    place = my_place()
    core = place[3]
    sibling, cross = pair_of(place)
    greet([sibling, cross])
    sems = Sems(send, recv)
    pieces = [pl.ds(64 * i, 64) for i in range(4)]
    over = [sems.start(a_ref.at[p], out_ref.at[1, core, p], cross) for p in pieces]
    own = sems.start(a_ref, out_ref.at[0, core], sibling)
    keep = pltpu.make_async_copy(a_ref, out_ref.at[0, core], local_sem.at[0])
    keep.start()
    passed = []
    for copy, p in zip(over, pieces):
        copy.wait_recv()
        passed.append(sems.start(out_ref.at[1, core, p], out_ref.at[1, core, p], sibling))
    for copy in [own, *passed]:
        copy.wait_recv()
    keep.wait()
    sems.finish()


def group_gather(array, cid):
    return call(
        group_kernel,
        jax.ShapeDtypeStruct((2, 2, *array.shape), array.dtype),
        [pltpu.SemaphoreType.DMA((1,))],
        9,
        cid,
        (array,),
    )


def group_sum_kernel(p_ref, out_ref, got, total, far, send, recv):
    place = my_place()
    core = place[3]
    sibling, cross = pair_of(place)
    greet([sibling, cross])
    sems = Sems(send, recv)
    in_other = [sems.start(p_ref.at[1, h, 1 - core], got.at[1, h], sibling) for h in range(2)]
    in_own = [sems.start(p_ref.at[0, h, 1 - core], got.at[0, h], sibling) for h in range(2)]
    over = []
    for h in range(2):
        in_other[h].wait_recv()
        total[1, h] = (p_ref[1, h, core].astype(f32) + got[1, h].astype(f32)).astype(bf16)
        over.append(sems.start(total.at[1, h], far.at[h], cross))
    last = []
    for h in range(2):
        in_own[h].wait_recv()
        over[h].wait_recv()
        out_ref[h, core] = (
            p_ref[0, h, core].astype(f32) + got[0, h].astype(f32) + far[h].astype(f32)
        ).astype(bf16)
        last.append(sems.start(out_ref.at[h, core], out_ref.at[h, core], sibling))
    for copy in last:
        copy.wait_recv()
    sems.finish()


def group_sum(part, cid):
    rows = (2, 64, D)
    return call(
        group_sum_kernel,
        jax.ShapeDtypeStruct((2, 2, 64, D), bf16),
        [pltpu.VMEM((2, *rows), bf16), pltpu.VMEM((2, *rows), bf16), pltpu.VMEM(rows, bf16)],
        8,
        cid,
        (part,),
    )


orders = (("z", "y", "x"), ("y", "x", "z"), ("x", "z", "y"))


def chips(ref, place, free, axis, at, rows):
    x, y, z, _ = place
    index = {"x": x, "y": y, "z": z}
    index[axis] = at
    every = slice(None)
    xlo, xhi = (every, every) if "x" in free else (index["x"] % 2, index["x"] // 2)
    return ref.at[
        xlo, every if "z" in free else index["z"], every if "y" in free else index["y"], xhi, rows
    ]


def swapped(values):
    width = values.shape[1]
    first = lanes(values.shape) % HD < HD // 2
    return jnp.where(first, pltpu.roll(values, width - 32, 1), pltpu.roll(values, 32, 1))


def opening_kernel(
    tok, cot, w_ref, small, turn, mark, t_out, w_out, s_out, q_out, all_ref, local_sem, send, recv
):
    place = my_place()
    x, y, z, core = place
    sibling, cross = pair_of(place)
    mate = dev(x + 1 - 2 * (x % 2), y, z, core)
    greet([sibling] + others(place, "xyz"))
    sems = Sems(send, recv)
    mine = (x // 2) * 2 + core
    theirs = (1 - x // 2) * 2 + core
    cut = ((0, 48), (48, 64))
    got, sent = (x % 2) * 112, (1 - x % 2) * 112

    def rows(start, at, size):
        return pl.ds(pl.multiple_of(start + at, 16), size)

    mark_rows = pl.ds(CHIP, KROWS - CHIP)
    here = all_ref.at[x % 2, z, y, x // 2]
    own = [sems.start(ref, t_out.at[i, :, core], sibling) for i, ref in enumerate((tok, cot))]
    over = [
        sems.start(w_ref.at[rows(sent, at, n)], w_out.at[mine, rows(sent, at, n)], cross)
        for at, n in cut
    ]
    over_small = sems.start(small, s_out.at[mine], cross)
    own += [sems.start(w_ref, w_out.at[mine], sibling), sems.start(small, s_out.at[mine], sibling)]
    keep = [
        pltpu.make_async_copy(tok, t_out.at[0, :, core], local_sem.at[0]),
        pltpu.make_async_copy(cot, t_out.at[1, :, core], local_sem.at[1]),
        pltpu.make_async_copy(w_ref, w_out.at[mine], local_sem.at[2]),
        pltpu.make_async_copy(small, s_out.at[mine], local_sem.at[3]),
        pltpu.make_async_copy(mark, here.at[mark_rows], local_sem.at[4]),
    ]
    for copy in keep:
        copy.start()
    shared, passed = [], []
    for copy, (at, n) in zip(over, cut):
        copy.wait_recv()
        piece = w_out.at[theirs, rows(got, at, n)]
        shared.append(sems.start(piece, piece, mate))
        passed.append(sems.start(piece, piece, sibling))
    over_small.wait_recv()
    passed.append(sems.start(s_out.at[theirs], s_out.at[theirs], sibling))
    for copy in keep:
        copy.wait()
    own[0].wait_recv()
    resid = t_out[0].reshape(CHIP, D).astype(f32)
    for copy, (at, n) in zip(shared, cut):
        copy.wait_recv()
        piece = w_out.at[theirs, rows(sent, at, n)]
        passed.append(sems.start(piece, piece, sibling))
    for copy in own[1:] + passed:
        copy.wait_recv()
    vectors = jnp.sum(s_out[...].astype(f32), 0)
    inverse = lax.rsqrt(jnp.mean(resid * resid, -1, keepdims=True) + norm_eps)
    normed = (resid * inverse * vectors[1:2, :D]).astype(bf16)
    projected = jnp.dot(
        normed, w_out[...].reshape(D, QKV), preferred_element_type=f32
    ) + vectors[0:1]
    first = core == 0
    queries = jnp.where(first, projected[:, :QC], projected[:, QC : 2 * QC])
    keys = projected[:, H * HD : H * HD + KVH * HD]
    keys = jnp.where(first, keys, pltpu.roll(keys, HD, 1))
    values = projected[:, (H + KVH) * HD :]
    values = jnp.where(first, pltpu.roll(values, HD, 1), values)
    cosine, sine = turn[0], turn[1]
    keys = keys * cosine + swapped(keys) * sine
    wide_turn = [jnp.concatenate([t] * 4, 1)[:, :QC] for t in (cosine, sine)]
    padded = jnp.concatenate([queries, jnp.zeros((CHIP, HD), f32)], 1)
    queries = queries * wide_turn[0] + swapped(padded)[:, :QC] * wide_turn[1]
    q_out[...] = queries.astype(bf16).reshape(2, 128, QC)
    here[0:CHIP, :] = jnp.where(lanes((CHIP, 128)) < HD, keys, values).astype(bf16)

    parts = [(0, 48, 48), (96, 48, 48), (192, 48, 32)]
    for stage in range(3):
        jobs = []
        for (row, n0, n1), order in zip(parts, orders):
            axis, free = order[stage], order[:stage]

            def view(at, half, row=row, n0=n0, n1=n1, axis=axis, free=free):
                rows = {None: pl.ds(row, n0 + n1), 0: pl.ds(row, n0), 1: pl.ds(row + n0, n1)}
                return chips(all_ref, place, free, axis, at, rows[half])

            jobs.append((axis, view))
        phases((ring_spread if stage == 2 else direct_spread)(place, sems, jobs))
    sems.finish()


def opening(tokens, out_grad, weight, small, turn, mark, cid):
    return call(
        opening_kernel,
        (
            jax.ShapeDtypeStruct((2, 2, 2, 64, D), bf16),
            jax.ShapeDtypeStruct((4, 224, QKV), bf16),
            jax.ShapeDtypeStruct((4, 16, QKV), bf16),
            jax.ShapeDtypeStruct((2, 128, QC), bf16),
            jax.ShapeDtypeStruct((2, 4, 4, 2, KROWS, 128), bf16),
        ),
        [pltpu.SemaphoreType.DMA((5,))],
        50,
        cid,
        (tokens.reshape(2, 64, D), out_grad.reshape(2, 64, D), weight, small, turn, mark),
    )


def added(into, terms, shape):
    if not shape:
        into[...] = sum([t[...].astype(f32) for t in terms], into[...].astype(f32)).astype(bf16)
        return

    def one(i, carry):
        rest, index = i, []
        for size in reversed(shape):
            index.insert(0, rest % size)
            rest = rest // size
        index = tuple(index)
        into[index] = sum(
            [t[index].astype(f32) for t in terms], into[index].astype(f32)
        ).astype(bf16)
        return carry

    lax.fori_loop(0, math.prod(shape), one, 0)


def ring_sum(place, sems, jobs):
    plans = []
    for axis, view, land, shape in jobs:
        at = along(place, axis)
        after, far, before = (at + 1) % 4, (at + 2) % 4, (at + 3) % 4
        right, left = moved(place, axis, 1), moved(place, axis, -1)
        early = [
            sems.ready(view(far, 1), land[0], right),
            sems.ready(view(far, 0), land[1], left),
            sems.ready(view(after, 0), land[2], right),
            sems.ready(view(before, 1), land[3], left),
        ]
        sums = [view(after, 1), view(before, 0)]
        late = [sems.ready(sums[0], land[4], right), sems.ready(sums[1], land[5], left)]
        plans.append((early, sums, late, [view(at, 0), view(at, 1)], land, shape))

    def first():
        for early, *_ in plans:
            for copy in early[:2]:
                copy.start()
        for early, *_ in plans:
            for copy in early[2:]:
                copy.start()

    def middle():
        for early, sums, late, own, land, shape in plans:
            for i in range(2):
                early[i].wait_recv()
                added(sums[i], [land[i]], shape)
                late[i].start()

    def last():
        for early, sums, late, own, land, shape in plans:
            early[2].wait_recv()
            late[1].wait_recv()
            added(own[0], [land[2], land[5]], shape)
            early[3].wait_recv()
            late[0].wait_recv()
            added(own[1], [land[3], land[4]], shape)

    return first, middle, last


def ring_spread(place, sems, jobs):
    plans = []
    for axis, view in jobs:
        at = along(place, axis)
        after, before = (at + 1) % 4, (at + 3) % 4
        right, left = moved(place, axis, 1), moved(place, axis, -1)
        here, from_left, from_right = view(at, None), view(before, 0), view(after, 1)
        plans.append(
            (
                [sems.ready(here, here, right), sems.ready(here, here, left)],
                [sems.ready(from_left, from_left, right), sems.ready(from_right, from_right, left)],
            )
        )

    def first():
        for one, two in plans:
            for copy in one:
                copy.start()

    def middle():
        for one, two in plans:
            for i in range(2):
                one[i].wait_recv()
                two[i].start()

    def last():
        for one, two in plans:
            for copy in two:
                copy.wait_recv()

    return first, middle, last


def direct_sum(place, sems, jobs):
    plans = []
    for axis, view, land, shape in jobs:
        at = along(place, axis)
        copies = [
            sems.ready(view((at + k) % 4, None), land[k - 1], moved(place, axis, k))
            for k in (1, 3, 2)
        ]
        plans.append((copies, view(at, None), land, shape))

    def first():
        for copies, *_ in plans:
            for copy in copies:
                copy.start()

    def last():
        for copies, own, land, shape in plans:
            for copy in copies:
                copy.wait_recv()
            added(own, land, shape)

    return first, last


def direct_spread(place, sems, jobs):
    plans = []
    for axis, view in jobs:
        here = view(along(place, axis), None)
        plans.append([sems.ready(here, here, moved(place, axis, k)) for k in (1, 3, 2)])

    def first():
        for copies in plans:
            for copy in copies:
                copy.start()

    def last():
        for copies in plans:
            for copy in copies:
                copy.wait_recv()

    return first, last


def whole_sum(place, sems, axis, source, land, result):
    copies = [
        sems.ready(source, land[k - 1], moved(place, axis, k)) for k in (1, 3, 2)
    ]

    def first():
        for copy in copies:
            copy.start()

    def last():
        for copy in copies:
            copy.wait_recv()
        total = sum([t[...].astype(f32) for t in land], source[...].astype(f32))
        result[...] = total.astype(bf16)

    return first, last


def phases(made):
    for phase in made:
        phase()


sum_parts = [(0, 48, 48), (96, 48, 48), (192, 32, 32)]


def kv_shape(free):
    lead = ()
    if "x" in free:
        lead += (2,)
    if "z" in free:
        lead += (4,)
    if "y" in free:
        lead += (4,)
    if "x" in free:
        lead += (2,)
    return lead


def closing_kernel(
    part_ref, dq_ref, turn, big_ref, out_ref, big_out, work, own, group, local_sem, *rest
):
    lands, (send, recv) = rest[:-2], rest[-2:]
    place = my_place()
    x, y, z, core = place
    sibling, cross = pair_of(place)
    keep = [
        pltpu.make_async_copy(part_ref, work, local_sem.at[0]),
        pltpu.make_async_copy(big_ref, big_out.at[z, y], local_sem.at[1]),
    ]
    for copy in keep:
        copy.start()
    greet([sibling] + others(place, "xyz"))
    for copy in keep:
        copy.wait()
    sems = Sems(send, recv)
    big1 = weight_spread(direct_spread, place, sems, big_parts, big_out, 1)
    big0 = [
        weight_spread(ring_spread, place, sems, big_parts, big_out, 0, only) for only in range(4)
    ]
    at_land = 0
    for stage in range(3):
        jobs = []
        for (row, n0, n1), order in zip(sum_parts, orders):
            axis, free = order[stage], order[stage + 1 :]

            def view(at, half, row=row, n0=n0, n1=n1, axis=axis, free=free):
                rows = {None: pl.ds(row, n0 + n1), 0: pl.ds(row, n0), 1: pl.ds(row + n0, n1)}
                return chips(work, place, free, axis, at, rows[half])

            n_lands = 6 if stage == 0 else 3
            jobs.append((axis, view, lands[at_land : at_land + n_lands], kv_shape(free)))
            at_land += n_lands
        made = (ring_sum if stage == 0 else direct_sum)(place, sems, jobs)
        made[0]()
        if stage == 0:
            big1[0]()
            made[1]()
            big1[1]()
            big0[0][0]()
        elif stage == 1:
            big0[1][0]()
        else:
            big0[0][1]()
        made[-1]()
    grads = work[x % 2, z, y, x // 2].astype(f32)
    cosine, sine = turn[0], turn[1]
    keys = grads * cosine - swapped(grads) * sine
    dq = dq_ref[...].reshape(CHIP, QC)
    padded = jnp.concatenate([dq, jnp.zeros((CHIP, HD), f32)], 1)
    wide_turn = [jnp.concatenate([t] * 4, 1)[:, :QC] for t in (cosine, sine)]
    queries = dq * wide_turn[0] - swapped(padded)[:, :QC] * wide_turn[1]
    lane = lanes((CHIP, 128))
    both = jnp.where(lane < HD, keys, grads)
    own[...] = jnp.concatenate([queries, jnp.zeros((CHIP, HD), f32), both], 1).astype(bf16)
    pieces = [pl.ds(64 * i, 64) for i in range(4)]
    over = [sems.start(own.at[p], group.at[1, core, p], cross) for p in pieces]
    beside = sems.start(own, group.at[0, core], sibling)
    big0[2][0]()
    big0[1][1]()
    big0[3][0]()
    group[0, core] = own[...]
    passed = []
    for copy, p in zip(over, pieces):
        copy.wait_recv()
        passed.append(sems.start(group.at[1, core, p], group.at[1, core, p], sibling))

    def put(chip):
        low, high = group[chip, 0].astype(f32), group[chip, 1].astype(f32)
        low_kv, high_kv = low[:, 512:], high[:, 512:]
        out_ref[chip] = jnp.concatenate(
            [
                low[:, :QC],
                high[:, :QC],
                jnp.where(lane < HD, low_kv, pltpu.roll(high_kv, HD, 1)),
                jnp.where(lane < HD, pltpu.roll(low_kv, HD, 1), high_kv),
            ],
            1,
        ).astype(bf16)

    beside.wait_recv()
    put(0)
    for copy in passed:
        copy.wait_recv()
    big0[2][1]()
    put(1)
    big0[3][1]()
    for one in big0:
        one[2]()
    sems.finish()


def closing(part, dq, turn, big, cid):
    lands = []
    for stage in range(3):
        for (row, n0, n1), order in zip(sum_parts, orders):
            lead = kv_shape(order[stage + 1 :])
            for n in (n1, n0, n0, n1, n1, n0) if stage == 0 else [n0 + n1] * 3:
                lands.append(pltpu.VMEM((*lead, n, 128), bf16))
    shape = (2, 4, 4, 2, CHIP, 128)
    return call(
        closing_kernel,
        (
            jax.ShapeDtypeStruct((2, CHIP, QKV), bf16),
            jax.ShapeDtypeStruct((4, 4, big_rows, D), bf16),
        ),
        [
            pltpu.VMEM(shape, bf16),
            pltpu.VMEM((CHIP, 640), bf16),
            pltpu.VMEM((2, 2, CHIP, 640), bf16),
            pltpu.SemaphoreType.DMA((2,)),
            *lands,
        ],
        18 + 18 + 9 + 6 + 32,
        cid,
        (part, dq, turn, big),
    )


big_rows, small_rows = 240, 32
big_parts = [
    ("zy", (0, 128, 0, D), (0, 64, 0, D), (64, 64, 0, D)),
    ("yz", (128, 112, 0, D), (128, 64, 0, D), (192, 48, 0, D)),
]
small_parts = [("zy", (0, 32, 0, 512)), ("yz", (0, 32, 512, 384))]


def block_at(ref, lead, block):
    row, rows, column, columns = block
    return ref.at[(*lead, pl.ds(row, rows), pl.ds(column, columns))]


def weight_view(ref, place, order, stage, halves, only=slice(None)):
    _, y, z, _ = place

    def view(at, half):
        if stage == 0:
            lead = (at, only) if order[0] == "z" else (only, at)
        else:
            lead = (z, at) if order[0] == "z" else (at, y)
        return block_at(ref, lead, halves[0 if half is None else half + 1])

    return view


def sum_lands(parts, stage):
    lead = (4,) if stage == 0 else ()
    return [
        pltpu.VMEM((*lead, halves[h + 1][1], halves[h + 1][3]), bf16)
        for _, *halves in parts
        for h in (1, 0, 0, 1, 1, 0)
    ]


def weight_sum(kind, place, sems, parts, work, stage, lands):
    n = len(lands) // len(parts)
    return kind(
        place,
        sems,
        [
            (
                order[stage],
                weight_view(work, place, order, stage, halves),
                lands[n * i : n * i + n],
                (4,) if stage == 0 else (),
            )
            for i, (order, *halves) in enumerate(parts)
        ],
    )


def weight_spread(kind, place, sems, parts, out, stage, only=slice(None)):
    return kind(
        place,
        sems,
        [
            (order[stage], weight_view(out, place, order, stage, halves, only))
            for order, *halves in parts
        ],
    )


def mate_of(place):
    x, y, z, core = place
    return dev(x + 1 - 2 * (x % 2), y, z, core)


def final_kernel(
    small_ref, vec_ref, small_out, vec_out,
    work, swap, vec_sums, vec_lands, local_sem, *more,
):
    lands, (send, recv) = more[:-2], more[-2:]
    place = my_place()
    x, y, z, core = place
    mate = mate_of(place)
    load = pltpu.make_async_copy(small_ref, work, local_sem.at[0])
    load.start()
    greet([*others(place, "yz"), mate])
    load.wait()
    sems = Sems(send, recv)
    sum0 = weight_sum(direct_sum, place, sems, small_parts, work, 0, lands[:6])
    sum1 = weight_sum(direct_sum, place, sems, small_parts, work, 1, lands[6:])
    vec_land = [vec_lands.at[i] for i in range(7)]
    vec0 = whole_sum(place, sems, "z", vec_ref, vec_land[:3], vec_sums.at[0])
    vec1 = whole_sum(place, sems, "y", vec_sums.at[0], vec_land[3:6], vec_sums.at[1])
    vec_pair = sems.ready(vec_sums.at[1], vec_land[6], mate)
    pair = sems.ready(work.at[z, y], swap, mate)
    out1 = weight_spread(direct_spread, place, sems, small_parts, small_out, 1)
    out0 = weight_spread(direct_spread, place, sems, small_parts, small_out, 0)
    sum0[0]()
    vec0[0]()
    sum0[1]()
    sum1[0]()
    vec0[1]()
    vec1[0]()
    sum1[1]()
    pair.start()
    vec1[1]()
    vec_pair.start()
    pair.wait_recv()
    small_out[z, y] = (work[z, y].astype(f32) + swap[...].astype(f32)).astype(bf16)
    out1[0]()
    vec_pair.wait_recv()
    vec_out[...] = vec_sums[1].astype(f32) + vec_land[6][...].astype(f32)
    out1[1]()
    phases(out0)
    sems.finish()


def final(small, vectors, cid):
    shape = (4, 4, small_rows, D)
    vmem = pl.BlockSpec(memory_space=pltpu.VMEM)
    return call(
        final_kernel,
        (jax.ShapeDtypeStruct(shape, bf16), jax.ShapeDtypeStruct((16, D), f32)),
        [
            pltpu.VMEM(shape, bf16),
            pltpu.VMEM((small_rows, D), bf16),
            pltpu.VMEM((2, 16, D), bf16),
            pltpu.VMEM((7, 16, D), bf16),
            pltpu.SemaphoreType.DMA((1,)),
            *[
                pltpu.VMEM((*lead, block[1], block[3]), bf16)
                for lead in ((4,), ())
                for _, block in small_parts
                for _ in range(3)
            ],
        ],
        12 + 8 + 12,
        cid,
        (small.reshape(shape), vectors),
        [pl.BlockSpec(memory_space=pl.ANY), vmem],
    )


NT = (((1,), (1,)), ((), ()))
ROWS = G * 128


def lanes(shape):
    return lax.broadcasted_iota(jnp.int32, shape, len(shape) - 1)


def split3(value):
    one = value.astype(bf16).astype(f32)
    two = (value - one).astype(bf16).astype(f32)
    three = (value - one - two).astype(bf16).astype(f32)
    return one, two, three


def keys_of(kv_ref, c, half):
    start = half * 128 if isinstance(half, int) else pl.multiple_of(half * 128, 128)
    tile = kv_ref[c, :, pl.ds(start, 128), :].reshape(256, 128)
    lane = lanes((256, 128))
    ones = jnp.ones((256, 128), bf16)
    return jnp.where(lane < HD, tile, ones), jnp.where(lane < HD, ones, tile)


def both_keys(kv_ref, c0, c1):
    pairs = zip(keys_of(kv_ref, c0, 0), keys_of(kv_ref, c1, 0))
    return [jnp.concatenate(pair, 0) for pair in pairs]


def hidden_keys(xhi):
    row = lax.broadcasted_iota(jnp.int32, (ROWS, 256), 0) % 128
    key = lax.broadcasted_iota(jnp.int32, (ROWS, 256), 1)
    return key > row + xhi * 128


def forward_kernel(scal, q_ref, kv_ref, o_ref, qe_ref, peak, acc):
    me, xhi = scal[32], scal[33]
    for h in range(2):
        for g in range(G):
            piece = q_ref[h, :, g * HD : (g + 1) * HD].astype(f32) * (1.0 / math.sqrt(HD))
            wide_piece = jnp.concatenate([piece, jnp.zeros((128, HD), f32)], 1)
            qe_ref[h, g * 128 : (g + 1) * 128, :] = wide_piece.astype(bf16)
    peak[...] = jnp.full((2, ROWS, 128), -1e30, f32)
    acc[...] = jnp.zeros((2, ROWS, 128), f32)

    def fold(half, kk, vv, hide=None):
        s = lax.dot_general(qe_ref[half], kk, NT, preferred_element_type=f32)
        if hide is not None:
            s = jnp.where(hide, -1e30, s)
        tiles = [s[:, e : e + 128] for e in range(0, s.shape[1], 128)]
        old = peak[half]
        top = jnp.maximum(
            old, jnp.max(functools.reduce(jnp.maximum, tiles), 1, keepdims=True)
        )
        peak[half] = top
        p = jnp.concatenate([jnp.exp(t - top) for t in tiles], 1).astype(bf16)
        acc[half] = acc[half] * jnp.exp(old - top) + jnp.dot(p, vv, preferred_element_type=f32)

    def early_pair(c0, c1):
        fold(1, *both_keys(kv_ref, c0, c1))

    def other(c):
        sel = scal[c]
        fold(sel, *keys_of(kv_ref, c, sel))

    def one(i, carry):
        c0, c1 = (me + 2 * i + 1) % 32, (me + 2 * i + 2) % 32
        early_pair(c0, c1)
        other(c0)
        other(c1)
        return carry

    lax.fori_loop(0, 15, one, 0)
    early_pair((me + 31) % 32, me)
    other((me + 31) % 32)
    fold(0, *keys_of(kv_ref, me, 0), hidden_keys(xhi))
    fold(1, *keys_of(kv_ref, me, 1), hidden_keys(xhi))
    lane = lanes((ROWS, 128))
    for h in range(2):
        total = acc[h][:, :1]
        held = qe_ref[h].astype(f32)
        for i, part in enumerate(split3(-(peak[h][:, :1] + jnp.log(total)))):
            held = jnp.where(lane == HD + i, part, held)
        qe_ref[h] = held.astype(bf16)
        out = acc[h] / total
        for g in range(G):
            o_ref[h, :, g * HD : (g + 1) * HD] = out[g * 128 : (g + 1) * 128, HD:]


def local_call(kernel, out_shape, scratch, args, flops):
    vmem = pl.BlockSpec(memory_space=pltpu.VMEM)
    return pl.pallas_call(
        kernel,
        out_shape=out_shape,
        in_specs=[pl.BlockSpec(memory_space=pltpu.SMEM)] + [vmem] * (len(args) - 1),
        out_specs=jax.tree.map(lambda _: vmem, out_shape),
        scratch_shapes=scratch,
        compiler_params=pltpu.CompilerParams(vmem_limit_bytes=VLIM),
        cost_estimate=pl.CostEstimate(
            flops=flops, bytes_accessed=10_000_000, transcendentals=15_000_000
        ),
    )(*args)


def attention_forward(scal, q, kv):
    return local_call(
        forward_kernel,
        (
            jax.ShapeDtypeStruct((2, 128, QC), f32),
            jax.ShapeDtypeStruct((2, ROWS, 128), bf16),
        ),
        [pltpu.VMEM((2, ROWS, 128), f32), pltpu.VMEM((2, ROWS, 128), f32)],
        (scal, q, kv),
        20_000_000_000,
    )


def backward_kernel(
    scal, qe_ref, o_ref, g_ref, kv_ref, gate_ref, up_ref, down_ref,
    dq_ref, dkv_ref, sum_ref,
    ge, qt, gt, dq, work, swap, local_sem, *more,
):
    lands, (send, recv) = more[:-2], more[-2:]
    place = my_place()
    x, y, z, core = place
    me, xhi = lax.axis_index("ctx"), x // 2
    loads = []
    for i, ref in enumerate((gate_ref, up_ref, down_ref)):
        row = 0
        while row < FS:
            chunk, at = divmod(i * FS + row, big_rows)
            n = min(FS - row, big_rows - at)
            into = work.at[chunk // 4, chunk % 4, pl.ds(at, n)]
            loads.append(
                pltpu.make_async_copy(ref.at[pl.ds(row, n)], into, local_sem.at[len(loads)])
            )
            row += n
    for copy in loads:
        copy.start()
    unused = 3 * FS - 15 * big_rows
    work[3, 3, unused:] = jnp.zeros((big_rows - unused, D), bf16)
    greet([moved(place, a, b) for a in "yz" for b in (1, -1)] + [mate_of(place)])
    for copy in loads:
        copy.wait()
    sems = Sems(send, recv)
    sum0 = weight_sum(ring_sum, place, sems, big_parts, work, 0, lands[:12])
    sum1 = weight_sum(ring_sum, place, sems, big_parts, work, 1, lands[12:])
    pair = sems.ready(work.at[z, y], swap, mate_of(place))
    sum0[0]()

    lane = lanes((128, 128))
    for h in range(2):
        for g in range(G):
            cols = slice(g * HD, (g + 1) * HD)
            piece = g_ref[h, :, cols].astype(f32)
            delta = jnp.sum(piece * o_ref[h, :, cols], 1, keepdims=True)
            held = jnp.concatenate([jnp.zeros((128, HD), f32), piece], 1)
            for i, value in enumerate(split3(-delta)):
                held = jnp.where(lane == i, value, held)
            rows = slice(g * 128, (g + 1) * 128)
            ge[h, rows, :] = held.astype(bf16)
            gt[h, :, rows] = held.T.astype(bf16)
            qt[h, :, rows] = qe_ref[h, rows, :].astype(f32).T.astype(bf16)
    dq[...] = jnp.zeros((2, ROWS, 128), f32)

    def picked(sel, early, late):
        return jnp.where(jnp.full(early.shape, sel, jnp.int32) > 0, late, early)

    def tile(half, kk, vv, hide=None, late=None):
        def rows_of(ref):
            return ref[half] if late is None else picked(half, ref[0], ref[1])

        s = lax.dot_general(rows_of(qe_ref), kk, NT, preferred_element_type=f32)
        if hide is not None:
            s = jnp.where(hide, -1e30, s)
        p = jnp.exp(s)
        dp = lax.dot_general(rows_of(ge), vv, NT, preferred_element_type=f32)
        ds = (p * dp).astype(bf16)
        step = jnp.dot(ds, kk, preferred_element_type=f32)
        if late is None:
            dq[half] += step
        else:
            dq[1] += step * late
            dq[0] += step * (1.0 - late)
        dk = jnp.dot(rows_of(qt), ds, preferred_element_type=f32)
        dv = jnp.dot(rows_of(gt), p.astype(bf16), preferred_element_type=f32)
        return jnp.concatenate([dk[:HD], dv[HD:]], 0).T

    def put(c, half, value):
        dkv_ref[c, :, half * 128 : (half + 1) * 128, :] = value.astype(bf16).reshape(2, 128, 128)

    def other(c, early):
        sel = scal[c]
        late = sel.astype(f32)
        pairs = zip(keys_of(kv_ref, c, 0), keys_of(kv_ref, c, 1))
        step = tile(sel, *[picked(sel, *pair) for pair in pairs], late=late)
        put(c, 0, early + step * (1.0 - late))
        put(c, 1, step * late)

    beside = {3: [sum0[1]], 10: [sum0[2], sum1[0]], 12: [sum1[1]], 14: [sum1[2], pair.start]}

    def one(i, carry):
        for at, steps in beside.items():

            @pl.when(i == at)
            def _(steps=steps):
                for step in steps:
                    step()

        c0, c1 = (me + 2 * i + 1) % 32, (me + 2 * i + 2) % 32
        early = tile(1, *both_keys(kv_ref, c0, c1))
        other(c0, early[:256])
        other(c1, early[256:])
        return carry

    lax.fori_loop(0, 15, one, 0)
    final_c = (me + 31) % 32
    early = tile(1, *both_keys(kv_ref, final_c, me))
    other(final_c, early[:256])
    put(me, 0, early[256:] + tile(0, *keys_of(kv_ref, me, 0), hidden_keys(xhi)))
    put(me, 1, tile(1, *keys_of(kv_ref, me, 1), hidden_keys(xhi)))
    for h in range(2):
        for g in range(G):
            dq_ref[h, :, g * HD : (g + 1) * HD] = dq[h, g * 128 : (g + 1) * 128, :HD] * (
                1.0 / math.sqrt(HD)
            )
    pair.wait_recv()
    sum_ref[...] = (work[z, y].astype(f32) + swap[...].astype(f32)).astype(bf16)
    sems.finish()


def attention_backward(scal, qe, o, grad, kv, weight_grads, cid):
    big = (4, 4, big_rows, D)
    vmem = pl.BlockSpec(memory_space=pltpu.VMEM)
    return call(
        backward_kernel,
        (
            jax.ShapeDtypeStruct((2, 128, QC), f32),
            jax.ShapeDtypeStruct((32, 2, CHIP, 128), bf16),
            jax.ShapeDtypeStruct((big_rows, D), bf16),
        ),
        [
            pltpu.VMEM((2, ROWS, 128), bf16),
            pltpu.VMEM((2, 128, ROWS), bf16),
            pltpu.VMEM((2, 128, ROWS), bf16),
            pltpu.VMEM((2, ROWS, 128), f32),
            pltpu.VMEM(big, bf16),
            pltpu.VMEM((big_rows, D), bf16),
            pltpu.SemaphoreType.DMA((20,)),
            *sum_lands(big_parts, 0),
            *sum_lands(big_parts, 1),
        ],
        25,
        cid,
        (scal, qe, o, grad, kv, *weight_grads),
        [
            pl.BlockSpec(memory_space=pltpu.SMEM),
            *[vmem] * 4,
            *[pl.BlockSpec(memory_space=pl.ANY)] * 3,
        ],
    )


def rms_inverse(values):
    return lax.rsqrt(jnp.mean(values * values, -1, keepdims=True) + norm_eps)


def rms_pull(values, inverse, gain, grad):
    scaled = values * inverse
    e = grad * gain
    return inverse * (e - scaled * jnp.mean(e * scaled, -1, keepdims=True))


def rotation(positions):
    lane = jnp.arange(128)
    frequency = rope_base ** (-(2.0 * (lane % 32).astype(f32)) / HD)
    angles = positions.astype(f32)[:, None] * frequency[None, :]
    sign = jnp.where(lane % HD < HD // 2, -1.0, 1.0)
    return jnp.stack([jnp.cos(angles), jnp.sin(angles) * sign])


def dot(a, b):
    return jnp.dot(a, b, preferred_element_type=f32)


def body(
    tokens,
    out_grad,
    norm1_gain,
    qkv_weight,
    qkv_bias,
    out_weight,
    norm2_gain,
    gate_weight,
    up_weight,
    down_weight,
    positions,
):
    ctx = lax.axis_index("ctx")
    wsh = lax.axis_index("wsh")
    xhi, core = wsh // 2, wsh % 2
    my_block = positions[0] // 256

    def cut(array, start, size, axis):
        return lax.dynamic_slice_in_dim(array, start, size, axis)

    def own_rows(array):
        return cut(array.reshape(2, 2, 64, -1), core, 1, 1).reshape(TOK, -1)

    swap = [
        (c * 4 + w, ((c + 16) % 32) * 4 + (w + 2) % 4) for c in range(32) for w in range(4)
    ]
    twin = [(c * 4 + w, c * 4 + w + 1 - 2 * (w % 2)) for c in range(32) for w in range(4)]

    def crossed(array):
        return lax.ppermute(array, ("ctx", "wsh"), swap)

    def spread(vector, width):
        column = jnp.arange(QKV)
        values = jnp.pad(jnp.tile(vector, 4), (0, QKV - 4 * width))
        return jnp.where(column // width == wsh, values, 0)

    small = jnp.stack([spread(qkv_bias, 288), spread(norm1_gain, 224), spread(norm2_gain, 224)])
    small = jnp.pad(small, ((0, 13), (0, 0))).astype(bf16)
    offset = jnp.arange(128, dtype=jnp.int32) + xhi * 128
    turn = rotation(jnp.concatenate([my_block * 256 + offset, (63 - my_block) * 256 + offset]))
    mark = jnp.broadcast_to(my_block.astype(bf16), (KROWS - CHIP, 128))
    t_all, w_all, s_all, queries, kv_all = opening(
        tokens, out_grad, qkv_weight, small, turn, mark, 0
    )
    out_weight, kv_all = lax.optimization_barrier((out_weight, kv_all))
    out_full = lax.all_gather(out_weight, "wsh", axis=0, tiled=True)
    qkv_full = w_all.reshape(D, QKV)
    vectors = jnp.sum(s_all[:, 1:3, :D].astype(f32), 0)
    gain_one, gain_two = vectors[0], vectors[1]
    t_chip = t_all.reshape(2, CHIP, D)
    kv_all = kv_all.reshape(32, 2, KROWS, 128)
    blocks = kv_all[:, 0, CHIP, 0].astype(jnp.int32)
    scal = jnp.concatenate(
        [(blocks > my_block).astype(jnp.int32), jnp.stack([ctx, xhi]).astype(jnp.int32)]
    )
    t_chip, kv_all = lax.optimization_barrier((t_chip, kv_all))
    t_other = crossed(t_chip)
    attended_f, qe = attention_forward(scal, queries, kv_all)
    att = group_gather(attended_f.astype(bf16).reshape(CHIP, QC), 2)
    t_both = jnp.stack([t_chip, t_other], 1).reshape(2, 2 * CHIP, D)
    resid_both = t_both[0].astype(f32)
    cot = t_both[1]
    att_cols = [att[:, i].reshape(2 * CHIP, QC) for i in range(2)]
    stream = resid_both + dot(att_cols[0], out_full[:QC]) + dot(att_cols[1], out_full[QC:])
    inv_two = rms_inverse(stream)
    normed_two = (stream * inv_two * gain_two).astype(bf16)
    gate_pre = dot(normed_two, gate_weight)
    up_pre = dot(normed_two, up_weight)
    hidden_grad = jnp.einsum("td,fd->tf", cot, down_weight, preferred_element_type=f32)
    sigma = jax.nn.sigmoid(gate_pre)
    activated = gate_pre * sigma
    hidden = (activated * up_pre).astype(bf16)
    gate_grad = (hidden_grad * up_pre * sigma * (1.0 + gate_pre * (1.0 - sigma))).astype(bf16)
    up_grad = (hidden_grad * activated).astype(bf16)
    norm_part = jnp.einsum(
        "tf,df->td", gate_grad, gate_weight, preferred_element_type=f32
    ) + jnp.einsum("tf,df->td", up_grad, up_weight, preferred_element_type=f32)
    norm_grad = group_sum(norm_part.astype(bf16).reshape(2, 2, 2, 64, D), 3).reshape(CHIP, D)

    mlp_part = dot(hidden, down_weight).astype(bf16).reshape(2, 2, 2, 64, D)
    norm_other = crossed(norm_grad)
    mlp_got = lax.ppermute(cut(mlp_part, 1 - core, 1, 2), ("ctx", "wsh"), twin)
    mlp_sum = cut(mlp_part, core, 1, 2).astype(f32) + mlp_got.astype(f32)
    mlp_far = crossed(mlp_sum[1].astype(bf16))
    gate_wgrad = jnp.einsum("tf,td->fd", gate_grad, normed_two, preferred_element_type=f32)
    up_wgrad = jnp.einsum("tf,td->fd", up_grad, normed_two, preferred_element_type=f32)
    down_wgrad = jnp.einsum("tf,td->fd", hidden, cot, preferred_element_type=f32)

    def stream_pull(part, grad):
        rows = slice(part * CHIP, (part + 1) * CHIP)
        return cot[rows].astype(f32) + rms_pull(
            stream[rows], inv_two[rows], gain_two, grad.astype(f32)
        )

    stream_grad = stream_pull(0, norm_grad)
    branch_grad = stream_grad.astype(bf16)
    att_grad = jnp.einsum(
        "td,id->ti", branch_grad, cut(out_full, core * QC, QC, 0), preferred_element_type=f32
    ).astype(bf16)
    large = [w.astype(bf16) for w in (gate_wgrad, up_wgrad, down_wgrad)]
    dq, dkv_part, large_own = attention_backward(
        scal, qe, attended_f, att_grad.reshape(2, 128, QC), kv_all, large, 5
    )
    norm_other, mlp_far, dq = lax.optimization_barrier((norm_other, mlp_far, dq))
    pg, large = closing(dkv_part.reshape(2, 4, 4, 2, CHIP, 128), dq, turn, large_own, 4)
    pg, large = pg.reshape(2 * CHIP, QKV), large.reshape(16 * big_rows, D)

    mlp_own = (mlp_sum[0] + mlp_far.astype(f32)).reshape(TOK, D)
    output = (own_rows(stream[:CHIP]) + mlp_own).astype(bf16)

    bias_grad = cut(jnp.sum(pg.astype(f32), 0), wsh * 288, 288, 0)
    inv_one = rms_inverse(resid_both)
    scaled_one = cut(resid_both, wsh * 224, 224, 1) * inv_one
    normed_cols = (scaled_one * norm1_gain.astype(f32)).astype(bf16)
    qkv_wgrad = jnp.einsum("td,tf->df", normed_cols, pg, preferred_element_type=f32)
    one_cols = jnp.einsum("tf,df->td", pg, qkv_weight, preferred_element_type=f32)
    gain_one_grad = jnp.sum(one_cols * scaled_one, 0)
    branch_both = jnp.concatenate(
        [branch_grad, stream_pull(1, norm_other).astype(bf16)], 0
    )
    norm_both = jnp.concatenate([norm_grad, norm_other], 0)
    scaled_two = cut(stream, wsh * 224, 224, 1) * inv_two
    gain_two_grad = jnp.sum(cut(norm_both, wsh * 224, 224, 1).astype(f32) * scaled_two, 0)
    att_mine = cut(jnp.where(wsh < 2, att_cols[0], att_cols[1]), (wsh % 2) * 224, 224, 1)
    out_wgrad = jnp.einsum("ti,td->id", att_mine, branch_both, preferred_element_type=f32)
    pg_own = own_rows(pg[:CHIP])
    one_grad = jnp.einsum("tf,df->td", pg_own, qkv_full, preferred_element_type=f32)
    resid_own = tokens.astype(f32)
    token_grad = own_rows(stream_grad) + rms_pull(
        resid_own, rms_inverse(resid_own), gain_one, one_grad
    )
    vectors = jnp.stack(
        [jnp.pad(v, (0, D - v.shape[0])) for v in (bias_grad, gain_one_grad, gain_two_grad)]
    )
    small = jnp.concatenate(
        [out_wgrad.astype(bf16), qkv_wgrad.astype(bf16).reshape(288, D)], 0
    )
    vectors = jnp.pad(vectors, ((0, 13), (0, 0))).astype(bf16)
    small, vectors = final(small, vectors, 6)
    small = small.reshape(16 * small_rows, D)
    return (
        output,
        token_grad,
        vectors[1, :224],
        small[224:].reshape(224, QKV).astype(f32),
        vectors[0, :288],
        small[:224].astype(f32),
        vectors[2, :224],
        large[:FS].astype(f32).T,
        large[FS : 2 * FS].astype(f32).T,
        large[2 * FS : 3 * FS].astype(f32),
    )


def solution(mesh):
    rows = P(("ctx", "wsh"), None)
    return jax.shard_map(
        body,
        mesh=mesh,
        in_specs=(
            rows,
            rows,
            P("wsh"),
            P("wsh", None),
            P("wsh"),
            P("wsh", None),
            P("wsh"),
            P(None, "wsh"),
            P(None, "wsh"),
            P("wsh", None),
            P(("ctx", "wsh")),
        ),
        out_specs=(
            rows,
            rows,
            P("wsh"),
            P("wsh", None),
            P("wsh"),
            P("wsh", None),
            P("wsh"),
            P(None, "wsh"),
            P(None, "wsh"),
            P("wsh", None),
        ),
        check_vma=False,
    )
```

```python
import functools
import math

import jax
import jax.numpy as jnp
from jax import lax
from jax.experimental import pallas as pl
from jax.experimental.pallas import tpu as pltpu
from jax.sharding import PartitionSpec as P

H = 14
KVH = 2
HD = 64
G = H // KVH
D = 896
FS = 1216
QKV = 1152
QC = G * HD
PC = QC + 2 * HD
TOK = 128
CHIP = 256
KROWS = 272

MESH = pl.DeviceIdType.MESH
VLIM = 56 * 1024 * 1024
norm_eps = 1e-06
rope_base = 1000000.0
f32 = jnp.float32
bf16 = jnp.bfloat16


def my_place():
    c = lax.axis_index("ctx")
    w = lax.axis_index("wsh")
    return (w // 2) * 2 + c // 16, c % 4, (c // 4) % 4, w % 2


def dev(x, y, z, core):
    return ((x % 2) * 16 + z * 4 + y, (x // 2) * 2 + core)


def moved(place, axis, by):
    x, y, z, core = place
    if axis == "x":
        return dev((x + by + 4) % 4, y, z, core)
    if axis == "y":
        return dev(x, (y + by + 4) % 4, z, core)
    return dev(x, y, (z + by + 4) % 4, core)


def along(place, axis):
    return place["xyz".index(axis)]


def others(place, axes):
    return [moved(place, a, k) for a in axes for k in (1, 2, 3)]


def greet(devices):
    barrier = pltpu.get_barrier_semaphore()
    for device in devices:
        pl.semaphore_signal(barrier, inc=1, device_id=device, device_id_type=MESH)
    pl.semaphore_wait(barrier, len(devices))


class Sems:
    def __init__(self, send, recv):
        self.send, self.recv, self.at = send, recv, 0
        self.started = []

    def copy(self, src, dst, device):
        i = self.at
        self.at += 1
        return pltpu.make_async_remote_copy(
            src_ref=src,
            dst_ref=dst,
            send_sem=self.send.at[i],
            recv_sem=self.recv.at[i],
            device_id=device,
            device_id_type=MESH,
        )

    def ready(self, src, dst, device):
        copy = self.copy(src, dst, device)
        self.started.append(copy)
        return copy

    def start(self, src, dst, device):
        copy = self.ready(src, dst, device)
        copy.start()
        return copy

    def finish(self):
        for copy in self.started:
            copy.wait_send()


def call(kernel, out_shape, scratch, n_sems, cid, args, specs=None):
    vmem = pl.BlockSpec(memory_space=pltpu.VMEM)
    outs = jax.tree.map(lambda _: vmem, out_shape)
    return pl.pallas_call(
        kernel,
        out_shape=out_shape,
        in_specs=specs if specs is not None else [vmem] * len(args),
        out_specs=outs,
        scratch_shapes=[
            *scratch,
            pltpu.SemaphoreType.DMA((n_sems,)),
            pltpu.SemaphoreType.DMA((n_sems,)),
        ],
        compiler_params=pltpu.CompilerParams(
            collective_id=cid, has_side_effects=True, vmem_limit_bytes=VLIM
        ),
    )(*args)


def pair_of(place):
    x, y, z, core = place
    return dev(x, y, z, 1 - core), dev(3 - x, y, z, core)


orders = (("z", "y", "x"), ("y", "x", "z"), ("x", "z", "y"))


def chips(ref, place, free, axis, at, rows):
    x, y, z, _ = place
    index = {"x": x, "y": y, "z": z}
    index[axis] = at
    every = slice(None)
    xlo, xhi = (every, every) if "x" in free else (index["x"] % 2, index["x"] // 2)
    return ref.at[
        xlo, every if "z" in free else index["z"], every if "y" in free else index["y"], xhi, rows
    ]


def swapped(values):
    width = values.shape[1]
    first = lanes(values.shape) % HD < HD // 2
    return jnp.where(first, pltpu.roll(values, width - 32, 1), pltpu.roll(values, 32, 1))


def opening_kernel(
    tok, cot, w_ref, small, turn, mark, t_out, w_out, s_out, q_out, all_ref, local_sem, send, recv
):
    place = my_place()
    x, y, z, core = place
    sibling, cross = pair_of(place)
    mate = dev(x + 1 - 2 * (x % 2), y, z, core)
    greet([sibling] + others(place, "xyz"))
    sems = Sems(send, recv)
    mine = (x // 2) * 2 + core
    theirs = (1 - x // 2) * 2 + core
    cut = ((0, 48), (48, 64))
    got, sent = (x % 2) * 112, (1 - x % 2) * 112

    def rows(start, at, size):
        return pl.ds(pl.multiple_of(start + at, 16), size)

    mark_rows = pl.ds(CHIP, KROWS - CHIP)
    here = all_ref.at[x % 2, z, y, x // 2]
    own = [sems.start(ref, t_out.at[i, :, core], sibling) for i, ref in enumerate((tok, cot))]
    over = [
        sems.start(w_ref.at[rows(sent, at, n)], w_out.at[mine, rows(sent, at, n)], cross)
        for at, n in cut
    ]
    over_small = sems.start(small, s_out.at[mine], cross)
    own += [sems.start(w_ref, w_out.at[mine], sibling), sems.start(small, s_out.at[mine], sibling)]
    keep = [
        pltpu.make_async_copy(tok, t_out.at[0, :, core], local_sem.at[0]),
        pltpu.make_async_copy(cot, t_out.at[1, :, core], local_sem.at[1]),
        pltpu.make_async_copy(w_ref, w_out.at[mine], local_sem.at[2]),
        pltpu.make_async_copy(small, s_out.at[mine], local_sem.at[3]),
        pltpu.make_async_copy(mark, here.at[mark_rows], local_sem.at[4]),
    ]
    for copy in keep:
        copy.start()
    shared, passed = [], []
    for copy, (at, n) in zip(over, cut):
        copy.wait_recv()
        piece = w_out.at[theirs, rows(got, at, n)]
        shared.append(sems.start(piece, piece, mate))
        passed.append(sems.start(piece, piece, sibling))
    over_small.wait_recv()
    passed.append(sems.start(s_out.at[theirs], s_out.at[theirs], sibling))
    for copy in keep:
        copy.wait()
    own[0].wait_recv()
    resid = t_out[0].reshape(CHIP, D).astype(f32)
    for copy, (at, n) in zip(shared, cut):
        copy.wait_recv()
        piece = w_out.at[theirs, rows(sent, at, n)]
        passed.append(sems.start(piece, piece, sibling))
    for copy in own[1:] + passed:
        copy.wait_recv()
    vectors = jnp.sum(s_out[...].astype(f32), 0)
    inverse = lax.rsqrt(jnp.mean(resid * resid, -1, keepdims=True) + norm_eps)
    normed = (resid * inverse * vectors[1:2, :D]).astype(bf16)
    projected = jnp.dot(
        normed, w_out[...].reshape(D, QKV), preferred_element_type=f32
    ) + vectors[0:1]
    first = core == 0
    queries = jnp.where(first, projected[:, :QC], projected[:, QC : 2 * QC])
    keys = projected[:, H * HD : H * HD + KVH * HD]
    keys = jnp.where(first, keys, pltpu.roll(keys, HD, 1))
    values = projected[:, (H + KVH) * HD :]
    values = jnp.where(first, pltpu.roll(values, HD, 1), values)
    cosine, sine = turn[0], turn[1]
    keys = keys * cosine + swapped(keys) * sine
    wide_turn = [jnp.concatenate([t] * 4, 1)[:, :QC] for t in (cosine, sine)]
    padded = jnp.concatenate([queries, jnp.zeros((CHIP, HD), f32)], 1)
    queries = queries * wide_turn[0] + swapped(padded)[:, :QC] * wide_turn[1]
    q_out[...] = queries.astype(bf16).reshape(2, 128, QC)
    here[0:CHIP, :] = jnp.where(lanes((CHIP, 128)) < HD, keys, values).astype(bf16)

    parts = [(0, 48, 48), (96, 48, 48), (192, 48, 32)]
    for stage in range(3):
        jobs = []
        for (row, n0, n1), order in zip(parts, orders):
            axis, free = order[stage], order[:stage]

            def view(at, half, row=row, n0=n0, n1=n1, axis=axis, free=free):
                rows = {None: pl.ds(row, n0 + n1), 0: pl.ds(row, n0), 1: pl.ds(row + n0, n1)}
                return chips(all_ref, place, free, axis, at, rows[half])

            jobs.append((axis, view))
        phases((ring_spread if stage == 2 else direct_spread)(place, sems, jobs))
    sems.finish()


def opening(tokens, out_grad, weight, small, turn, mark, cid):
    return call(
        opening_kernel,
        (
            jax.ShapeDtypeStruct((2, 2, 2, 64, D), bf16),
            jax.ShapeDtypeStruct((4, 224, QKV), bf16),
            jax.ShapeDtypeStruct((4, 16, QKV), bf16),
            jax.ShapeDtypeStruct((2, 128, QC), bf16),
            jax.ShapeDtypeStruct((2, 4, 4, 2, KROWS, 128), bf16),
        ),
        [pltpu.SemaphoreType.DMA((5,))],
        50,
        cid,
        (tokens.reshape(2, 64, D), out_grad.reshape(2, 64, D), weight, small, turn, mark),
    )


def added(into, terms, shape):
    if not shape:
        into[...] = sum([t[...].astype(f32) for t in terms], into[...].astype(f32)).astype(bf16)
        return

    def one(i, carry):
        rest, index = i, []
        for size in reversed(shape):
            index.insert(0, rest % size)
            rest = rest // size
        index = tuple(index)
        into[index] = sum(
            [t[index].astype(f32) for t in terms], into[index].astype(f32)
        ).astype(bf16)
        return carry

    lax.fori_loop(0, math.prod(shape), one, 0)


def ring_sum(place, sems, jobs):
    plans = []
    for axis, view, land, shape in jobs:
        at = along(place, axis)
        after, far, before = (at + 1) % 4, (at + 2) % 4, (at + 3) % 4
        right, left = moved(place, axis, 1), moved(place, axis, -1)
        early = [
            sems.ready(view(far, 1), land[0], right),
            sems.ready(view(far, 0), land[1], left),
            sems.ready(view(after, 0), land[2], right),
            sems.ready(view(before, 1), land[3], left),
        ]
        sums = [view(after, 1), view(before, 0)]
        late = [sems.ready(sums[0], land[4], right), sems.ready(sums[1], land[5], left)]
        plans.append((early, sums, late, [view(at, 0), view(at, 1)], land, shape))

    def first():
        for early, *_ in plans:
            for copy in early[:2]:
                copy.start()
        for early, *_ in plans:
            for copy in early[2:]:
                copy.start()

    def middle():
        for early, sums, late, own, land, shape in plans:
            for i in range(2):
                early[i].wait_recv()
                added(sums[i], [land[i]], shape)
                late[i].start()

    def last():
        for early, sums, late, own, land, shape in plans:
            early[2].wait_recv()
            late[1].wait_recv()
            added(own[0], [land[2], land[5]], shape)
            early[3].wait_recv()
            late[0].wait_recv()
            added(own[1], [land[3], land[4]], shape)

    return first, middle, last


def ring_spread(place, sems, jobs):
    plans = []
    for axis, view in jobs:
        at = along(place, axis)
        after, before = (at + 1) % 4, (at + 3) % 4
        right, left = moved(place, axis, 1), moved(place, axis, -1)
        here, from_left, from_right = view(at, None), view(before, 0), view(after, 1)
        plans.append(
            (
                [sems.ready(here, here, right), sems.ready(here, here, left)],
                [sems.ready(from_left, from_left, right), sems.ready(from_right, from_right, left)],
            )
        )

    def first():
        for one, two in plans:
            for copy in one:
                copy.start()

    def middle():
        for one, two in plans:
            for i in range(2):
                one[i].wait_recv()
                two[i].start()

    def last():
        for one, two in plans:
            for copy in two:
                copy.wait_recv()

    return first, middle, last


def direct_sum(place, sems, jobs):
    plans = []
    for axis, view, land, shape in jobs:
        at = along(place, axis)
        copies = [
            sems.ready(view((at + k) % 4, None), land[k - 1], moved(place, axis, k))
            for k in (1, 3, 2)
        ]
        plans.append((copies, view(at, None), land, shape))

    def first():
        for copies, *_ in plans:
            for copy in copies:
                copy.start()

    def last():
        for copies, own, land, shape in plans:
            for copy in copies:
                copy.wait_recv()
            added(own, land, shape)

    return first, last


def direct_spread(place, sems, jobs):
    plans = []
    for axis, view in jobs:
        here = view(along(place, axis), None)
        plans.append([sems.ready(here, here, moved(place, axis, k)) for k in (1, 3, 2)])

    def first():
        for copies in plans:
            for copy in copies:
                copy.start()

    def last():
        for copies in plans:
            for copy in copies:
                copy.wait_recv()

    return first, last


def whole_sum(place, sems, axis, source, land, result):
    copies = [
        sems.ready(source, land[k - 1], moved(place, axis, k)) for k in (1, 3, 2)
    ]

    def first():
        for copy in copies:
            copy.start()

    def last():
        for copy in copies:
            copy.wait_recv()
        total = sum([t[...].astype(f32) for t in land], source[...].astype(f32))
        result[...] = total.astype(bf16)

    return first, last


def phases(made):
    for phase in made:
        phase()


sum_parts = [(0, 48, 48), (96, 48, 48), (192, 32, 32)]


def kv_shape(free):
    lead = ()
    if "x" in free:
        lead += (2,)
    if "z" in free:
        lead += (4,)
    if "y" in free:
        lead += (4,)
    if "x" in free:
        lead += (2,)
    return lead


def closing_kernel(
    part_ref, dq_ref, turn, big_ref, out_ref, big_out, work, own, group, local_sem, *rest
):
    lands, (send, recv) = rest[:-2], rest[-2:]
    place = my_place()
    x, y, z, core = place
    sibling, cross = pair_of(place)
    keep = [
        pltpu.make_async_copy(part_ref, work, local_sem.at[0]),
        pltpu.make_async_copy(big_ref, big_out.at[z, y], local_sem.at[1]),
    ]
    for copy in keep:
        copy.start()
    greet([sibling] + others(place, "xyz"))
    for copy in keep:
        copy.wait()
    sems = Sems(send, recv)
    big1 = weight_spread(direct_spread, place, sems, big_parts, big_out, 1)
    big0 = [
        weight_spread(ring_spread, place, sems, big_parts, big_out, 0, only) for only in range(4)
    ]
    at_land = 0
    for stage in range(3):
        jobs = []
        for (row, n0, n1), order in zip(sum_parts, orders):
            axis, free = order[stage], order[stage + 1 :]

            def view(at, half, row=row, n0=n0, n1=n1, axis=axis, free=free):
                rows = {None: pl.ds(row, n0 + n1), 0: pl.ds(row, n0), 1: pl.ds(row + n0, n1)}
                return chips(work, place, free, axis, at, rows[half])

            n_lands = 6 if stage == 0 else 3
            jobs.append((axis, view, lands[at_land : at_land + n_lands], kv_shape(free)))
            at_land += n_lands
        made = (ring_sum if stage == 0 else direct_sum)(place, sems, jobs)
        made[0]()
        if stage == 0:
            big1[0]()
            made[1]()
            big1[1]()
            big0[0][0]()
        elif stage == 1:
            big0[1][0]()
        else:
            big0[0][1]()
        made[-1]()
    grads = work[x % 2, z, y, x // 2].astype(f32)
    cosine, sine = turn[0], turn[1]
    keys = grads * cosine - swapped(grads) * sine
    dq = dq_ref[...].reshape(CHIP, QC)
    padded = jnp.concatenate([dq, jnp.zeros((CHIP, HD), f32)], 1)
    wide_turn = [jnp.concatenate([t] * 4, 1)[:, :QC] for t in (cosine, sine)]
    queries = dq * wide_turn[0] - swapped(padded)[:, :QC] * wide_turn[1]
    lane = lanes((CHIP, 128))
    both = jnp.where(lane < HD, keys, grads)
    own[...] = jnp.concatenate([queries, jnp.zeros((CHIP, HD), f32), both], 1).astype(bf16)
    pieces = [pl.ds(64 * i, 64) for i in range(4)]
    over = [sems.start(own.at[p], group.at[1, core, p], cross) for p in pieces]
    beside = sems.start(own, group.at[0, core], sibling)
    big0[2][0]()
    big0[1][1]()
    big0[3][0]()
    group[0, core] = own[...]
    passed = []
    for copy, p in zip(over, pieces):
        copy.wait_recv()
        passed.append(sems.start(group.at[1, core, p], group.at[1, core, p], sibling))

    def put(chip):
        low, high = group[chip, 0].astype(f32), group[chip, 1].astype(f32)
        low_kv, high_kv = low[:, 512:], high[:, 512:]
        out_ref[chip] = jnp.concatenate(
            [
                low[:, :QC],
                high[:, :QC],
                jnp.where(lane < HD, low_kv, pltpu.roll(high_kv, HD, 1)),
                jnp.where(lane < HD, pltpu.roll(low_kv, HD, 1), high_kv),
            ],
            1,
        ).astype(bf16)

    beside.wait_recv()
    put(0)
    for copy in passed:
        copy.wait_recv()
    big0[2][1]()
    put(1)
    big0[3][1]()
    for one in big0:
        one[2]()
    sems.finish()


def closing(part, dq, turn, big, cid):
    lands = []
    for stage in range(3):
        for (row, n0, n1), order in zip(sum_parts, orders):
            lead = kv_shape(order[stage + 1 :])
            for n in (n1, n0, n0, n1, n1, n0) if stage == 0 else [n0 + n1] * 3:
                lands.append(pltpu.VMEM((*lead, n, 128), bf16))
    shape = (2, 4, 4, 2, CHIP, 128)
    return call(
        closing_kernel,
        (
            jax.ShapeDtypeStruct((2, CHIP, QKV), bf16),
            jax.ShapeDtypeStruct((4, 4, big_rows, D), bf16),
        ),
        [
            pltpu.VMEM(shape, bf16),
            pltpu.VMEM((CHIP, 640), bf16),
            pltpu.VMEM((2, 2, CHIP, 640), bf16),
            pltpu.SemaphoreType.DMA((2,)),
            *lands,
        ],
        18 + 18 + 9 + 6 + 32,
        cid,
        (part, dq, turn, big),
    )


big_rows, small_rows = 240, 32
big_parts = [
    ("zy", (0, 128, 0, D), (0, 64, 0, D), (64, 64, 0, D)),
    ("yz", (128, 112, 0, D), (128, 64, 0, D), (192, 48, 0, D)),
]
small_parts = [("zy", (0, 32, 0, 512)), ("yz", (0, 32, 512, 384))]


def block_at(ref, lead, block):
    row, rows, column, columns = block
    return ref.at[(*lead, pl.ds(row, rows), pl.ds(column, columns))]


def weight_view(ref, place, order, stage, halves, only=slice(None)):
    _, y, z, _ = place

    def view(at, half):
        if stage == 0:
            lead = (at, only) if order[0] == "z" else (only, at)
        else:
            lead = (z, at) if order[0] == "z" else (at, y)
        return block_at(ref, lead, halves[0 if half is None else half + 1])

    return view


def sum_lands(parts, stage):
    lead = (4,) if stage == 0 else ()
    return [
        pltpu.VMEM((*lead, halves[h + 1][1], halves[h + 1][3]), bf16)
        for _, *halves in parts
        for h in (1, 0, 0, 1, 1, 0)
    ]


def weight_sum(kind, place, sems, parts, work, stage, lands):
    n = len(lands) // len(parts)
    return kind(
        place,
        sems,
        [
            (
                order[stage],
                weight_view(work, place, order, stage, halves),
                lands[n * i : n * i + n],
                (4,) if stage == 0 else (),
            )
            for i, (order, *halves) in enumerate(parts)
        ],
    )


def weight_spread(kind, place, sems, parts, out, stage, only=slice(None)):
    return kind(
        place,
        sems,
        [
            (order[stage], weight_view(out, place, order, stage, halves, only))
            for order, *halves in parts
        ],
    )


def mate_of(place):
    x, y, z, core = place
    return dev(x + 1 - 2 * (x % 2), y, z, core)


def final_kernel(
    small_ref, vec_ref, small_out, vec_out,
    work, swap, vec_sums, vec_lands, local_sem, *more,
):
    lands, (send, recv) = more[:-2], more[-2:]
    place = my_place()
    x, y, z, core = place
    mate = mate_of(place)
    load = pltpu.make_async_copy(small_ref, work, local_sem.at[0])
    load.start()
    greet([*others(place, "yz"), mate])
    load.wait()
    sems = Sems(send, recv)
    sum0 = weight_sum(direct_sum, place, sems, small_parts, work, 0, lands[:6])
    sum1 = weight_sum(direct_sum, place, sems, small_parts, work, 1, lands[6:])
    vec_land = [vec_lands.at[i] for i in range(7)]
    vec0 = whole_sum(place, sems, "z", vec_ref, vec_land[:3], vec_sums.at[0])
    vec1 = whole_sum(place, sems, "y", vec_sums.at[0], vec_land[3:6], vec_sums.at[1])
    vec_pair = sems.ready(vec_sums.at[1], vec_land[6], mate)
    pair = sems.ready(work.at[z, y], swap, mate)
    out1 = weight_spread(direct_spread, place, sems, small_parts, small_out, 1)
    out0 = weight_spread(direct_spread, place, sems, small_parts, small_out, 0)
    sum0[0]()
    vec0[0]()
    sum0[1]()
    sum1[0]()
    vec0[1]()
    vec1[0]()
    sum1[1]()
    pair.start()
    vec1[1]()
    vec_pair.start()
    pair.wait_recv()
    small_out[z, y] = (work[z, y].astype(f32) + swap[...].astype(f32)).astype(bf16)
    out1[0]()
    vec_pair.wait_recv()
    vec_out[...] = vec_sums[1].astype(f32) + vec_land[6][...].astype(f32)
    out1[1]()
    phases(out0)
    sems.finish()


def final(small, vectors, cid):
    shape = (4, 4, small_rows, D)
    vmem = pl.BlockSpec(memory_space=pltpu.VMEM)
    return call(
        final_kernel,
        (jax.ShapeDtypeStruct(shape, bf16), jax.ShapeDtypeStruct((16, D), f32)),
        [
            pltpu.VMEM(shape, bf16),
            pltpu.VMEM((small_rows, D), bf16),
            pltpu.VMEM((2, 16, D), bf16),
            pltpu.VMEM((7, 16, D), bf16),
            pltpu.SemaphoreType.DMA((1,)),
            *[
                pltpu.VMEM((*lead, block[1], block[3]), bf16)
                for lead in ((4,), ())
                for _, block in small_parts
                for _ in range(3)
            ],
        ],
        12 + 8 + 12,
        cid,
        (small.reshape(shape), vectors),
        [pl.BlockSpec(memory_space=pl.ANY), vmem],
    )


NT = (((1,), (1,)), ((), ()))
ROWS = G * 128


def lanes(shape):
    return lax.broadcasted_iota(jnp.int32, shape, len(shape) - 1)


def split3(value):
    one = value.astype(bf16).astype(f32)
    two = (value - one).astype(bf16).astype(f32)
    three = (value - one - two).astype(bf16).astype(f32)
    return one, two, three


def keys_of(kv_ref, c, half):
    start = half * 128 if isinstance(half, int) else pl.multiple_of(half * 128, 128)
    tile = kv_ref[c, :, pl.ds(start, 128), :].reshape(256, 128)
    lane = lanes((256, 128))
    ones = jnp.ones((256, 128), bf16)
    return jnp.where(lane < HD, tile, ones), jnp.where(lane < HD, ones, tile)


def both_keys(kv_ref, c0, c1):
    pairs = zip(keys_of(kv_ref, c0, 0), keys_of(kv_ref, c1, 0))
    return [jnp.concatenate(pair, 0) for pair in pairs]


def hidden_keys(xhi):
    row = lax.broadcasted_iota(jnp.int32, (ROWS, 256), 0) % 128
    key = lax.broadcasted_iota(jnp.int32, (ROWS, 256), 1)
    return key > row + xhi * 128


def forward_kernel(scal, q_ref, kv_ref, o_ref, qe_ref, peak, acc):
    me, xhi = scal[32], scal[33]
    for h in range(2):
        for g in range(G):
            piece = q_ref[h, :, g * HD : (g + 1) * HD].astype(f32) * (1.0 / math.sqrt(HD))
            wide_piece = jnp.concatenate([piece, jnp.zeros((128, HD), f32)], 1)
            qe_ref[h, g * 128 : (g + 1) * 128, :] = wide_piece.astype(bf16)
    peak[...] = jnp.full((2, ROWS, 128), -1e30, f32)
    acc[...] = jnp.zeros((2, ROWS, 128), f32)

    def fold(half, kk, vv, hide=None):
        s = lax.dot_general(qe_ref[half], kk, NT, preferred_element_type=f32)
        if hide is not None:
            s = jnp.where(hide, -1e30, s)
        tiles = [s[:, e : e + 128] for e in range(0, s.shape[1], 128)]
        old = peak[half]
        top = jnp.maximum(
            old, jnp.max(functools.reduce(jnp.maximum, tiles), 1, keepdims=True)
        )
        peak[half] = top
        p = jnp.concatenate([jnp.exp(t - top) for t in tiles], 1).astype(bf16)
        acc[half] = acc[half] * jnp.exp(old - top) + jnp.dot(p, vv, preferred_element_type=f32)

    def early_pair(c0, c1):
        fold(1, *both_keys(kv_ref, c0, c1))

    def other(c):
        sel = scal[c]
        fold(sel, *keys_of(kv_ref, c, sel))

    def one(i, carry):
        c0, c1 = (me + 2 * i + 1) % 32, (me + 2 * i + 2) % 32
        early_pair(c0, c1)
        other(c0)
        other(c1)
        return carry

    lax.fori_loop(0, 15, one, 0)
    early_pair((me + 31) % 32, me)
    other((me + 31) % 32)
    fold(0, *keys_of(kv_ref, me, 0), hidden_keys(xhi))
    fold(1, *keys_of(kv_ref, me, 1), hidden_keys(xhi))
    lane = lanes((ROWS, 128))
    for h in range(2):
        total = acc[h][:, :1]
        held = qe_ref[h].astype(f32)
        for i, part in enumerate(split3(-(peak[h][:, :1] + jnp.log(total)))):
            held = jnp.where(lane == HD + i, part, held)
        qe_ref[h] = held.astype(bf16)
        out = acc[h] / total
        for g in range(G):
            o_ref[h, :, g * HD : (g + 1) * HD] = out[g * 128 : (g + 1) * 128, HD:]


def local_call(kernel, out_shape, scratch, args, flops):
    vmem = pl.BlockSpec(memory_space=pltpu.VMEM)
    return pl.pallas_call(
        kernel,
        out_shape=out_shape,
        in_specs=[pl.BlockSpec(memory_space=pltpu.SMEM)] + [vmem] * (len(args) - 1),
        out_specs=jax.tree.map(lambda _: vmem, out_shape),
        scratch_shapes=scratch,
        compiler_params=pltpu.CompilerParams(vmem_limit_bytes=VLIM),
        cost_estimate=pl.CostEstimate(
            flops=flops, bytes_accessed=10_000_000, transcendentals=15_000_000
        ),
    )(*args)


def attention_forward(scal, q, kv):
    return local_call(
        forward_kernel,
        (
            jax.ShapeDtypeStruct((2, 128, QC), f32),
            jax.ShapeDtypeStruct((2, ROWS, 128), bf16),
        ),
        [pltpu.VMEM((2, ROWS, 128), f32), pltpu.VMEM((2, ROWS, 128), f32)],
        (scal, q, kv),
        20_000_000_000,
    )


def backward_kernel(
    scal, qe_ref, o_ref, g_ref, kv_ref, gate_ref, up_ref, down_ref,
    dq_ref, dkv_ref, sum_ref,
    ge, qt, gt, dq, work, swap, local_sem, *more,
):
    lands, (send, recv) = more[:-2], more[-2:]
    place = my_place()
    x, y, z, core = place
    me, xhi = lax.axis_index("ctx"), x // 2
    loads = []
    for i, ref in enumerate((gate_ref, up_ref, down_ref)):
        row = 0
        while row < FS:
            chunk, at = divmod(i * FS + row, big_rows)
            n = min(FS - row, big_rows - at)
            into = work.at[chunk // 4, chunk % 4, pl.ds(at, n)]
            loads.append(
                pltpu.make_async_copy(ref.at[pl.ds(row, n)], into, local_sem.at[len(loads)])
            )
            row += n
    for copy in loads:
        copy.start()
    unused = 3 * FS - 15 * big_rows
    work[3, 3, unused:] = jnp.zeros((big_rows - unused, D), bf16)
    greet([moved(place, a, b) for a in "yz" for b in (1, -1)] + [mate_of(place)])
    for copy in loads:
        copy.wait()
    sems = Sems(send, recv)
    sum0 = weight_sum(ring_sum, place, sems, big_parts, work, 0, lands[:12])
    sum1 = weight_sum(ring_sum, place, sems, big_parts, work, 1, lands[12:])
    pair = sems.ready(work.at[z, y], swap, mate_of(place))
    sum0[0]()

    lane = lanes((128, 128))
    for h in range(2):
        for g in range(G):
            cols = slice(g * HD, (g + 1) * HD)
            piece = g_ref[h, :, cols].astype(f32)
            delta = jnp.sum(piece * o_ref[h, :, cols], 1, keepdims=True)
            held = jnp.concatenate([jnp.zeros((128, HD), f32), piece], 1)
            for i, value in enumerate(split3(-delta)):
                held = jnp.where(lane == i, value, held)
            rows = slice(g * 128, (g + 1) * 128)
            ge[h, rows, :] = held.astype(bf16)
            gt[h, :, rows] = held.T.astype(bf16)
            qt[h, :, rows] = qe_ref[h, rows, :].astype(f32).T.astype(bf16)
    dq[...] = jnp.zeros((2, ROWS, 128), f32)

    def picked(sel, early, late):
        return jnp.where(jnp.full(early.shape, sel, jnp.int32) > 0, late, early)

    def tile(half, kk, vv, hide=None, late=None):
        def rows_of(ref):
            return ref[half] if late is None else picked(half, ref[0], ref[1])

        s = lax.dot_general(rows_of(qe_ref), kk, NT, preferred_element_type=f32)
        if hide is not None:
            s = jnp.where(hide, -1e30, s)
        p = jnp.exp(s)
        dp = lax.dot_general(rows_of(ge), vv, NT, preferred_element_type=f32)
        ds = (p * dp).astype(bf16)
        step = jnp.dot(ds, kk, preferred_element_type=f32)
        if late is None:
            dq[half] += step
        else:
            dq[1] += step * late
            dq[0] += step * (1.0 - late)
        dk = jnp.dot(rows_of(qt), ds, preferred_element_type=f32)
        dv = jnp.dot(rows_of(gt), p.astype(bf16), preferred_element_type=f32)
        return jnp.concatenate([dk[:HD], dv[HD:]], 0).T

    def put(c, half, value):
        dkv_ref[c, :, half * 128 : (half + 1) * 128, :] = value.astype(bf16).reshape(2, 128, 128)

    def other(c, early):
        sel = scal[c]
        late = sel.astype(f32)
        pairs = zip(keys_of(kv_ref, c, 0), keys_of(kv_ref, c, 1))
        step = tile(sel, *[picked(sel, *pair) for pair in pairs], late=late)
        put(c, 0, early + step * (1.0 - late))
        put(c, 1, step * late)

    beside = {3: [sum0[1]], 10: [sum0[2], sum1[0]], 12: [sum1[1]], 14: [sum1[2], pair.start]}

    def one(i, carry):
        for at, steps in beside.items():

            @pl.when(i == at)
            def _(steps=steps):
                for step in steps:
                    step()

        c0, c1 = (me + 2 * i + 1) % 32, (me + 2 * i + 2) % 32
        early = tile(1, *both_keys(kv_ref, c0, c1))
        other(c0, early[:256])
        other(c1, early[256:])
        return carry

    lax.fori_loop(0, 15, one, 0)
    final_c = (me + 31) % 32
    early = tile(1, *both_keys(kv_ref, final_c, me))
    other(final_c, early[:256])
    put(me, 0, early[256:] + tile(0, *keys_of(kv_ref, me, 0), hidden_keys(xhi)))
    put(me, 1, tile(1, *keys_of(kv_ref, me, 1), hidden_keys(xhi)))
    for h in range(2):
        for g in range(G):
            dq_ref[h, :, g * HD : (g + 1) * HD] = dq[h, g * 128 : (g + 1) * 128, :HD] * (
                1.0 / math.sqrt(HD)
            )
    pair.wait_recv()
    sum_ref[...] = (work[z, y].astype(f32) + swap[...].astype(f32)).astype(bf16)
    sems.finish()


def attention_backward(scal, qe, o, grad, kv, weight_grads, cid):
    big = (4, 4, big_rows, D)
    vmem = pl.BlockSpec(memory_space=pltpu.VMEM)
    return call(
        backward_kernel,
        (
            jax.ShapeDtypeStruct((2, 128, QC), f32),
            jax.ShapeDtypeStruct((32, 2, CHIP, 128), bf16),
            jax.ShapeDtypeStruct((big_rows, D), bf16),
        ),
        [
            pltpu.VMEM((2, ROWS, 128), bf16),
            pltpu.VMEM((2, 128, ROWS), bf16),
            pltpu.VMEM((2, 128, ROWS), bf16),
            pltpu.VMEM((2, ROWS, 128), f32),
            pltpu.VMEM(big, bf16),
            pltpu.VMEM((big_rows, D), bf16),
            pltpu.SemaphoreType.DMA((20,)),
            *sum_lands(big_parts, 0),
            *sum_lands(big_parts, 1),
        ],
        25,
        cid,
        (scal, qe, o, grad, kv, *weight_grads),
        [
            pl.BlockSpec(memory_space=pltpu.SMEM),
            *[vmem] * 4,
            *[pl.BlockSpec(memory_space=pl.ANY)] * 3,
        ],
    )


TN = (((0,), (0,)), ((), ()))
TILE = 256
TILES = -(-FS // TILE)


def middle_kernel(
    att_ref, chip_ref, other_ref, gain_ref, out_w, gate_w, up_w, down_w,
    att_out, stream_out, norm_out, pull_out, grad_out, final_out, gate_out, up_out, down_out,
    own_att, wo, wgate, wup, wdown, normed, hidden, gate_grad, up_grad, acc,
    part, got, total, far, mpart, mgot, mtotal, mfar, local_sem, send, recv,
):
    place = my_place()
    core = place[3]
    sibling, cross = pair_of(place)
    loads = [
        pltpu.make_async_copy(src, dst, local_sem.at[i])
        for i, (src, dst) in enumerate(
            (
                (out_w, wo),
                (gate_w, wgate.at[pl.ds(0, FS)]),
                (up_w, wup.at[pl.ds(0, FS)]),
                (down_w, wdown.at[pl.ds(0, FS)]),
            )
        )
    ]
    for copy in loads:
        copy.start()
    for ref in (wgate, wup, wdown):
        ref[FS:] = jnp.zeros((TILE * TILES - FS, D), bf16)
    own_att[...] = att_ref[...].reshape(CHIP, QC).astype(bf16)
    greet([sibling, cross])
    sems = Sems(send, recv)
    pieces = [pl.ds(64 * i, 64) for i in range(4)]
    over = [sems.start(own_att.at[p], att_out.at[1, core, p], cross) for p in pieces]
    beside = sems.start(own_att, att_out.at[0, core], sibling)
    att_out[0, core] = own_att[...]

    def exchange(p, got, total, far):
        near = [
            [sems.ready(p.at[c, h, 1 - core], got.at[c, h], sibling) for h in range(2)]
            for c in range(2)
        ]
        across = [sems.ready(total.at[h], far.at[h], cross) for h in range(2)]

        def first():
            for c in (1, 0):
                for h in range(2):
                    near[c][h].start()

        def middle():
            for h in range(2):
                near[1][h].wait_recv()
                total[h] = (p[1, h, core].astype(f32) + got[1, h].astype(f32)).astype(bf16)
                across[h].start()

        def value(h):
            near[0][h].wait_recv()
            across[h].wait_recv()
            return p[0, h, core].astype(f32) + got[0, h].astype(f32) + far[h].astype(f32)

        return first, middle, value

    norm_sum = exchange(part, got, total, far)
    mlp_sum = exchange(mpart, mgot, mtotal, mfar)
    gain = gain_ref[...]
    cots = (chip_ref.at[1], other_ref.at[1])

    def tile_rows(f):
        return pl.ds(pl.multiple_of(f * TILE, TILE), TILE)

    def stream_rows(c, tokens):
        sides = [att_out[c, i].astype(f32) for i in range(2)]
        attended = jnp.concatenate(sides, 1).astype(bf16)
        stream = tokens.astype(f32) + jnp.dot(attended, wo[...], preferred_element_type=f32)
        stream_out[c] = stream.reshape(2, 2, 64, D)
        inverse = lax.rsqrt(jnp.mean(stream * stream, -1, keepdims=True) + norm_eps)
        normed[c] = (stream * inverse * gain).astype(bf16)

    def hidden_rows(c):
        acc[c] = jnp.zeros((CHIP, D), f32)

        def one(f, carry):
            rows = tile_rows(f)
            gate = lax.dot_general(normed[c], wgate[rows], NT, preferred_element_type=f32)
            up = lax.dot_general(normed[c], wup[rows], NT, preferred_element_type=f32)
            pull = lax.dot_general(cots[c][...], wdown[rows], NT, preferred_element_type=f32)
            sigma = jax.nn.sigmoid(gate)
            active = gate * sigma
            hidden[c, f] = (active * up).astype(bf16)
            gate_pull = (pull * up * sigma * (1.0 + gate * (1.0 - sigma))).astype(bf16)
            up_pull = (pull * active).astype(bf16)
            gate_grad[c, f] = gate_pull
            up_grad[c, f] = up_pull
            acc[c] += jnp.dot(gate_pull, wgate[rows], preferred_element_type=f32) + jnp.dot(
                up_pull, wup[rows], preferred_element_type=f32
            )
            return carry

        lax.fori_loop(0, TILES, one, 0)
        part[c] = acc[c].reshape(2, 2, 64, D).astype(bf16)

    def down_rows(c):
        acc[c] = jnp.zeros((CHIP, D), f32)

        def one(f, carry):
            acc[c] += jnp.dot(hidden[c, f], wdown[tile_rows(f)], preferred_element_type=f32)
            return carry

        lax.fori_loop(0, TILES, one, 0)
        mpart[c] = acc[c].reshape(2, 2, 64, D).astype(bf16)

    def weight_grad(source, rights, out):
        def one(f, carry):
            both = [
                lax.dot_general(source[c, f], right, TN, preferred_element_type=f32)
                for c, right in enumerate(rights)
            ]
            out[tile_rows(f)] = (both[0] + both[1]).astype(bf16)
            return carry

        lax.fori_loop(0, TILES, one, 0)

    loads[0].wait()
    beside.wait_recv()
    stream_rows(0, chip_ref[0])
    passed = []
    for copy, p in zip(over, pieces):
        copy.wait_recv()
        passed.append(sems.start(att_out.at[1, core, p], att_out.at[1, core, p], sibling))
    for copy in loads[1:]:
        copy.wait()
    hidden_rows(0)
    for copy in passed:
        copy.wait_recv()
    stream_rows(1, other_ref[0])
    hidden_rows(1)
    norm_sum[0]()
    for c in range(2):
        down_rows(c)
    norm_sum[1]()
    mlp_sum[0]()
    weight_grad(gate_grad, [normed[c] for c in range(2)], gate_out)
    near = []
    for h in range(2):
        norm_out[0, h, core] = norm_sum[2](h).astype(bf16)
        mine = norm_out.at[0, h, core]
        near.append(sems.start(mine, mine, sibling))
    mlp_sum[1]()
    weight_grad(up_grad, [normed[c] for c in range(2)], up_out)
    for copy in near:
        copy.wait_recv()
    last = sems.start(norm_out.at[0], norm_out.at[1], cross)
    stream = stream_out[0].reshape(CHIP, D)
    inverse = lax.rsqrt(jnp.mean(stream * stream, -1, keepdims=True) + norm_eps)
    scaled = stream * inverse
    e = norm_out[0].reshape(CHIP, D).astype(f32) * gain
    pull = cots[0][...].astype(f32) + inverse * (
        e - scaled * jnp.mean(e * scaled, -1, keepdims=True)
    )
    pull_out[...] = pull
    mine = wo[pl.ds(pl.multiple_of(core * QC, 64), QC), :]
    grad = lax.dot_general(pull.astype(bf16), mine, NT, preferred_element_type=f32)
    grad_out[...] = grad.astype(bf16).reshape(2, 128, QC)
    for h in range(2):
        final_out[h] = (stream_out[0, h, core] + mlp_sum[2](h)).astype(bf16)
    weight_grad(hidden, [cot[...] for cot in cots], down_out)
    last.wait_recv()
    sems.finish()


def middle(attended, chip, other, gain, out_full, gate, up, down, cid):
    rows = (2, 2, 64, D)
    width = TILE * TILES
    vmem = pl.BlockSpec(memory_space=pltpu.VMEM)
    hbm = pl.BlockSpec(memory_space=pl.ANY)
    tiles = pltpu.VMEM((2, TILES, CHIP, TILE), bf16)
    exchanged = [
        pltpu.VMEM((2, *rows), bf16),
        pltpu.VMEM((2, 2, 64, D), bf16),
        pltpu.VMEM((2, 64, D), bf16),
        pltpu.VMEM((2, 64, D), bf16),
    ]
    return call(
        middle_kernel,
        (
            jax.ShapeDtypeStruct((2, 2, CHIP, QC), bf16),
            jax.ShapeDtypeStruct((2, *rows), f32),
            jax.ShapeDtypeStruct((2, *rows), bf16),
            jax.ShapeDtypeStruct((CHIP, D), f32),
            jax.ShapeDtypeStruct((2, 128, QC), bf16),
            jax.ShapeDtypeStruct((2, 64, D), bf16),
            *[jax.ShapeDtypeStruct((width, D), bf16)] * 3,
        ),
        [
            pltpu.VMEM((CHIP, QC), bf16),
            pltpu.VMEM((D, D), bf16),
            *[pltpu.VMEM((width, D), bf16)] * 3,
            pltpu.VMEM((2, CHIP, D), bf16),
            tiles,
            tiles,
            tiles,
            pltpu.VMEM((2, CHIP, D), f32),
            *exchanged,
            *exchanged,
            pltpu.SemaphoreType.DMA((4,)),
        ],
        9 + 12 + 3,
        cid,
        (attended, chip, other, gain, out_full, gate, up, down),
        [*[vmem] * 4, *[hbm] * 4],
    )


def rms_inverse(values):
    return lax.rsqrt(jnp.mean(values * values, -1, keepdims=True) + norm_eps)


def rms_pull(values, inverse, gain, grad):
    scaled = values * inverse
    e = grad * gain
    return inverse * (e - scaled * jnp.mean(e * scaled, -1, keepdims=True))


def rotation(positions):
    lane = jnp.arange(128)
    frequency = rope_base ** (-(2.0 * (lane % 32).astype(f32)) / HD)
    angles = positions.astype(f32)[:, None] * frequency[None, :]
    sign = jnp.where(lane % HD < HD // 2, -1.0, 1.0)
    return jnp.stack([jnp.cos(angles), jnp.sin(angles) * sign])


def dot(a, b):
    return jnp.dot(a, b, preferred_element_type=f32)


def body(
    tokens,
    out_grad,
    norm1_gain,
    qkv_weight,
    qkv_bias,
    out_weight,
    norm2_gain,
    gate_weight,
    up_weight,
    down_weight,
    positions,
):
    ctx = lax.axis_index("ctx")
    wsh = lax.axis_index("wsh")
    xhi, core = wsh // 2, wsh % 2
    my_block = positions[0] // 256

    def cut(array, start, size, axis):
        return lax.dynamic_slice_in_dim(array, start, size, axis)

    def own_rows(array):
        return cut(array.reshape(2, 2, 64, -1), core, 1, 1).reshape(TOK, -1)

    swap = [
        (c * 4 + w, ((c + 16) % 32) * 4 + (w + 2) % 4) for c in range(32) for w in range(4)
    ]

    def crossed(array):
        return lax.ppermute(array, ("ctx", "wsh"), swap)

    def spread(vector, width):
        column = jnp.arange(QKV)
        values = jnp.pad(jnp.tile(vector, 4), (0, QKV - 4 * width))
        return jnp.where(column // width == wsh, values, 0)

    small = jnp.stack([spread(qkv_bias, 288), spread(norm1_gain, 224), spread(norm2_gain, 224)])
    small = jnp.pad(small, ((0, 13), (0, 0))).astype(bf16)
    offset = jnp.arange(128, dtype=jnp.int32) + xhi * 128
    turn = rotation(jnp.concatenate([my_block * 256 + offset, (63 - my_block) * 256 + offset]))
    mark = jnp.broadcast_to(my_block.astype(bf16), (KROWS - CHIP, 128))
    t_all, w_all, s_all, queries, kv_all = opening(
        tokens, out_grad, qkv_weight, small, turn, mark, 0
    )
    out_weight, kv_all = lax.optimization_barrier((out_weight, kv_all))
    out_full = lax.all_gather(out_weight, "wsh", axis=0, tiled=True)
    qkv_full = w_all.reshape(D, QKV)
    vectors = jnp.sum(s_all[:, 1:3, :D].astype(f32), 0)
    gain_one, gain_two = vectors[0], vectors[1]
    t_chip = t_all.reshape(2, CHIP, D)
    kv_all = kv_all.reshape(32, 2, KROWS, 128)
    blocks = kv_all[:, 0, CHIP, 0].astype(jnp.int32)
    scal = jnp.concatenate(
        [(blocks > my_block).astype(jnp.int32), jnp.stack([ctx, xhi]).astype(jnp.int32)]
    )
    t_chip, kv_all = lax.optimization_barrier((t_chip, kv_all))
    t_other = crossed(t_chip)
    attended_f, qe = attention_forward(scal, queries, kv_all)
    att, stream, norm_both, stream_grad, att_grad, output, *large = middle(
        attended_f,
        t_chip,
        t_other,
        gain_two[None],
        out_full,
        gate_weight.T,
        up_weight.T,
        down_weight,
        2,
    )
    output = output.reshape(TOK, D)
    stream = stream.reshape(2 * CHIP, D)
    norm_both = norm_both.reshape(2 * CHIP, D)
    dq, dkv_part, large_own = attention_backward(
        scal, qe, attended_f, att_grad, kv_all, large, 5
    )
    pg, large = closing(dkv_part.reshape(2, 4, 4, 2, CHIP, 128), dq, turn, large_own, 4)
    pg, large = pg.reshape(2 * CHIP, QKV), large.reshape(16 * big_rows, D)

    resid_both = jnp.concatenate([t_chip[0], t_other[0]], 0).astype(f32)
    bias_grad = cut(jnp.sum(pg.astype(f32), 0), wsh * 288, 288, 0)
    inv_one = rms_inverse(resid_both)
    scaled_one = cut(resid_both, wsh * 224, 224, 1) * inv_one
    normed_cols = (scaled_one * norm1_gain.astype(f32)).astype(bf16)
    qkv_wgrad = jnp.einsum("td,tf->df", normed_cols, pg, preferred_element_type=f32)
    one_cols = jnp.einsum("tf,df->td", pg, qkv_weight, preferred_element_type=f32)
    gain_one_grad = jnp.sum(one_cols * scaled_one, 0)
    inv_two = rms_inverse(stream)
    other_grad = t_other[1].astype(f32) + rms_pull(
        stream[CHIP:], inv_two[CHIP:], gain_two, norm_both[CHIP:].astype(f32)
    )
    branch_both = jnp.concatenate([stream_grad.astype(bf16), other_grad.astype(bf16)], 0)
    scaled_two = cut(stream, wsh * 224, 224, 1) * inv_two
    gain_two_grad = jnp.sum(cut(norm_both, wsh * 224, 224, 1).astype(f32) * scaled_two, 0)
    att_mine = jnp.where(wsh < 2, att[:, 0], att[:, 1]).reshape(2 * CHIP, QC)
    att_mine = cut(att_mine, (wsh % 2) * 224, 224, 1)
    out_wgrad = jnp.einsum("ti,td->id", att_mine, branch_both, preferred_element_type=f32)
    pg_own = own_rows(pg[:CHIP])
    one_grad = jnp.einsum("tf,df->td", pg_own, qkv_full, preferred_element_type=f32)
    resid_own = tokens.astype(f32)
    token_grad = own_rows(stream_grad) + rms_pull(
        resid_own, rms_inverse(resid_own), gain_one, one_grad
    )
    vectors = jnp.stack(
        [jnp.pad(v, (0, D - v.shape[0])) for v in (bias_grad, gain_one_grad, gain_two_grad)]
    )
    small = jnp.concatenate(
        [out_wgrad.astype(bf16), qkv_wgrad.astype(bf16).reshape(288, D)], 0
    )
    vectors = jnp.pad(vectors, ((0, 13), (0, 0))).astype(bf16)
    small, vectors = final(small, vectors, 6)
    small = small.reshape(16 * small_rows, D)
    return (
        output,
        token_grad,
        vectors[1, :224],
        small[224:].reshape(224, QKV).astype(f32),
        vectors[0, :288],
        small[:224].astype(f32),
        vectors[2, :224],
        large[:FS].astype(f32).T,
        large[FS : 2 * FS].astype(f32).T,
        large[2 * FS : 3 * FS].astype(f32),
    )


def solution(mesh):
    rows = P(("ctx", "wsh"), None)
    return jax.shard_map(
        body,
        mesh=mesh,
        in_specs=(
            rows,
            rows,
            P("wsh"),
            P("wsh", None),
            P("wsh"),
            P("wsh", None),
            P("wsh"),
            P(None, "wsh"),
            P(None, "wsh"),
            P("wsh", None),
            P(("ctx", "wsh")),
        ),
        out_specs=(
            rows,
            rows,
            P("wsh"),
            P("wsh", None),
            P("wsh"),
            P("wsh", None),
            P("wsh"),
            P(None, "wsh"),
            P(None, "wsh"),
            P("wsh", None),
        ),
        check_vma=False,
    )
```
